512 devices in a mesh: depth: 16 (over x_hi, y, core), tile: 32 (over z, x_lo).
Axes of the slice: x: 4 (x_hi: 2, x_lo: 2; x = x_hi * 2 + x_lo), y: 4, z: 16, core: 2. Of those that a mesh axis runs over, the one named last changes fastest.
Arguments:
- volume: float32 [16, 1024, 1024], P('depth', 'tile'), may hold values from 0.05 to 100
- measured: float32 [1024, 1024], P('tile'), may hold values from 0.15 to 0.6
- point_spread: bfloat16 [16, 13, 13], P('depth'), may hold values from 7.390976e-05 to 0.0007362366
- entry_block: int32 [32, 4096], P('tile', 'depth'), may hold values from 0 to 63
- entry_neuron: int32 [32, 4096], P('tile', 'depth'), may hold values from -1 to 8191, as said below
- footprints: bfloat16 [32, 4096, 4, 128], P('tile', 'depth'), may hold values from 0.049804688 to 1
- seed_plane: int32 [8192], replicated, may hold values from 0 to 15
- seed_row: int32 [8192], replicated, may hold values from 0 to 1023
- seed_col: int32 [8192], replicated, may hold values from 0 to 1023
- owner_slot: int32 [8192], replicated, may hold values from 0 to 8191, each once
Outputs:
- estimate: float32 [16, 1024, 1024], P('depth', 'tile')
- demixed: float32 [8192], P(('depth', 'tile'))
The draws below stay inside these ranges and needn't reach their ends.
Inputs may be any that keep to these rules, and one draw needn't show every extreme that they name: `entry_neuron`: -1 marks an empty slot; on each device the active slots come first, from 85 to 256 of them, and some device has all 256 slots active; neuron ids may repeat.
All inputs are finite; a program needn't handle non-finite values.
Results may differ from the reference program's by a relative error of at most 0.0025.
Values may be sent and summed in bfloat16 or wider, within the bound.
No kernel may reach another device: no remote copies, remote signals or barrier semaphores. Data moves between devices by JAX's collectives and lax.ppermute only.
A program may use at most 64 MiB of HBM per device.

```python
import math
import jax
import jax.numpy as jnp
from jax import lax

PL_DEV = 1
ROWS_DEV = 32
COLS = 1024
E_DEV = 256
ITERS = 2
RADIUS = 6
BR = 4
CB = 128
TILES = 32
DEPTHS = 16
PLANES = 16
ROWS = 1024
KSIZE = 13
BLOCKS_DEV = 64
NEURONS = 8192


def draw_volume(key, part):
    key_back, key_bright, key_pick = jax.random.split(jax.random.fold_in(key, 29), 3)
    shape = (PLANES, ROWS, COLS)
    background = jnp.exp(jax.random.uniform(key_back, shape, jnp.float32, jnp.log(0.05), jnp.log(5.0)))
    bright = jnp.exp(jax.random.uniform(key_bright, shape, jnp.float32, jnp.log(5.0), jnp.log(100.0)))
    chance = 1.0 / 128.0
    picked = jax.random.uniform(key_pick, shape, jnp.float32) < chance
    result = jnp.where(picked, bright, background)
    return jnp.clip(result, 0.05, 100.0).astype(jnp.float32)


def draw_entry_neuron(key, part):
    key_count, key_full, key_ids = jax.random.split(jax.random.fold_in(key, 17), 3)
    count = jax.random.randint(key_count, (TILES, DEPTHS), E_DEV // 3, E_DEV + 1)
    full = jax.random.randint(key_full, (), 0, TILES * DEPTHS)
    device_ids = jnp.arange(TILES * DEPTHS).reshape(TILES, DEPTHS)
    is_full = device_ids == full
    count = jnp.where(is_full, E_DEV, count)
    ids = jax.random.randint(key_ids, (TILES, DEPTHS, E_DEV), 0, NEURONS)
    slot_ids = jnp.arange(E_DEV)[None, None, :]
    first_full = is_full[:, :, None] & (slot_ids == 0)
    ids = jnp.where(first_full, NEURONS - 1, ids)
    result = jnp.where(slot_ids < count[:, :, None], ids, -1)
    return result.reshape(TILES, DEPTHS * E_DEV).astype(jnp.int32)


def touch_ends(values, rng, low, top_value):
    shape = values.shape
    place = [jax.random.randint(jax.random.fold_in(rng, axis), (), 0, shape[axis]) for axis in range(len(shape))]
    values = values.at[tuple(place)].set(low)
    longest = shape.index(max(shape))
    place[longest] = (place[longest] + 1) % shape[longest]
    return values.at[tuple(place)].set(top_value)


def levels(rng, extent, shards, low, high):
    loudness = 1.0
    for dim, blocks in shards:
        steps = jax.random.uniform(jax.random.fold_in(jax.random.fold_in(rng, 6), dim), (blocks,), jnp.float32, low / len(shards), high / len(shards))
        loudness = loudness * jnp.repeat(jnp.exp(steps), extent[dim] // blocks).reshape((-1,) + (1,) * (len(extent) - 1 - dim))
    return loudness


def setup_inputs(seed: int = 0) -> dict:
    splits = jax.random.split(jax.random.key(seed), 11)
    volume = draw_volume(jax.random.fold_in(splits[10], 71), 0)
    measured = jnp.clip(jnp.exp(math.log(0.6) - 1.3862944 * jax.random.uniform(splits[1], (ROWS, COLS), jnp.float32) ** levels(splits[1], (ROWS, COLS), ((0, 32),), -0.2, 0.2)), 0.15, 0.6)
    point_spread = jnp.clip(jnp.exp(math.log(0.0007362366) - 2.2987066 * jax.random.uniform(splits[2], (PLANES, KSIZE, KSIZE), jnp.float32) ** levels(splits[2], (PLANES, KSIZE, KSIZE), ((0, 16),), -0.2, 0.2)), 7.390975952148438e-05, 0.0007362366).astype(jnp.bfloat16)
    entry_block = touch_ends(jax.random.randint(splits[3], (TILES, DEPTHS * E_DEV), 0, BLOCKS_DEV), jax.random.fold_in(splits[3], 1), 0, BLOCKS_DEV - 1).astype(jnp.int32)
    entry_neuron = draw_entry_neuron(jax.random.fold_in(splits[10], 71), 0)
    footprints = jnp.clip(jnp.exp(math.log(1.0) - 2.9996462 * jax.random.uniform(splits[5], (TILES, DEPTHS * E_DEV, BR, CB), jnp.float32) ** levels(splits[5], (TILES, DEPTHS * E_DEV, BR, CB), ((0, 32), (1, 16)), -0.2, 0.2)), 0.049804688, 1.0).astype(jnp.bfloat16)
    seed_plane = touch_ends(jax.random.randint(splits[6], (NEURONS,), 0, PLANES), jax.random.fold_in(splits[6], 1), 0, PLANES - 1).astype(jnp.int32)
    seed_row = touch_ends(jax.random.randint(splits[7], (NEURONS,), 0, ROWS), jax.random.fold_in(splits[7], 1), 0, ROWS - 1).astype(jnp.int32)
    seed_col = touch_ends(jax.random.randint(splits[8], (NEURONS,), 0, COLS), jax.random.fold_in(splits[8], 1), 0, COLS - 1).astype(jnp.int32)
    owner_slot = jax.random.permutation(splits[9], NEURONS).astype(jnp.int32)
    return {"volume": volume, "measured": measured, "point_spread": point_spread, "entry_block": entry_block, "entry_neuron": entry_neuron, "footprints": footprints, "seed_plane": seed_plane, "seed_row": seed_row, "seed_col": seed_col, "owner_slot": owner_slot}


def reference(volume, measured, point_spread, entry_block, entry_neuron, footprints, seed_plane, seed_row, seed_col, owner_slot):
    spread_f = point_spread.astype(jnp.float32)
    norm = jnp.sum(spread_f, axis=(1, 2))
    numbers = ("NCHW", "OIHW", "NCHW")
    padding = ((RADIUS, RADIUS), (RADIUS, RADIUS))
    estimate = volume
    for sweep in range(ITERS):
        rounded = estimate.astype(jnp.bfloat16)
        forward = lax.conv_general_dilated(rounded[None], point_spread[None], (1, 1), padding, dimension_numbers=numbers, preferred_element_type=jnp.float32)[0, 0]
        ratio = (measured / forward).astype(jnp.bfloat16)
        flipped = point_spread[:, None, ::-1, ::-1]
        backward = lax.conv_general_dilated(ratio[None, None], flipped, (1, 1), padding, dimension_numbers=numbers, preferred_element_type=jnp.float32)[0]
        estimate = estimate * backward / norm[:, None, None]
    row_groups = ROWS_DEV // BR
    col_groups = COLS // CB
    blocked = estimate.reshape(DEPTHS, PL_DEV, TILES, row_groups, BR, col_groups, CB)
    blocked = blocked.transpose(2, 0, 1, 3, 5, 4, 6).reshape(TILES * DEPTHS * BLOCKS_DEV, BR, CB)
    tile_ids = jnp.arange(TILES, dtype=jnp.int32)[:, None, None]
    depth_ids = jnp.arange(DEPTHS, dtype=jnp.int32)[None, :, None]
    local_block = entry_block.reshape(TILES, DEPTHS, E_DEV)
    segment = ((tile_ids * DEPTHS + depth_ids) * BLOCKS_DEV + local_block).reshape(-1).astype(jnp.int32)
    neuron = entry_neuron.reshape(-1)
    active = (neuron >= 0).astype(jnp.float32)
    slot_pos = owner_slot[jnp.maximum(neuron, 0)].astype(jnp.int32)
    weights = footprints.reshape(-1, BR, CB).astype(jnp.float32)
    picked = blocked[segment]
    slot_proj = jnp.sum(weights * picked, axis=(1, 2)) * active
    projection = jnp.zeros((NEURONS,), jnp.float32).at[slot_pos].add(slot_proj)
    seed_value = estimate[seed_plane, seed_row, seed_col]
    initial = jnp.zeros((NEURONS,), jnp.float32).at[owner_slot].set(seed_value)
    scaled = weights * (initial[slot_pos] * active)[:, None, None]
    rebuilt = jax.ops.segment_sum(scaled, segment, num_segments=TILES * DEPTHS * BLOCKS_DEV)
    slot_over = jnp.sum(weights * rebuilt[segment], axis=(1, 2)) * active
    intersection = jnp.zeros((NEURONS,), jnp.float32).at[slot_pos].add(slot_over)
    demixed = initial * projection / (intersection + 100.0 * initial)
    return estimate, demixed
```

```python
import jax
import jax.numpy as jnp
from jax import lax
from jax.experimental import pallas as pl
from jax.experimental.pallas import tpu as pltpu
from jax.sharding import PartitionSpec as P

F32 = jnp.float32
BF16 = jnp.bfloat16
I32 = jnp.int32
KS = 13
RADIUS = 6
ROWS = 32
COLS = 1024
CB = 128
NCB = COLS // CB
DEPTHS = 16
TILES = 32
SLOTS = 256
NEURONS = 8192
HALO = 24
H1 = 48
H2 = 24
VMEM = pl.BlockSpec(memory_space=pltpu.VMEM)
SMEM = pl.BlockSpec(memory_space=pltpu.SMEM)


def call(kernel, outs, n_in, scalars=(), scratch=(), mib=24):
    return pl.pallas_call(
        kernel,
        out_shape=[jax.ShapeDtypeStruct(s, t) for s, t in outs],
        in_specs=[SMEM if i in scalars else VMEM for i in range(n_in)],
        out_specs=[VMEM] * len(outs),
        scratch_shapes=list(scratch),
        compiler_params=pltpu.CompilerParams(vmem_limit_bytes=mib * 2**20),
    )


def iota(shape, dim):
    return lax.broadcasted_iota(I32, shape, dim)


def band(psf, rows, inner, offset, flip):
    lanes = KS * inner
    lane = iota((1, lanes), 1)
    tap_b = jnp.zeros((1, lanes), I32)
    for m in range(1, KS):
        tap_b = tap_b + (lane >= m * inner).astype(I32)
    inside = lane - tap_b * inner
    pick_b = (KS - 1) - tap_b if flip else tap_b
    hot = (iota((CB, lanes), 0) == pick_b).astype(F32).astype(BF16)
    taps = jnp.dot(psf, hot, preferred_element_type=F32)
    delta = inside - iota((rows, lanes), 0) + offset
    result = jnp.zeros((rows, lanes), F32)
    for m in range(KS):
        a = (KS - 1) - m if flip else m
        result = jnp.where(delta == m, taps[a : a + 1, :], result)
    return result.astype(BF16)


def shifted(field, stack):
    rows = field.shape[0]
    padded = jnp.concatenate([field, jnp.zeros((rows, CB), F32)], axis=1)
    width = COLS + CB
    for b in range(KS):
        shift = (RADIUS - b) % width
        moved = pltpu.roll(padded, shift, 1) if shift else padded
        stack[b * rows : (b + 1) * rows, :] = moved[:, :COLS].astype(BF16)


def split2(x):
    high = x.astype(BF16)
    return high, (x - high.astype(F32)).astype(BF16)


def split3(x):
    high = x.astype(BF16)
    rest = x - high.astype(F32)
    mid = rest.astype(BF16)
    return high, mid, (rest - mid.astype(F32)).astype(BF16)


def column_of(row):
    n = row.shape[1]
    return jnp.transpose(jnp.broadcast_to(row, (CB, n)))


def prepare_kernel(psf, block, neuron, weights, owner, t1f, t1b, t2f, t2b, gram, q_row, q_col, n_col, b_col):
    spread = psf[...]
    t1f[...] = band(spread, 80, 80, 0, False)
    t1b[...] = band(spread, 64, 80, 4, True)
    t2f[...] = band(spread, 48, 64, -4, False)
    t2b[...] = band(spread, 32, 48, 0, True)
    foot = weights[...]
    product = lax.dot_general(foot, foot, (((1,), (1,)), ((), ())), preferred_element_type=F32)
    blocks = column_of(block[...].astype(F32))
    neurons = column_of(neuron[...].astype(F32))
    same = jnp.concatenate([blocks, blocks], axis=1) == block[...].astype(F32)
    gram[...] = jnp.where(same, product, 0.0)
    n_int = neurons.astype(I32)
    n_col[...] = n_int
    b_col[...] = blocks.astype(I32)
    table = owner[...]
    tables = jnp.concatenate([(table >> 7).astype(F32), (table & 127).astype(F32)], axis=1).astype(BF16)
    hot = (iota((SLOTS, 64), 1) == (n_int[:, :64] >> 7)).astype(F32).astype(BF16)
    found = jnp.dot(hot, tables, preferred_element_type=F32)
    lane_hot = iota((SLOTS, CB), 1) == (n_int & 127)
    value = jnp.where(lane_hot, found[:, :CB] * 128.0 + found[:, CB:], 0.0)
    place = jnp.sum(value, axis=1, keepdims=True)
    place = jnp.broadcast_to(place, (SLOTS, CB))
    place = jnp.where(n_int >= 0, place, -1.0)
    q_col[...] = place.astype(I32)
    q_row[...] = jnp.transpose(place)[0:8, :].astype(I32)


def forward1_kernel(where, psf_band, volume, left, right, measured, pieces, meas1, meas2, stack):
    half = where[0]
    field = jnp.concatenate([left[:, :COLS], volume[...], right[:, :COLS]], axis=0)
    shifted(field, stack)
    value = jnp.dot(psf_band[...], stack[...], preferred_element_type=F32)
    for cb in range(NCB):
        part = value[:, cb * CB : (cb + 1) * CB].astype(BF16)
        pieces[2 * cb] = part[:H1]
        pieces[2 * cb + 1, 0:32, :] = part[H1:]
        pieces[2 * cb + 1, 32:48, :] = jnp.zeros((16, CB), BF16)
    sensor = jnp.concatenate([left[:, COLS:], measured[...], right[:, COLS:]], axis=0)
    second = jnp.concatenate([sensor[54:80], jnp.zeros((22, CB), F32)], axis=0)
    meas1[...] = jnp.where(half == 0, sensor[6:54], second)
    meas2[...] = jnp.where(half == 0, sensor[18:42], sensor[42:66])


def ratio_kernel(rows, valid, pad):
    def kernel(where, parts, measured, out):
        total = parts[0].astype(F32)
        for j in range(1, DEPTHS):
            total = total + parts[j].astype(F32)
        sensor = measured[...]
        inside = (iota((rows, CB), 0) + where[0] * rows < valid) & (sensor != 0.0)
        ratio = jnp.where(inside, sensor / jnp.where(inside, total, 1.0), 0.0)
        if pad:
            ratio = jnp.concatenate([ratio, jnp.zeros((pad, CB), F32)], axis=0)
        ratio = ratio.astype(BF16)
        for j in range(DEPTHS):
            out[j] = ratio

    return kernel


def spread_norm(psf):
    return jnp.sum(jnp.sum(psf[...].astype(F32), axis=0, keepdims=True), axis=1, keepdims=True)


def middle_kernel(psf, band_b, band_f, volume, left, right, ratio, pieces, estimate, stack_b, stack_f):
    columns = []
    for cb in range(NCB):
        columns.append(jnp.concatenate([ratio[2 * cb].astype(F32), ratio[2 * cb + 1].astype(F32)[:32]], axis=0))
    shifted(jnp.concatenate(columns, axis=1), stack_b)
    backward = jnp.dot(band_b[...], stack_b[...], preferred_element_type=F32)
    field = jnp.concatenate([left[8:24, :COLS], volume[...], right[0:16, :COLS]], axis=0)
    updated = field * backward / spread_norm(psf)
    estimate[...] = updated[16:48]
    shifted(updated, stack_f)
    value = jnp.dot(band_f[...], stack_f[...], preferred_element_type=F32)
    for cb in range(NCB):
        pieces[2 * cb] = value[:H2, cb * CB : (cb + 1) * CB]
        pieces[2 * cb + 1] = value[H2:, cb * CB : (cb + 1) * CB]


def last_kernel(where, psf, band_b, before, ratio, weights, b_col, s_plane, s_row, s_col, estimate, seeds, proj, stack, lines):
    columns = []
    for cb in range(NCB):
        columns.append(
            jnp.concatenate([ratio[2 * cb].astype(F32)[:H2], ratio[2 * cb + 1].astype(F32)[:H2]], axis=0)
        )
    shifted(jnp.concatenate(columns, axis=1), stack)
    backward = jnp.dot(band_b[...], stack[...], preferred_element_type=F32)
    updated = before[...] * backward / spread_norm(psf)
    estimate[...] = updated
    tall = jnp.concatenate([updated[:, c * CB : (c + 1) * CB] for c in range(NCB)], axis=0)
    flat = jnp.transpose(tall)
    left_side = jnp.concatenate(split2(flat), axis=0)
    chunk = NEURONS // DEPTHS
    for j in range(DEPTHS):
        row, col = s_row[j], s_col[j]
        local = (s_plane[j] == where[1]) & ((row >> 5) == where[2])
        key = jnp.where(local, (col >> 7) * ROWS + (row & (ROWS - 1)), -1)
        hot = (iota((SLOTS, chunk), 0) == key).astype(F32).astype(BF16)
        found = jnp.dot(left_side, hot, preferred_element_type=F32)
        found = found[:CB] + found[CB:]
        seeds[j] = jnp.sum(
            jnp.where(iota((CB, chunk), 0) == (col & (CB - 1)), found, 0.0), axis=0, keepdims=True
        )
    lines[...] = tall
    blocks = [lines[pl.ds(br, 64, stride=4), :] for br in range(4)]
    blocked = jnp.concatenate(blocks, axis=1)
    number = b_col[:, :64]
    number = (number & 7) * 8 + (number >> 3)
    hot = (iota((SLOTS, 64), 1) == number).astype(F32).astype(BF16)
    high, low = split2(blocked)
    picked = jnp.dot(hot, high, preferred_element_type=F32) + jnp.dot(hot, low, preferred_element_type=F32)
    product = weights[...].astype(F32) * picked
    total = product[:, :CB]
    for br in range(1, 4):
        total = total + product[:, br * CB : (br + 1) * CB]
    proj[...] = jnp.broadcast_to(jnp.sum(total, axis=1, keepdims=True), (SLOTS, CB))


def slots_kernel(where, initial, owner, gram, q_row, q_col, n_col, proj, out, own):
    table = jnp.concatenate([initial[j] for j in range(DEPTHS)], axis=0)
    chunk = NEURONS // DEPTHS
    number = n_col[...]
    hot = (iota((SLOTS, DEPTHS), 1) == (number[:, :DEPTHS] >> 9)).astype(F32).astype(BF16)
    parts = split3(table)
    found = jnp.dot(hot, parts[0], preferred_element_type=F32)
    found = found + jnp.dot(hot, parts[1], preferred_element_type=F32)
    found = found + jnp.dot(hot, parts[2], preferred_element_type=F32)
    wide = jnp.concatenate([number] * 4, axis=1) & (chunk - 1)
    value = jnp.where(iota((SLOTS, chunk), 1) == wide, found, 0.0)
    value = value[:, :128] + value[:, 128:256] + value[:, 256:384] + value[:, 384:]
    start = jnp.broadcast_to(jnp.sum(value, axis=1, keepdims=True), (SLOTS, CB))
    start_row = jnp.transpose(start)[0:1, :]
    terms = gram[...] * start_row
    over = jnp.sum(terms[:, :CB] + terms[:, CB:], axis=1, keepdims=True)
    place = q_col[...]
    lane = iota((SLOTS, CB), 1)
    target = ((place >> 4) & 3) * 32 + (place & 15)
    sent = jnp.where(lane == target, proj[...], 0.0) + jnp.where(lane == target + 16, over, 0.0)
    row_hot = (iota((CB, SLOTS), 0) == (q_row[0:1, :] >> 6)).astype(F32).astype(BF16)
    parts = split3(sent)
    dense = jnp.dot(row_hot, parts[0], preferred_element_type=F32)
    dense = dense + jnp.dot(row_hot, parts[1], preferred_element_type=F32)
    dense = dense + jnp.dot(row_hot, parts[2], preferred_element_type=F32)
    for j in range(DEPTHS):
        out[j] = dense[j * 8 : (j + 1) * 8]
    base = where[3]
    holder = owner[...]
    lanes = iota((1, CB), 1)
    result = jnp.zeros((1, CB), F32)
    for i in range(16):
        mine = jnp.sum(jnp.where(holder == base + i, table, 0.0), axis=0, keepdims=True)
        result = jnp.where(lanes == i, jnp.sum(mine, axis=1, keepdims=True), result)
    own[...] = result


def fold_kernel(parts, out):
    total = parts[0]
    for j in range(1, DEPTHS):
        total = total + parts[j]
    for m in range(4):
        moved = pltpu.roll(total, (CB - 32 * m) % CB, 1) if m else total
        for r in range(8):
            out[4 * r + m] = moved[r : r + 1]


def final_kernel(parts, own, out):
    total = parts[0]
    for j in range(1, TILES):
        total = total + parts[j]
    over = pltpu.roll(total, CB - 16, 1)
    initial = own[...]
    real = iota((1, CB), 1) < 16
    bottom = jnp.where(real, over + 100.0 * initial, 1.0)
    out[...] = jnp.where(real, initial * total, 0.0) / bottom


def swap(pieces, axis):
    return lax.all_to_all(pieces, axis, 0, 0)


def body(
    volume,
    measured,
    point_spread,
    entry_block,
    entry_neuron,
    footprints,
    seed_plane,
    seed_row,
    seed_col,
    owner_slot,
):
    d = lax.axis_index("depth")
    t = lax.axis_index("tile")
    where = jnp.stack([d % 2, d, t, (d * TILES + t) * 16]).astype(I32)
    vol = volume[0]
    sensor = lax.dynamic_slice(measured, (0, (d // 2) * CB), (ROWS, CB))
    down = jnp.concatenate([vol[ROWS - HALO :], sensor[ROWS - HALO :]], axis=1)
    up = jnp.concatenate([vol[:HALO], sensor[:HALO]], axis=1)
    left = lax.ppermute(down, "tile", [(i, i + 1) for i in range(TILES - 1)])
    right = lax.ppermute(up, "tile", [(i + 1, i) for i in range(TILES - 1)])
    psf = jnp.pad(point_spread[0], ((0, 16 - KS), (0, CB - KS)))
    weights = footprints[0].reshape(SLOTS, 512)
    t1f, t1b, t2f, t2b, gram, q_row, q_col, n_col, b_col = call(
        prepare_kernel,
        [
            ((80, KS * 80), BF16),
            ((64, KS * 80), BF16),
            ((48, KS * 64), BF16),
            ((32, KS * 48), BF16),
            ((SLOTS, SLOTS), F32),
            ((8, SLOTS), I32),
            ((SLOTS, CB), I32),
            ((SLOTS, CB), I32),
            ((SLOTS, CB), I32),
        ],
        5,
    )(psf, entry_block, entry_neuron, weights, owner_slot.reshape(64, CB))
    pieces, meas1, meas2 = call(
        forward1_kernel,
        [((DEPTHS, H1, CB), BF16), ((H1, CB), F32), ((H2, CB), F32)],
        6,
        scalars=(0,),
        scratch=[pltpu.VMEM((KS * 80, COLS), BF16)],
    )(where, t1f, vol, left, right, sensor)
    [ratio] = call(ratio_kernel(H1, 68, 0), [((DEPTHS, H1, CB), BF16)], 3, scalars=(0,))(
        where, swap(pieces, "depth"), meas1
    )
    pieces, before = call(
        middle_kernel,
        [((DEPTHS, H2, CB), F32), ((ROWS, COLS), F32)],
        7,
        scratch=[pltpu.VMEM((KS * 80, COLS), BF16), pltpu.VMEM((KS * 64, COLS), BF16)],
    )(psf, t1b, t2f, vol, left, right, swap(ratio, "depth"))
    [ratio] = call(ratio_kernel(H2, 44, 8), [((DEPTHS, 32, CB), BF16)], 3, scalars=(0,))(
        where, swap(pieces, "depth"), meas2
    )
    chunk = NEURONS // DEPTHS
    shape = (DEPTHS, 1, chunk)
    estimate, seeds, proj = call(
        last_kernel,
        [((ROWS, COLS), F32), (shape, F32), ((SLOTS, CB), F32)],
        10,
        scalars=(0,),
        scratch=[pltpu.VMEM((KS * 48, COLS), BF16), pltpu.VMEM((NCB * ROWS, CB), F32)],
    )(
        where,
        psf,
        t2b,
        before,
        swap(ratio, "depth"),
        weights,
        b_col,
        seed_plane.reshape(shape),
        seed_row.reshape(shape),
        seed_col.reshape(shape),
    )
    mine = jnp.sum(swap(seeds, "depth"), axis=0)
    mine = jnp.sum(swap(jnp.broadcast_to(mine, (TILES, 1, chunk)), "tile"), axis=0)
    initial = swap(jnp.broadcast_to(mine, shape), "depth")
    sent, own = call(slots_kernel, [((DEPTHS, 8, CB), F32), ((1, CB), F32)], 8, scalars=(0,))(
        where, initial, owner_slot.reshape(DEPTHS, chunk), gram, q_row, q_col, n_col, proj
    )
    [sent] = call(fold_kernel, [((TILES, 1, CB), F32)], 1)(swap(sent, "depth"))
    [demixed] = call(final_kernel, [((1, CB), F32)], 2)(swap(sent, "tile"), own)
    return estimate[None], demixed[0, :16]


def solution(mesh):
    in_specs = (
        P("depth", "tile", None),
        P("tile", None),
        P("depth", None, None),
        P("tile", "depth"),
        P("tile", "depth"),
        P("tile", "depth", None, None),
        P(),
        P(),
        P(),
        P(),
    )
    out_specs = (P("depth", "tile", None), P(("depth", "tile")))
    return jax.shard_map(body, mesh=mesh, in_specs=in_specs, out_specs=out_specs, check_vma=False)
```

```python
import jax
import jax.numpy as jnp
from jax import lax
from jax.experimental import pallas as pl
from jax.experimental.pallas import tpu as pltpu
from jax.sharding import PartitionSpec as P

F32 = jnp.float32
BF16 = jnp.bfloat16
I32 = jnp.int32
KS = 13
RADIUS = 6
ROWS = 32
COLS = 1024
CB = 128
NCB = COLS // CB
DEPTHS = 16
TILES = 32
SLOTS = 256
NEURONS = 8192
HALO = 24
WIN = 64
LIVE = WIN + 2 * HALO
ROW = DEPTHS
BLOCK = 16
DEEP = 32 * ROW
VMEM = pl.BlockSpec(memory_space=pltpu.VMEM)
SMEM = pl.BlockSpec(memory_space=pltpu.SMEM)


def call(kernel, outs, n_in, scalars=(), scratch=(), mib=24):
    return pl.pallas_call(
        kernel,
        out_shape=[jax.ShapeDtypeStruct(s, t) for s, t in outs],
        in_specs=[SMEM if i in scalars else VMEM for i in range(n_in)],
        out_specs=[VMEM] * len(outs),
        scratch_shapes=list(scratch),
        compiler_params=pltpu.CompilerParams(vmem_limit_bytes=mib * 2**20),
    )


def iota(shape, dim):
    return lax.broadcasted_iota(I32, shape, dim)


def split2(x):
    high = x.astype(BF16)
    return high, (x - high.astype(F32)).astype(BF16)


def split3(x):
    high = x.astype(BF16)
    rest = x - high.astype(F32)
    mid = rest.astype(BF16)
    return high, mid, (rest - mid.astype(F32)).astype(BF16)


def column_of(row):
    n = row.shape[1]
    return jnp.transpose(jnp.broadcast_to(row, (CB, n)))


def prepare_kernel(block, neuron, weights, owner, gram, q_row, q_col, n_col, b_col):
    foot = weights[...]
    product = lax.dot_general(foot, foot, (((1,), (1,)), ((), ())), preferred_element_type=F32)
    blocks = column_of(block[...].astype(F32))
    neurons = column_of(neuron[...].astype(F32))
    same = jnp.concatenate([blocks, blocks], axis=1) == block[...].astype(F32)
    gram[...] = jnp.where(same, product, 0.0)
    n_int = neurons.astype(I32)
    n_col[...] = n_int
    b_col[...] = blocks.astype(I32)
    table = owner[...]
    tables = jnp.concatenate([(table >> 7).astype(F32), (table & 127).astype(F32)], axis=1).astype(BF16)
    hot = (iota((SLOTS, 64), 1) == (n_int[:, :64] >> 7)).astype(F32).astype(BF16)
    found = jnp.dot(hot, tables, preferred_element_type=F32)
    lane_hot = iota((SLOTS, CB), 1) == (n_int & 127)
    value = jnp.where(lane_hot, found[:, :CB] * 128.0 + found[:, CB:], 0.0)
    place = jnp.sum(value, axis=1, keepdims=True)
    place = jnp.broadcast_to(place, (SLOTS, CB))
    place = jnp.where(n_int >= 0, place, -1.0)
    q_col[...] = place.astype(I32)
    q_row[...] = jnp.transpose(place)[0:8, :].astype(I32)


def window_kernel(where, volume, spread, measured, windows, sensor, wide):
    lane = iota((ROWS, CB), 1)
    zeros = jnp.zeros((ROWS, CB), F32)
    padded = jnp.concatenate([zeros, volume[...], zeros], axis=1)
    for j in range(DEPTHS):
        start = CB - HALO + WIN * j
        low = start // CB * CB
        moved = pltpu.roll(padded[:, low : low + 2 * CB], 2 * CB - start % CB, 1)[:, :CB]
        windows[j] = jnp.where(lane < LIVE, moved, spread[...])
    wide[:, :CB] = zeros
    wide[:, CB : CB + COLS] = measured[...]
    wide[:, CB + COLS :] = zeros
    start = CB - HALO + WIN * where[0]
    low = pl.multiple_of((start >> 7) * CB, CB)
    moved = pltpu.roll(wide[:, pl.ds(low, 2 * CB)], 2 * CB - (start & (CB - 1)), 1)[:, :CB]
    sensor[...] = jnp.where(lane < LIVE, moved, 0.0)


def arrange_kernel(parts, sensor, own, down, up):
    lane = iota((ROW, CB), 1)
    for r in range(ROWS):
        line = jnp.where(lane < LIVE, parts[pl.ds(r, ROW, stride=ROWS), :], 0.0)
        own[r * ROW : (r + 1) * ROW, :] = line
        if r < HALO:
            up[r * ROW : (r + 1) * ROW, :] = line
        if r >= ROWS - HALO:
            at = (r - ROWS + HALO) * ROW
            down[at : at + ROW, :] = line
    up[HALO * ROW :, :] = sensor[:HALO]
    down[HALO * ROW :, :] = sensor[ROWS - HALO :]


def tables_kernel(parts, ahead, behind, scale):
    taps = jnp.concatenate([parts[pl.ds(a, ROW, stride=ROWS), :] for a in range(16)], axis=0)
    taps = jnp.where(iota((256, CB), 1) >= LIVE, taps, 0.0)
    first = jnp.transpose(taps)[LIVE:, :]
    first = jnp.concatenate([first, jnp.zeros((16, 256), F32)], axis=1)
    for i in range(BLOCK):
        moved = pltpu.roll(first, i * ROW, 1) if i else first
        ahead[i * 16 : (i + 1) * 16, :] = moved.astype(BF16)
    lane = iota((CB, DEEP), 1)
    hot = (iota((CB, DEEP), 0) == LIVE + KS - 1 - (lane >> 5)).astype(F32).astype(BF16)
    spread = jnp.dot(taps.astype(BF16), hot, preferred_element_type=F32)
    inside = iota((ROW, DEEP), 1)
    within = jnp.where(inside < KS * 32, inside & 31, 32)
    second = jnp.zeros((ROW, DEEP), F32)
    for a in range(KS):
        second = jnp.where(within == KS - 1 - a, spread[a * ROW : (a + 1) * ROW], second)
    for i in range(BLOCK):
        moved = pltpu.roll(second, i, 1) if i else second
        behind[i * ROW : (i + 1) * ROW, :] = moved.astype(BF16)
    total = taps[:ROW]
    for a in range(1, KS):
        total = total + taps[a * ROW : (a + 1) * ROW]
    norm = jnp.sum(total, axis=1, keepdims=True)
    scale[...] = jnp.broadcast_to(1.0 / norm, (ROW, CB))


def lane_shift(x, b):
    shift = (RADIUS - b) % CB
    return pltpu.roll(x, shift, 1) if shift else x


def iterate_kernel(
    where, own, left, right, sensor, ahead, behind, scale, s_plane, s_row, s_col,
    sent, exact, rounded, first, second, light, sums, ratio, stack, packed,
):
    rows = (HALO * ROW, (HALO + ROWS) * ROW, (2 * HALO + ROWS) * ROW)
    exact[: rows[0], :] = left[: rows[0]]
    exact[rows[0] : rows[1], :] = own[...]
    exact[rows[1] : rows[2], :] = right[: rows[0]]
    exact[rows[2] :, :] = jnp.zeros((16 * ROW, CB), F32)
    rounded[...] = exact[...].astype(BF16)
    light[:HALO, :] = left[rows[0] :]
    light[HALO : HALO + ROWS, :] = sensor[...]
    light[HALO + ROWS : 2 * HALO + ROWS, :] = right[rows[0] :]
    light[2 * HALO + ROWS :, :] = jnp.zeros((16, CB), F32)
    for m in range(4):
        stack[m * DEEP + KS * 32 : (m + 1) * DEEP, :] = jnp.zeros((DEEP - KS * 32, CB), BF16)
    tall = jnp.concatenate([scale[...]] * BLOCK, axis=0)

    def divide(source, blocks, offset, valid):
        for m in range(blocks):
            sums[...] = jnp.dot(
                ahead[...], source[m * 256 : m * 256 + DEEP, :], preferred_element_type=F32
            )
            total = lane_shift(sums[pl.ds(0, BLOCK, stride=16), :], 0)
            for b in range(1, KS):
                total = total + lane_shift(sums[pl.ds(b, BLOCK, stride=16), :], b)
            seen = light[m * BLOCK + offset : (m + 1) * BLOCK + offset, :]
            inside = (iota((BLOCK, CB), 0) < valid - m * BLOCK) & (seen != 0.0) & (total != 0.0)
            value = jnp.where(inside, seen / jnp.where(inside, total, 1.0), 0.0)
            ratio[m * BLOCK : (m + 1) * BLOCK, :] = value

    def spread_back(blocks):
        height = 16 * blocks + 16
        for b in range(KS):
            moved = lane_shift(ratio[:height, :], b).astype(BF16)
            for m in range(blocks):
                stack[m * DEEP + b * 32 : m * DEEP + (b + 1) * 32, :] = moved[m * 16 : m * 16 + 32]

    def back(m):
        value = jnp.dot(behind[...], stack[m * DEEP : (m + 1) * DEEP, :], preferred_element_type=F32)
        return value * tall

    divide(rounded, 5, 6, 68)
    spread_back(4)
    for m in range(4):
        value = exact[(m * 16 + 12) * ROW : (m * 16 + 28) * ROW, :] * back(m)
        first[m * 256 : (m + 1) * 256, :] = value
        second[m * 256 : (m + 1) * 256, :] = value.astype(BF16)
    divide(second, 3, 18, 44)
    spread_back(2)
    done = [first[(m * 16 + 12) * ROW : (m * 16 + 28) * ROW, :] * back(m) for m in range(2)]
    lane = iota((256, CB), 1)
    flat = jnp.where(lane < WIN, pltpu.roll(done[0], CB - HALO, 1), pltpu.roll(done[1], WIN - HALO, 1))
    packed[...] = flat
    for p in range(DEPTHS):
        sent[p, 0:16, :] = packed[pl.ds(p, 16, stride=ROW), :]
        sent[p, 20:24, :] = jnp.zeros((4, CB), F32)
    left_side = jnp.concatenate(split2(jnp.transpose(flat)), axis=0)
    chunk = NEURONS // DEPTHS
    for j in range(DEPTHS):
        plane, row, col = s_plane[j], s_row[j], s_col[j]
        local = ((row >> 5) == where[1]) & ((col >> 6) == where[0])
        key = jnp.where(local, (row & 15) * ROW + plane, -1)
        hot = (iota((256, chunk), 0) == key).astype(F32).astype(BF16)
        found = jnp.dot(left_side, hot, preferred_element_type=F32)
        found = found[:CB] + found[CB:]
        spot = ((row >> 4) & 1) * WIN + (col & (WIN - 1))
        picked = jnp.sum(jnp.where(iota((CB, chunk), 0) == spot, found, 0.0), axis=0, keepdims=True)
        for i in range(4):
            sent[j, 16 + i : 17 + i, :] = picked[:, i * CB : (i + 1) * CB]


def sum_kernel(count, at, copies):
    def kernel(parts, out):
        total = parts[0, at : at + 4, :]
        for j in range(1, count):
            total = total + parts[j, at : at + 4, :]
        for j in range(copies):
            out[j] = total

    return kernel


def home_kernel(parts, weights, b_col, estimate, proj, lines):
    lane = iota((16, CB), 1)
    for c in range(NCB):
        a, b = parts[2 * c, :16, :], parts[2 * c + 1, :16, :]
        top = jnp.where(lane < WIN, a, pltpu.roll(b, WIN, 1))
        bottom = jnp.where(lane < WIN, pltpu.roll(a, WIN, 1), b)
        estimate[:16, c * CB : (c + 1) * CB] = top
        estimate[16:, c * CB : (c + 1) * CB] = bottom
        lines[c * ROWS : c * ROWS + 16, :] = top
        lines[c * ROWS + 16 : (c + 1) * ROWS, :] = bottom
    blocks = [lines[pl.ds(br, 64, stride=4), :] for br in range(4)]
    blocked = jnp.concatenate(blocks, axis=1)
    number = b_col[:, :64]
    number = (number & 7) * 8 + (number >> 3)
    hot = (iota((SLOTS, 64), 1) == number).astype(F32).astype(BF16)
    high, low = split2(blocked)
    picked = jnp.dot(hot, high, preferred_element_type=F32) + jnp.dot(hot, low, preferred_element_type=F32)
    product = weights[...].astype(F32) * picked
    total = product[:, :CB]
    for br in range(1, 4):
        total = total + product[:, br * CB : (br + 1) * CB]
    proj[...] = jnp.broadcast_to(jnp.sum(total, axis=1, keepdims=True), (SLOTS, CB))


def slots_kernel(where, initial, owner, gram, q_row, q_col, n_col, proj, out, own):
    table = jnp.concatenate([initial[j] for j in range(DEPTHS)], axis=0)
    number = n_col[...]
    hot = (iota((SLOTS, 64), 1) == (number[:, :64] >> 7)).astype(F32).astype(BF16)
    parts = split3(table)
    found = jnp.dot(hot, parts[0], preferred_element_type=F32)
    found = found + jnp.dot(hot, parts[1], preferred_element_type=F32)
    found = found + jnp.dot(hot, parts[2], preferred_element_type=F32)
    value = jnp.where(iota((SLOTS, CB), 1) == (number & (CB - 1)), found, 0.0)
    start = jnp.broadcast_to(jnp.sum(value, axis=1, keepdims=True), (SLOTS, CB))
    start_row = jnp.transpose(start)[0:1, :]
    terms = gram[...] * start_row
    over = jnp.sum(terms[:, :CB] + terms[:, CB:], axis=1, keepdims=True)
    place = q_col[...]
    lane = iota((SLOTS, CB), 1)
    target = ((place >> 4) & 3) * 32 + (place & 15)
    sent = jnp.where(lane == target, proj[...], 0.0) + jnp.where(lane == target + 16, over, 0.0)
    row_hot = (iota((CB, SLOTS), 0) == (q_row[0:1, :] >> 6)).astype(F32).astype(BF16)
    parts = split3(sent)
    dense = jnp.dot(row_hot, parts[0], preferred_element_type=F32)
    dense = dense + jnp.dot(row_hot, parts[1], preferred_element_type=F32)
    dense = dense + jnp.dot(row_hot, parts[2], preferred_element_type=F32)
    for j in range(DEPTHS):
        out[j] = dense[j * 8 : (j + 1) * 8]
    base = where[2]
    holder = owner[...]
    lanes = iota((1, CB), 1)
    result = jnp.zeros((1, CB), F32)
    for i in range(16):
        mine = jnp.sum(jnp.where(holder == base + i, table, 0.0), axis=0, keepdims=True)
        result = jnp.where(lanes == i, jnp.sum(mine, axis=1, keepdims=True), result)
    own[...] = result


def fold_kernel(parts, out):
    total = parts[0]
    for j in range(1, DEPTHS):
        total = total + parts[j]
    for m in range(4):
        moved = pltpu.roll(total, (CB - 32 * m) % CB, 1) if m else total
        for r in range(8):
            out[4 * r + m] = moved[r : r + 1]


def final_kernel(parts, own, out):
    total = parts[0]
    for j in range(1, TILES):
        total = total + parts[j]
    over = pltpu.roll(total, CB - 16, 1)
    initial = own[...]
    real = iota((1, CB), 1) < 16
    bottom = jnp.where(real, over + 100.0 * initial, 1.0)
    out[...] = jnp.where(real, initial * total, 0.0) / bottom


def swap(pieces, axis):
    return lax.all_to_all(pieces, axis, 0, 0)


def body(
    volume,
    measured,
    point_spread,
    entry_block,
    entry_neuron,
    footprints,
    seed_plane,
    seed_row,
    seed_col,
    owner_slot,
):
    d = lax.axis_index("depth")
    t = lax.axis_index("tile")
    where = jnp.stack([d, t, (d * TILES + t) * 16]).astype(I32)
    table = owner_slot.reshape(64, CB)
    spread = jnp.pad(point_spread[0].astype(F32), ((0, ROWS - KS), (LIVE, CB - LIVE - KS)))
    windows, sensor = call(
        window_kernel,
        [((DEPTHS, ROWS, CB), F32), ((ROWS, CB), F32)],
        4,
        scalars=(0,),
        scratch=[pltpu.VMEM((ROWS, COLS + 2 * CB), F32)],
    )(where, volume[0], spread, measured)
    parts = swap(windows, "depth").reshape(DEPTHS * ROWS, CB)
    message = ((HALO * ROW + HALO, CB), F32)
    own, down, up = call(arrange_kernel, [((ROWS * ROW, CB), F32), message, message], 2)(parts, sensor)
    left = lax.ppermute(down, "tile", [(i, i + 1) for i in range(TILES - 1)])
    right = lax.ppermute(up, "tile", [(i + 1, i) for i in range(TILES - 1)])
    ahead, behind, scale = call(
        tables_kernel, [((256, DEEP), BF16), ((256, DEEP), BF16), ((ROW, CB), F32)], 1
    )(parts)
    weights = footprints[0].reshape(SLOTS, 512)
    gram, q_row, q_col, n_col, b_col = call(
        prepare_kernel,
        [
            ((SLOTS, SLOTS), F32),
            ((8, SLOTS), I32),
            ((SLOTS, CB), I32),
            ((SLOTS, CB), I32),
            ((SLOTS, CB), I32),
        ],
        4,
    )(entry_block, entry_neuron, weights, table)
    chunk = NEURONS // DEPTHS
    shape = (DEPTHS, 1, chunk)
    [sent] = call(
        iterate_kernel,
        [((DEPTHS, 24, CB), F32)],
        11,
        scalars=(0,),
        scratch=[
            pltpu.VMEM((96 * ROW, CB), F32),
            pltpu.VMEM((96 * ROW, CB), BF16),
            pltpu.VMEM((64 * ROW, CB), F32),
            pltpu.VMEM((64 * ROW, CB), BF16),
            pltpu.VMEM((96, CB), F32),
            pltpu.VMEM((256, CB), F32),
            pltpu.VMEM((80, CB), F32),
            pltpu.VMEM((4 * DEEP, CB), BF16),
            pltpu.VMEM((256, CB), F32),
        ],
    )(
        where,
        own,
        left,
        right,
        sensor,
        ahead,
        behind,
        scale,
        seed_plane.reshape(shape),
        seed_row.reshape(shape),
        seed_col.reshape(shape),
    )
    parts = swap(sent, "depth")
    [mine] = call(sum_kernel(DEPTHS, 16, TILES), [((TILES, 4, CB), F32)], 1)(parts)
    [mine] = call(sum_kernel(TILES, 0, DEPTHS), [((DEPTHS, 4, CB), F32)], 1)(swap(mine, "tile"))
    initial = swap(mine, "depth")
    estimate, proj = call(
        home_kernel,
        [((ROWS, COLS), F32), ((SLOTS, CB), F32)],
        3,
        scratch=[pltpu.VMEM((NCB * ROWS, CB), F32)],
    )(parts, weights, b_col)
    sent, own = call(slots_kernel, [((DEPTHS, 8, CB), F32), ((1, CB), F32)], 8, scalars=(0,))(
        where, initial, table, gram, q_row, q_col, n_col, proj
    )
    [sent] = call(fold_kernel, [((TILES, 1, CB), F32)], 1)(swap(sent, "depth"))
    [demixed] = call(final_kernel, [((1, CB), F32)], 2)(swap(sent, "tile"), own)
    return estimate[None], demixed[0, :16]


def solution(mesh):
    in_specs = (
        P("depth", "tile", None),
        P("tile", None),
        P("depth", None, None),
        P("tile", "depth"),
        P("tile", "depth"),
        P("tile", "depth", None, None),
        P(),
        P(),
        P(),
        P(),
    )
    out_specs = (P("depth", "tile", None), P(("depth", "tile")))
    return jax.shard_map(body, mesh=mesh, in_specs=in_specs, out_specs=out_specs, check_vma=False)
```

```python
import jax
import jax.numpy as jnp
from jax import lax
from jax.experimental import pallas as pl
from jax.experimental.pallas import tpu as pltpu
from jax.sharding import PartitionSpec as P

F32 = jnp.float32
BF16 = jnp.bfloat16
I32 = jnp.int32
KS = 13
RADIUS = 6
ROWS = 32
COLS = 1024
CB = 128
NCB = COLS // CB
DEPTHS = 16
TILES = 32
SLOTS = 256
NEURONS = 8192
HALO = 24
WIN = 64
LIVE = WIN + 2 * HALO
ROW = DEPTHS
BLOCK = 16
DEEP = 32 * ROW
VMEM = pl.BlockSpec(memory_space=pltpu.VMEM)
SMEM = pl.BlockSpec(memory_space=pltpu.SMEM)


def call(kernel, outs, n_in, scalars=(), scratch=(), mib=24):
    return pl.pallas_call(
        kernel,
        out_shape=[jax.ShapeDtypeStruct(s, t) for s, t in outs],
        in_specs=[SMEM if i in scalars else VMEM for i in range(n_in)],
        out_specs=[VMEM] * len(outs),
        scratch_shapes=list(scratch),
        compiler_params=pltpu.CompilerParams(vmem_limit_bytes=mib * 2**20),
    )


def iota(shape, dim):
    return lax.broadcasted_iota(I32, shape, dim)


def split2(x):
    high = x.astype(BF16)
    return high, (x - high.astype(F32)).astype(BF16)


def split3(x):
    high = x.astype(BF16)
    rest = x - high.astype(F32)
    mid = rest.astype(BF16)
    return high, mid, (rest - mid.astype(F32)).astype(BF16)


def column_of(row):
    n = row.shape[1]
    return jnp.transpose(jnp.broadcast_to(row, (CB, n)))


def prepare_kernel(block, neuron, weights, owner, gram, q_row, q_col, n_col, b_col):
    foot = weights[...]
    product = lax.dot_general(foot, foot, (((1,), (1,)), ((), ())), preferred_element_type=F32)
    blocks = column_of(block[...].astype(F32))
    neurons = column_of(neuron[...].astype(F32))
    same = jnp.concatenate([blocks, blocks], axis=1) == block[...].astype(F32)
    gram[...] = jnp.where(same, product, 0.0)
    n_int = neurons.astype(I32)
    n_col[...] = n_int
    b_col[...] = blocks.astype(I32)
    table = owner[...]
    tables = jnp.concatenate([(table >> 7).astype(F32), (table & 127).astype(F32)], axis=1).astype(BF16)
    hot = (iota((SLOTS, 64), 1) == (n_int[:, :64] >> 7)).astype(F32).astype(BF16)
    found = jnp.dot(hot, tables, preferred_element_type=F32)
    lane_hot = iota((SLOTS, CB), 1) == (n_int & 127)
    value = jnp.where(lane_hot, found[:, :CB] * 128.0 + found[:, CB:], 0.0)
    place = jnp.sum(value, axis=1, keepdims=True)
    place = jnp.broadcast_to(place, (SLOTS, CB))
    place = jnp.where(n_int >= 0, place, -1.0)
    q_col[...] = place.astype(I32)
    q_row[...] = jnp.transpose(place)[0:8, :].astype(I32)


def window_kernel(volume, spread, windows, local, arrived):
    copy = pltpu.make_async_copy(volume.at[0], local, arrived)
    copy.start()
    lane = iota((ROWS, CB), 1)
    taps = jnp.concatenate([spread[0].astype(F32), jnp.zeros((KS, CB - KS), F32)], axis=1)
    taps = jnp.concatenate([pltpu.roll(taps, LIVE, 1), jnp.zeros((ROWS - KS, CB), F32)], axis=0)
    zeros = jnp.zeros((ROWS, CB), F32)
    copy.wait()
    padded = jnp.concatenate([zeros, local[...], zeros], axis=1)
    for j in range(DEPTHS):
        start = CB - HALO + WIN * j
        low = start // CB * CB
        moved = pltpu.roll(padded[:, low : low + 2 * CB], 2 * CB - start % CB, 1)[:, :CB]
        windows[j] = jnp.where(lane < LIVE, moved, taps)


def arrange_kernel(where, parts, measured, own, sensor, down, up, wide):
    lane = iota((ROW, CB), 1)
    for r in range(ROWS):
        line = jnp.where(lane < LIVE, parts[pl.ds(r, ROW, stride=ROWS), :], 0.0)
        own[r * ROW : (r + 1) * ROW, :] = line
        if r < HALO:
            up[r * ROW : (r + 1) * ROW, :] = line.astype(BF16)
        if r >= ROWS - HALO:
            at = (r - ROWS + HALO) * ROW
            down[at : at + ROW, :] = line.astype(BF16)
    zeros = jnp.zeros((ROWS, CB), F32)
    wide[:, :CB] = zeros
    wide[:, CB : CB + COLS] = measured[...]
    wide[:, CB + COLS :] = zeros
    start = CB - HALO + WIN * where[0]
    low = pl.multiple_of((start >> 7) * CB, CB)
    moved = pltpu.roll(wide[:, pl.ds(low, 2 * CB)], 2 * CB - (start & (CB - 1)), 1)[:, :CB]
    view = jnp.where(iota((ROWS, CB), 1) < LIVE, moved, 0.0)
    sensor[...] = view
    for out, part in ((up, view[:HALO]), (down, view[ROWS - HALO :])):
        high = part.astype(BF16).astype(F32)
        out[HALO * ROW :, :] = jnp.concatenate([high, part - high], axis=0).astype(BF16)


def tables_kernel(parts, ahead, behind, scale):
    taps = jnp.concatenate([parts[pl.ds(a, ROW, stride=ROWS), :] for a in range(16)], axis=0)
    taps = jnp.where(iota((256, CB), 1) >= LIVE, taps, 0.0)
    first = jnp.transpose(taps)[LIVE:, :]
    first = jnp.concatenate([first, jnp.zeros((16, 256), F32)], axis=1)
    for i in range(BLOCK):
        moved = pltpu.roll(first, i * ROW, 1) if i else first
        ahead[i * 16 : (i + 1) * 16, :] = moved.astype(BF16)
    lane = iota((CB, DEEP), 1)
    hot = (iota((CB, DEEP), 0) == LIVE + KS - 1 - (lane >> 5)).astype(F32).astype(BF16)
    spread = jnp.dot(taps.astype(BF16), hot, preferred_element_type=F32)
    inside = iota((ROW, DEEP), 1)
    within = jnp.where(inside < KS * 32, inside & 31, 32)
    second = jnp.zeros((ROW, DEEP), F32)
    for a in range(KS):
        second = jnp.where(within == KS - 1 - a, spread[a * ROW : (a + 1) * ROW], second)
    for i in range(BLOCK):
        moved = pltpu.roll(second, i, 1) if i else second
        behind[i * ROW : (i + 1) * ROW, :] = moved.astype(BF16)
    total = taps[:ROW]
    for a in range(1, KS):
        total = total + taps[a * ROW : (a + 1) * ROW]
    norm = jnp.sum(total, axis=1, keepdims=True)
    scale[...] = jnp.broadcast_to(1.0 / norm, (ROW, CB))


def lane_shift(x, b):
    shift = (RADIUS - b) % CB
    return pltpu.roll(x, shift, 1) if shift else x


def iterate_kernel(
    where, own, left, right, sensor, ahead, behind, scale, s_plane, s_row, s_col,
    sent, exact, rounded, first, second, light, sums, ratio, stack, packed,
):
    rows = (HALO * ROW, (HALO + ROWS) * ROW, (2 * HALO + ROWS) * ROW)
    exact[: rows[0], :] = left[: rows[0]].astype(F32)
    exact[rows[0] : rows[1], :] = own[...]
    exact[rows[1] : rows[2], :] = right[: rows[0]].astype(F32)
    exact[rows[2] :, :] = jnp.zeros((16 * ROW, CB), F32)
    rounded[...] = exact[...].astype(BF16)
    before, after = left[rows[0] :].astype(F32), right[rows[0] :].astype(F32)
    light[:HALO, :] = before[:HALO] + before[HALO:]
    light[HALO : HALO + ROWS, :] = sensor[...]
    light[HALO + ROWS : 2 * HALO + ROWS, :] = after[:HALO] + after[HALO:]
    light[2 * HALO + ROWS :, :] = jnp.zeros((16, CB), F32)
    for m in range(4):
        stack[m * DEEP + KS * 32 : (m + 1) * DEEP, :] = jnp.zeros((DEEP - KS * 32, CB), BF16)
    tall = jnp.concatenate([scale[...]] * BLOCK, axis=0)

    def divide(source, blocks, offset, valid):
        for m in range(blocks):
            sums[...] = jnp.dot(
                ahead[...], source[m * 256 : m * 256 + DEEP, :], preferred_element_type=F32
            )
            total = lane_shift(sums[pl.ds(0, BLOCK, stride=16), :], 0)
            for b in range(1, KS):
                total = total + lane_shift(sums[pl.ds(b, BLOCK, stride=16), :], b)
            seen = light[m * BLOCK + offset : (m + 1) * BLOCK + offset, :]
            inside = (iota((BLOCK, CB), 0) < valid - m * BLOCK) & (seen != 0.0) & (total != 0.0)
            value = jnp.where(inside, seen / jnp.where(inside, total, 1.0), 0.0)
            ratio[m * BLOCK : (m + 1) * BLOCK, :] = value

    def spread_back(blocks):
        height = 16 * blocks + 16
        for b in range(KS):
            moved = lane_shift(ratio[:height, :], b).astype(BF16)
            for m in range(blocks):
                stack[m * DEEP + b * 32 : m * DEEP + (b + 1) * 32, :] = moved[m * 16 : m * 16 + 32]

    def back(m):
        value = jnp.dot(behind[...], stack[m * DEEP : (m + 1) * DEEP, :], preferred_element_type=F32)
        return value * tall

    divide(rounded, 5, 6, 68)
    spread_back(4)
    for m in range(4):
        value = exact[(m * 16 + 12) * ROW : (m * 16 + 28) * ROW, :] * back(m)
        first[m * 256 : (m + 1) * 256, :] = value
        second[m * 256 : (m + 1) * 256, :] = value.astype(BF16)
    divide(second, 3, 18, 44)
    spread_back(2)
    done = [first[(m * 16 + 12) * ROW : (m * 16 + 28) * ROW, :] * back(m) for m in range(2)]
    lane = iota((256, CB), 1)
    flat = jnp.where(lane < WIN, pltpu.roll(done[0], CB - HALO, 1), pltpu.roll(done[1], WIN - HALO, 1))
    packed[...] = flat
    for p in range(DEPTHS):
        sent[p, 0:16, :] = packed[pl.ds(p, 16, stride=ROW), :]
        sent[p, 20:24, :] = jnp.zeros((4, CB), F32)
    left_side = jnp.concatenate(split2(jnp.transpose(flat)), axis=0)
    chunk = NEURONS // DEPTHS
    for j in range(DEPTHS):
        plane, row, col = s_plane[j], s_row[j], s_col[j]
        local = ((row >> 5) == where[1]) & ((col >> 6) == where[0])
        key = jnp.where(local, (row & 15) * ROW + plane, -1)
        hot = (iota((256, chunk), 0) == key).astype(F32).astype(BF16)
        found = jnp.dot(left_side, hot, preferred_element_type=F32)
        found = found[:CB] + found[CB:]
        spot = ((row >> 4) & 1) * WIN + (col & (WIN - 1))
        picked = jnp.sum(jnp.where(iota((CB, chunk), 0) == spot, found, 0.0), axis=0, keepdims=True)
        for i in range(4):
            sent[j, 16 + i : 17 + i, :] = picked[:, i * CB : (i + 1) * CB]


def sum_kernel(count, at, copies):
    def kernel(parts, out):
        total = parts[0, at : at + 4, :]
        for j in range(1, count):
            total = total + parts[j, at : at + 4, :]
        for j in range(copies):
            out[j] = total

    return kernel


def home_kernel(parts, weights, b_col, estimate, proj, lines):
    lane = iota((16, CB), 1)
    for c in range(NCB):
        a, b = parts[2 * c, :16, :], parts[2 * c + 1, :16, :]
        top = jnp.where(lane < WIN, a, pltpu.roll(b, WIN, 1))
        bottom = jnp.where(lane < WIN, pltpu.roll(a, WIN, 1), b)
        estimate[:16, c * CB : (c + 1) * CB] = top
        estimate[16:, c * CB : (c + 1) * CB] = bottom
        lines[c * ROWS : c * ROWS + 16, :] = top
        lines[c * ROWS + 16 : (c + 1) * ROWS, :] = bottom
    blocks = [lines[pl.ds(br, 64, stride=4), :] for br in range(4)]
    blocked = jnp.concatenate(blocks, axis=1)
    number = b_col[:, :64]
    number = (number & 7) * 8 + (number >> 3)
    hot = (iota((SLOTS, 64), 1) == number).astype(F32).astype(BF16)
    high, low = split2(blocked)
    picked = jnp.dot(hot, high, preferred_element_type=F32) + jnp.dot(hot, low, preferred_element_type=F32)
    product = weights[...].astype(F32) * picked
    total = product[:, :CB]
    for br in range(1, 4):
        total = total + product[:, br * CB : (br + 1) * CB]
    proj[...] = jnp.broadcast_to(jnp.sum(total, axis=1, keepdims=True), (SLOTS, CB))


def slots_kernel(where, initial, owner, gram, q_row, q_col, n_col, proj, out, own):
    table = jnp.concatenate([initial[j] for j in range(DEPTHS)], axis=0)
    number = n_col[...]
    hot = (iota((SLOTS, 64), 1) == (number[:, :64] >> 7)).astype(F32).astype(BF16)
    parts = split3(table)
    found = jnp.dot(hot, parts[0], preferred_element_type=F32)
    found = found + jnp.dot(hot, parts[1], preferred_element_type=F32)
    found = found + jnp.dot(hot, parts[2], preferred_element_type=F32)
    value = jnp.where(iota((SLOTS, CB), 1) == (number & (CB - 1)), found, 0.0)
    start = jnp.broadcast_to(jnp.sum(value, axis=1, keepdims=True), (SLOTS, CB))
    start_row = jnp.transpose(start)[0:1, :]
    terms = gram[...] * start_row
    over = jnp.sum(terms[:, :CB] + terms[:, CB:], axis=1, keepdims=True)
    place = q_col[...]
    lane = iota((SLOTS, CB), 1)
    target = ((place >> 4) & 3) * 32 + (place & 15)
    sent = jnp.where(lane == target, proj[...], 0.0) + jnp.where(lane == target + 16, over, 0.0)
    row_hot = (iota((CB, SLOTS), 0) == (q_row[0:1, :] >> 6)).astype(F32).astype(BF16)
    parts = split3(sent)
    dense = jnp.dot(row_hot, parts[0], preferred_element_type=F32)
    dense = dense + jnp.dot(row_hot, parts[1], preferred_element_type=F32)
    dense = dense + jnp.dot(row_hot, parts[2], preferred_element_type=F32)
    for j in range(DEPTHS):
        out[j] = dense[j * 8 : (j + 1) * 8]
    base = where[2]
    holder = owner[...]
    lanes = iota((1, CB), 1)
    result = jnp.zeros((1, CB), F32)
    for i in range(16):
        mine = jnp.sum(jnp.where(holder == base + i, table, 0.0), axis=0, keepdims=True)
        result = jnp.where(lanes == i, jnp.sum(mine, axis=1, keepdims=True), result)
    own[...] = result


def fold_kernel(parts, out):
    total = parts[0]
    for j in range(1, DEPTHS):
        total = total + parts[j]
    for m in range(4):
        moved = pltpu.roll(total, (CB - 32 * m) % CB, 1) if m else total
        for r in range(8):
            out[4 * r + m] = moved[r : r + 1]


def final_kernel(parts, own, out):
    total = parts[0]
    for j in range(1, TILES):
        total = total + parts[j]
    over = pltpu.roll(total, CB - 16, 1)
    initial = own[...]
    real = iota((1, CB), 1) < 16
    bottom = jnp.where(real, over + 100.0 * initial, 1.0)
    out[...] = jnp.where(real, initial * total, 0.0) / bottom


def swap(pieces, axis):
    return lax.all_to_all(pieces, axis, 0, 0)


def body(
    volume,
    measured,
    point_spread,
    entry_block,
    entry_neuron,
    footprints,
    seed_plane,
    seed_row,
    seed_col,
    owner_slot,
):
    d = lax.axis_index("depth")
    t = lax.axis_index("tile")
    where = jnp.stack([d, t, (d * TILES + t) * 16]).astype(I32)
    table = owner_slot.reshape(64, CB)
    [windows] = pl.pallas_call(
        window_kernel,
        out_shape=[jax.ShapeDtypeStruct((DEPTHS, ROWS, CB), F32)],
        in_specs=[pl.BlockSpec(memory_space=pl.ANY), VMEM],
        out_specs=[VMEM],
        scratch_shapes=[pltpu.VMEM((ROWS, COLS), F32), pltpu.SemaphoreType.DMA],
        compiler_params=pltpu.CompilerParams(vmem_limit_bytes=24 * 2**20),
    )(volume, point_spread)
    parts = swap(windows, "depth").reshape(DEPTHS * ROWS, CB)
    message = ((HALO * ROW + 2 * HALO, CB), BF16)
    own, sensor, down, up = call(
        arrange_kernel,
        [((ROWS * ROW, CB), F32), ((ROWS, CB), F32), message, message],
        3,
        scalars=(0,),
        scratch=[pltpu.VMEM((ROWS, COLS + 2 * CB), F32)],
    )(where, parts, measured)
    left = lax.ppermute(down, "tile", [(i, i + 1) for i in range(TILES - 1)])
    right = lax.ppermute(up, "tile", [(i + 1, i) for i in range(TILES - 1)])
    ahead, behind, scale = call(
        tables_kernel, [((256, DEEP), BF16), ((256, DEEP), BF16), ((ROW, CB), F32)], 1
    )(parts)
    weights = footprints[0].reshape(SLOTS, 512)
    gram, q_row, q_col, n_col, b_col = call(
        prepare_kernel,
        [
            ((SLOTS, SLOTS), F32),
            ((8, SLOTS), I32),
            ((SLOTS, CB), I32),
            ((SLOTS, CB), I32),
            ((SLOTS, CB), I32),
        ],
        4,
    )(entry_block, entry_neuron, weights, table)
    chunk = NEURONS // DEPTHS
    shape = (DEPTHS, 1, chunk)
    [sent] = call(
        iterate_kernel,
        [((DEPTHS, 24, CB), F32)],
        11,
        scalars=(0,),
        scratch=[
            pltpu.VMEM((96 * ROW, CB), F32),
            pltpu.VMEM((96 * ROW, CB), BF16),
            pltpu.VMEM((64 * ROW, CB), F32),
            pltpu.VMEM((64 * ROW, CB), BF16),
            pltpu.VMEM((96, CB), F32),
            pltpu.VMEM((256, CB), F32),
            pltpu.VMEM((80, CB), F32),
            pltpu.VMEM((4 * DEEP, CB), BF16),
            pltpu.VMEM((256, CB), F32),
        ],
    )(
        where,
        own,
        left,
        right,
        sensor,
        ahead,
        behind,
        scale,
        seed_plane.reshape(shape),
        seed_row.reshape(shape),
        seed_col.reshape(shape),
    )
    parts = swap(sent, "depth")
    [mine] = call(sum_kernel(DEPTHS, 16, TILES), [((TILES, 4, CB), F32)], 1)(parts)
    [mine] = call(sum_kernel(TILES, 0, DEPTHS), [((DEPTHS, 4, CB), F32)], 1)(swap(mine, "tile"))
    initial = swap(mine, "depth")
    estimate, proj = call(
        home_kernel,
        [((ROWS, COLS), F32), ((SLOTS, CB), F32)],
        3,
        scratch=[pltpu.VMEM((NCB * ROWS, CB), F32)],
    )(parts, weights, b_col)
    sent, own = call(slots_kernel, [((DEPTHS, 8, CB), F32), ((1, CB), F32)], 8, scalars=(0,))(
        where, initial, table, gram, q_row, q_col, n_col, proj
    )
    [sent] = call(fold_kernel, [((TILES, 1, CB), F32)], 1)(swap(sent, "depth"))
    [demixed] = call(final_kernel, [((1, CB), F32)], 2)(swap(sent, "tile"), own)
    return estimate[None], demixed[0, :16]


def solution(mesh):
    in_specs = (
        P("depth", "tile", None),
        P("tile", None),
        P("depth", None, None),
        P("tile", "depth"),
        P("tile", "depth"),
        P("tile", "depth", None, None),
        P(),
        P(),
        P(),
        P(),
    )
    out_specs = (P("depth", "tile", None), P(("depth", "tile")))
    return jax.shard_map(body, mesh=mesh, in_specs=in_specs, out_specs=out_specs, check_vma=False)
```

```python
import jax
import jax.numpy as jnp
from jax import lax
from jax.experimental import pallas as pl
from jax.experimental.pallas import tpu as pltpu
from jax.sharding import PartitionSpec as P

F32 = jnp.float32
BF16 = jnp.bfloat16
I32 = jnp.int32
KS = 13
RADIUS = 6
ROWS = 32
COLS = 1024
CB = 128
NCB = COLS // CB
DEPTHS = 16
TILES = 32
SLOTS = 256
NEURONS = 8192
HALO = 24
WIN = 64
LIVE = WIN + 2 * HALO
ROW = DEPTHS
BLOCK = 16
DEEP = 32 * ROW
CAP = 64
NAMES = SLOTS + 16
VMEM = pl.BlockSpec(memory_space=pltpu.VMEM)
SMEM = pl.BlockSpec(memory_space=pltpu.SMEM)


def call(kernel, outs, n_in, scalars=(), scratch=(), mib=24):
    return pl.pallas_call(
        kernel,
        out_shape=[jax.ShapeDtypeStruct(s, t) for s, t in outs],
        in_specs=[SMEM if i in scalars else VMEM for i in range(n_in)],
        out_specs=[VMEM] * len(outs),
        scratch_shapes=list(scratch),
        compiler_params=pltpu.CompilerParams(vmem_limit_bytes=mib * 2**20),
    )


def iota(shape, dim):
    return lax.broadcasted_iota(I32, shape, dim)


def split2(x):
    high = x.astype(BF16)
    return high, (x - high.astype(F32)).astype(BF16)


def split3(x):
    high = x.astype(BF16)
    rest = x - high.astype(F32)
    mid = rest.astype(BF16)
    return high, mid, (rest - mid.astype(F32)).astype(BF16)


def column_of(row):
    n = row.shape[1]
    return jnp.transpose(jnp.broadcast_to(row, (CB, n)))


def lane_sum(x):
    return jnp.sum(x, axis=1, keepdims=True)


def prepare_kernel(
    where, block, neuron, weights, owner, s_plane, s_row, s_col,
    gram, q_row, q_col, b_col, a_row, a_lane, rank, code, first, most,
):
    foot = weights[...]
    product = lax.dot_general(foot, foot, (((1,), (1,)), ((), ())), preferred_element_type=F32)
    blocks = column_of(block[...].astype(F32))
    same = jnp.concatenate([blocks, blocks], axis=1) == block[...].astype(F32)
    gram[...] = jnp.where(same, product, 0.0)
    b_col[...] = blocks.astype(I32)
    table = owner[...]
    number = iota((64, CB), 0) * CB + iota((64, CB), 1)
    own = jnp.zeros((16, CB), F32)
    for i in range(16):
        hit = jnp.sum(jnp.where(table == where[2] + i, number.astype(F32), 0.0), axis=0, keepdims=True)
        own = jnp.where(iota((16, CB), 0) == i, lane_sum(hit), own)
    names = jnp.concatenate([column_of(neuron[...].astype(F32)), own], axis=0).astype(I32)
    row, col = s_row[...], s_col[...]
    tile, window = row >> 5, col >> 6
    tables = [tile, window, table >> 7, table & 127]
    tables = jnp.concatenate([x.astype(F32) for x in tables], axis=1).astype(BF16)
    hot = (iota((NAMES, 64), 1) == (names[:, :64] >> 7)).astype(F32).astype(BF16)
    found = jnp.dot(hot, tables, preferred_element_type=F32)
    lane_hot = iota((NAMES, CB), 1) == (names & 127)
    picked = [lane_sum(jnp.where(lane_hot, found[:, i * CB : (i + 1) * CB], 0.0)) for i in range(4)]
    n_tile, n_window = picked[0].astype(I32), picked[1].astype(I32)
    place = jnp.broadcast_to(picked[2] * 128.0 + picked[3], (NAMES, CB))[:SLOTS]
    place = jnp.where(names[:SLOTS] >= 0, place, -1.0)
    q_col[...] = place.astype(I32)
    q_row[...] = jnp.transpose(place)[0:8, :].astype(I32)
    keys = (tile * DEPTHS + window) * NEURONS + number
    low = jnp.broadcast_to((n_tile * DEPTHS + n_window) * NEURONS, (NAMES, CB))
    high = low + names
    count = jnp.zeros((NAMES, CB), F32)
    for r in range(64):
        key = keys[r : r + 1, :]
        count = count + jnp.where((key >= low) & (key < high), 1.0, 0.0)
    position = jnp.broadcast_to(lane_sum(count), (NAMES, CB)).astype(I32)
    at = (position // CAP) * 256 + n_tile * 8 + (n_window >> 1)
    a_row[...] = jnp.where(names >= 0, at, -1)
    a_lane[...] = (n_window & 1) * CAP + position % CAP
    local = (tile == where[1]) & (window == where[0])
    mask = local.astype(F32)
    before = (iota((CB, CB), 0) < iota((CB, CB), 1)).astype(F32).astype(BF16)
    inside = jnp.dot(mask.astype(BF16), before, preferred_element_type=F32)
    rows = jnp.broadcast_to(lane_sum(mask), (64, CB)).astype(BF16)
    above = (iota((64, 64), 1) < iota((64, 64), 0)).astype(F32).astype(BF16)
    inside = inside + jnp.dot(above, rows, preferred_element_type=F32)
    order = jnp.where(local, inside, -1.0).astype(I32)
    spot = ((row >> 4) & 1) * WIN + (col & (WIN - 1))
    coded = ((row & 15) * ROW + s_plane[...]) * CB + spot + 1
    rank[...] = order
    code[...] = coded
    first[...] = listed(order, coded, 0)
    both = jnp.zeros((TILES, DEPTHS), F32)
    for r in range(0, 64, 8):
        tiles = [iota((TILES, CB), 0) == tile[i : i + 1, :] for i in range(r, r + 8)]
        windows = [iota((DEPTHS, CB), 0) == window[i : i + 1, :] for i in range(r, r + 8)]
        tiles = jnp.concatenate([x.astype(F32) for x in tiles], axis=1).astype(BF16)
        windows = jnp.concatenate([x.astype(F32) for x in windows], axis=1).astype(BF16)
        both = both + lax.dot_general(
            tiles, windows, (((1,), (1,)), ((), ())), preferred_element_type=F32
        )
    top = jnp.max(jnp.max(both, axis=0, keepdims=True), axis=1, keepdims=True)
    most[...] = jnp.broadcast_to(top, (8, CB)).astype(I32)


def listed(order, coded, start):
    result = jnp.zeros((CAP, CB), F32)
    wanted = iota((CAP, CB), 0) + start
    for r in range(64):
        result = result + jnp.where(
            wanted == order[r : r + 1, :], coded[r : r + 1, :].astype(F32), 0.0
        )
    return jnp.broadcast_to(lane_sum(result), (CAP, CB)).astype(I32)


def seed_values(codes, flat):
    index = codes - 1
    key = jnp.concatenate([index, index], axis=1) >> 7
    hot = (iota((CAP, 256), 1) == key).astype(F32).astype(BF16)
    parts = split3(flat)
    found = jnp.dot(hot, parts[0], preferred_element_type=F32)
    found = found + jnp.dot(hot, parts[1], preferred_element_type=F32)
    found = found + jnp.dot(hot, parts[2], preferred_element_type=F32)
    value = lane_sum(jnp.where(iota((CAP, CB), 1) == (index & (CB - 1)), found, 0.0))
    value = jnp.broadcast_to(value, (CAP, CB))
    return jnp.transpose(jnp.concatenate([value, value], axis=0))[0:1, :]


def window_kernel(volume, spread, windows, local, arrived):
    copy = pltpu.make_async_copy(volume.at[0], local, arrived)
    copy.start()
    lane = iota((ROWS, CB), 1)
    taps = jnp.concatenate([spread[0].astype(F32), jnp.zeros((KS, CB - KS), F32)], axis=1)
    taps = jnp.concatenate([pltpu.roll(taps, LIVE, 1), jnp.zeros((ROWS - KS, CB), F32)], axis=0)
    zeros = jnp.zeros((ROWS, CB), F32)
    copy.wait()
    padded = jnp.concatenate([zeros, local[...], zeros], axis=1)
    for j in range(DEPTHS):
        start = CB - HALO + WIN * j
        low = start // CB * CB
        moved = pltpu.roll(padded[:, low : low + 2 * CB], 2 * CB - start % CB, 1)[:, :CB]
        windows[j] = jnp.where(lane < LIVE, moved, taps)


def arrange_kernel(where, parts, measured, own, sensor, down, up, wide):
    lane = iota((ROW, CB), 1)
    for r in range(ROWS):
        line = jnp.where(lane < LIVE, parts[pl.ds(r, ROW, stride=ROWS), :], 0.0)
        own[r * ROW : (r + 1) * ROW, :] = line
        if r < HALO:
            up[r * ROW : (r + 1) * ROW, :] = line.astype(BF16)
        if r >= ROWS - HALO:
            at = (r - ROWS + HALO) * ROW
            down[at : at + ROW, :] = line.astype(BF16)
    zeros = jnp.zeros((ROWS, CB), F32)
    wide[:, :CB] = zeros
    wide[:, CB : CB + COLS] = measured[...]
    wide[:, CB + COLS :] = zeros
    start = CB - HALO + WIN * where[0]
    low = pl.multiple_of((start >> 7) * CB, CB)
    moved = pltpu.roll(wide[:, pl.ds(low, 2 * CB)], 2 * CB - (start & (CB - 1)), 1)[:, :CB]
    view = jnp.where(iota((ROWS, CB), 1) < LIVE, moved, 0.0)
    sensor[...] = view
    for out, part in ((up, view[:HALO]), (down, view[ROWS - HALO :])):
        high = part.astype(BF16).astype(F32)
        out[HALO * ROW :, :] = jnp.concatenate([high, part - high], axis=0).astype(BF16)


def tables_kernel(parts, ahead, behind, scale):
    taps = jnp.concatenate([parts[pl.ds(a, ROW, stride=ROWS), :] for a in range(16)], axis=0)
    taps = jnp.where(iota((256, CB), 1) >= LIVE, taps, 0.0)
    first = jnp.transpose(taps)[LIVE:, :]
    first = jnp.concatenate([first, jnp.zeros((16, 256), F32)], axis=1)
    for i in range(BLOCK):
        moved = pltpu.roll(first, i * ROW, 1) if i else first
        ahead[i * 16 : (i + 1) * 16, :] = moved.astype(BF16)
    lane = iota((CB, DEEP), 1)
    hot = (iota((CB, DEEP), 0) == LIVE + KS - 1 - (lane >> 5)).astype(F32).astype(BF16)
    spread = jnp.dot(taps.astype(BF16), hot, preferred_element_type=F32)
    inside = iota((ROW, DEEP), 1)
    within = jnp.where(inside < KS * 32, inside & 31, 32)
    second = jnp.zeros((ROW, DEEP), F32)
    for a in range(KS):
        second = jnp.where(within == KS - 1 - a, spread[a * ROW : (a + 1) * ROW], second)
    for i in range(BLOCK):
        moved = pltpu.roll(second, i, 1) if i else second
        behind[i * ROW : (i + 1) * ROW, :] = moved.astype(BF16)
    total = taps[:ROW]
    for a in range(1, KS):
        total = total + taps[a * ROW : (a + 1) * ROW]
    norm = jnp.sum(total, axis=1, keepdims=True)
    scale[...] = jnp.broadcast_to(1.0 / norm, (ROW, CB))


def lane_shift(x, b):
    shift = (RADIUS - b) % CB
    return pltpu.roll(x, shift, 1) if shift else x


def iterate_kernel(
    own, left, right, sensor, ahead, behind, scale, codes,
    sent, flat, exact, rounded, first, second, light, sums, ratio, stack,
):
    rows = (HALO * ROW, (HALO + ROWS) * ROW, (2 * HALO + ROWS) * ROW)
    exact[: rows[0], :] = left[: rows[0]].astype(F32)
    exact[rows[0] : rows[1], :] = own[...]
    exact[rows[1] : rows[2], :] = right[: rows[0]].astype(F32)
    exact[rows[2] :, :] = jnp.zeros((16 * ROW, CB), F32)
    rounded[...] = exact[...].astype(BF16)
    before, after = left[rows[0] :].astype(F32), right[rows[0] :].astype(F32)
    light[:HALO, :] = before[:HALO] + before[HALO:]
    light[HALO : HALO + ROWS, :] = sensor[...]
    light[HALO + ROWS : 2 * HALO + ROWS, :] = after[:HALO] + after[HALO:]
    light[2 * HALO + ROWS :, :] = jnp.zeros((16, CB), F32)
    for m in range(4):
        stack[m * DEEP + KS * 32 : (m + 1) * DEEP, :] = jnp.zeros((DEEP - KS * 32, CB), BF16)
    tall = jnp.concatenate([scale[...]] * BLOCK, axis=0)

    def divide(source, blocks, offset, valid):
        for m in range(blocks):
            sums[...] = jnp.dot(
                ahead[...], source[m * 256 : m * 256 + DEEP, :], preferred_element_type=F32
            )
            total = lane_shift(sums[pl.ds(0, BLOCK, stride=16), :], 0)
            for b in range(1, KS):
                total = total + lane_shift(sums[pl.ds(b, BLOCK, stride=16), :], b)
            seen = light[m * BLOCK + offset : (m + 1) * BLOCK + offset, :]
            inside = (iota((BLOCK, CB), 0) < valid - m * BLOCK) & (seen != 0.0) & (total != 0.0)
            value = jnp.where(inside, seen / jnp.where(inside, total, 1.0), 0.0)
            ratio[m * BLOCK : (m + 1) * BLOCK, :] = value

    def spread_back(blocks):
        height = 16 * blocks + 16
        for b in range(KS):
            moved = lane_shift(ratio[:height, :], b).astype(BF16)
            for m in range(blocks):
                stack[m * DEEP + b * 32 : m * DEEP + (b + 1) * 32, :] = moved[m * 16 : m * 16 + 32]

    def back(m):
        value = jnp.dot(behind[...], stack[m * DEEP : (m + 1) * DEEP, :], preferred_element_type=F32)
        return value * tall

    divide(rounded, 5, 6, 68)
    spread_back(4)
    for m in range(4):
        value = exact[(m * 16 + 12) * ROW : (m * 16 + 28) * ROW, :] * back(m)
        first[m * 256 : (m + 1) * 256, :] = value
        second[m * 256 : (m + 1) * 256, :] = value.astype(BF16)
    divide(second, 3, 18, 44)
    spread_back(2)
    done = [first[(m * 16 + 12) * ROW : (m * 16 + 28) * ROW, :] * back(m) for m in range(2)]
    lane = iota((256, CB), 1)
    packed = jnp.where(lane < WIN, pltpu.roll(done[0], CB - HALO, 1), pltpu.roll(done[1], WIN - HALO, 1))
    flat[...] = packed
    values = jnp.broadcast_to(seed_values(codes[...], packed), (8, CB))
    for p in range(DEPTHS):
        sent[p, 0:16, :] = flat[pl.ds(p, 16, stride=ROW), :]
        sent[p, 16:24, :] = values


def more_kernel(start, rank, code, flat, sent):
    codes = listed(rank[...], code[...], start[0])
    values = jnp.broadcast_to(seed_values(codes, flat[...]), (8, CB))
    for p in range(DEPTHS):
        sent[p] = values


def gather_kernel(at):
    def kernel(parts, out):
        lane = iota((1, CB), 1)
        rows = [
            jnp.where(lane < CAP, parts[2 * m, at : at + 1, :], parts[2 * m + 1, at : at + 1, :])
            for m in range(8)
        ]
        total = jnp.concatenate(rows, axis=0)
        for j in range(TILES):
            out[j] = total

    return kernel


def look_kernel(start, parts, a_row, a_lane, known, out):
    table = jnp.concatenate([parts[t] for t in range(TILES)], axis=0)
    row = a_row[...] - start[0] * (256 // CAP)
    hot = (iota((NAMES, 256), 1) == jnp.concatenate([row, row], axis=1)).astype(F32).astype(BF16)
    parts = split3(table)
    found = jnp.dot(hot, parts[0], preferred_element_type=F32)
    found = found + jnp.dot(hot, parts[1], preferred_element_type=F32)
    found = found + jnp.dot(hot, parts[2], preferred_element_type=F32)
    value = lane_sum(jnp.where(iota((NAMES, CB), 1) == a_lane[...], found, 0.0))
    out[...] = known[...] + jnp.broadcast_to(value, (NAMES, CB))


def home_kernel(parts, weights, b_col, estimate, proj, lines):
    lane = iota((16, CB), 1)
    for c in range(NCB):
        a, b = parts[2 * c, :16, :], parts[2 * c + 1, :16, :]
        top = jnp.where(lane < WIN, a, pltpu.roll(b, WIN, 1))
        bottom = jnp.where(lane < WIN, pltpu.roll(a, WIN, 1), b)
        estimate[:16, c * CB : (c + 1) * CB] = top
        estimate[16:, c * CB : (c + 1) * CB] = bottom
        lines[c * ROWS : c * ROWS + 16, :] = top
        lines[c * ROWS + 16 : (c + 1) * ROWS, :] = bottom
    blocks = [lines[pl.ds(br, 64, stride=4), :] for br in range(4)]
    blocked = jnp.concatenate(blocks, axis=1)
    number = b_col[:, :64]
    number = (number & 7) * 8 + (number >> 3)
    hot = (iota((SLOTS, 64), 1) == number).astype(F32).astype(BF16)
    high, low = split2(blocked)
    picked = jnp.dot(hot, high, preferred_element_type=F32) + jnp.dot(hot, low, preferred_element_type=F32)
    product = weights[...].astype(F32) * picked
    total = product[:, :CB]
    for br in range(1, 4):
        total = total + product[:, br * CB : (br + 1) * CB]
    proj[...] = jnp.broadcast_to(jnp.sum(total, axis=1, keepdims=True), (SLOTS, CB))


def slots_kernel(start, gram, q_row, q_col, proj, out, own):
    padded = jnp.concatenate([start[...], jnp.zeros((3 * CB - NAMES, CB), F32)], axis=0)
    row = jnp.transpose(padded)[0:1, :]
    own[...] = row[:, SLOTS:]
    start_row = row[:, :SLOTS]
    terms = gram[...] * start_row
    over = jnp.sum(terms[:, :CB] + terms[:, CB:], axis=1, keepdims=True)
    place = q_col[...]
    lane = iota((SLOTS, CB), 1)
    target = ((place >> 4) & 3) * 32 + (place & 15)
    sent = jnp.where(lane == target, proj[...], 0.0) + jnp.where(lane == target + 16, over, 0.0)
    row_hot = (iota((CB, SLOTS), 0) == (q_row[0:1, :] >> 6)).astype(F32).astype(BF16)
    parts = split3(sent)
    dense = jnp.dot(row_hot, parts[0], preferred_element_type=F32)
    dense = dense + jnp.dot(row_hot, parts[1], preferred_element_type=F32)
    dense = dense + jnp.dot(row_hot, parts[2], preferred_element_type=F32)
    for j in range(DEPTHS):
        out[j] = dense[j * 8 : (j + 1) * 8]


def fold_kernel(parts, out):
    total = parts[0]
    for j in range(1, DEPTHS):
        total = total + parts[j]
    for m in range(4):
        moved = pltpu.roll(total, (CB - 32 * m) % CB, 1) if m else total
        for r in range(8):
            out[4 * r + m] = moved[r : r + 1]


def final_kernel(parts, own, out):
    total = parts[0]
    for j in range(1, TILES):
        total = total + parts[j]
    over = pltpu.roll(total, CB - 16, 1)
    initial = own[...]
    real = iota((1, CB), 1) < 16
    bottom = jnp.where(real, over + 100.0 * initial, 1.0)
    out[...] = jnp.where(real, initial * total, 0.0) / bottom


def swap(pieces, axis):
    return lax.all_to_all(pieces, axis, 0, 0)


def body(
    volume,
    measured,
    point_spread,
    entry_block,
    entry_neuron,
    footprints,
    seed_plane,
    seed_row,
    seed_col,
    owner_slot,
):
    d = lax.axis_index("depth")
    t = lax.axis_index("tile")
    where = jnp.stack([d, t, (d * TILES + t) * 16]).astype(I32)
    table = owner_slot.reshape(64, CB)
    [windows] = pl.pallas_call(
        window_kernel,
        out_shape=[jax.ShapeDtypeStruct((DEPTHS, ROWS, CB), F32)],
        in_specs=[pl.BlockSpec(memory_space=pl.ANY), VMEM],
        out_specs=[VMEM],
        scratch_shapes=[pltpu.VMEM((ROWS, COLS), F32), pltpu.SemaphoreType.DMA],
        compiler_params=pltpu.CompilerParams(vmem_limit_bytes=24 * 2**20),
    )(volume, point_spread)
    parts = swap(windows, "depth").reshape(DEPTHS * ROWS, CB)
    message = ((HALO * ROW + 2 * HALO, CB), BF16)
    own, sensor, down, up = call(
        arrange_kernel,
        [((ROWS * ROW, CB), F32), ((ROWS, CB), F32), message, message],
        3,
        scalars=(0,),
        scratch=[pltpu.VMEM((ROWS, COLS + 2 * CB), F32)],
    )(where, parts, measured)
    left = lax.ppermute(down, "tile", [(i, i + 1) for i in range(TILES - 1)])
    right = lax.ppermute(up, "tile", [(i + 1, i) for i in range(TILES - 1)])
    ahead, behind, scale = call(
        tables_kernel, [((256, DEEP), BF16), ((256, DEEP), BF16), ((ROW, CB), F32)], 1
    )(parts)
    weights = footprints[0].reshape(SLOTS, 512)
    column = ((SLOTS, CB), I32)
    names = ((NAMES, CB), I32)
    square = ((64, CB), I32)
    gram, q_row, q_col, b_col, a_row, a_lane, rank, code, first, most = call(
        prepare_kernel,
        [
            ((SLOTS, SLOTS), F32),
            ((8, SLOTS), I32),
            column,
            column,
            names,
            names,
            square,
            square,
            ((CAP, CB), I32),
            ((8, CB), I32),
        ],
        8,
        scalars=(0,),
    )(
        where,
        entry_block,
        entry_neuron,
        weights,
        table,
        seed_plane.reshape(64, CB),
        seed_row.reshape(64, CB),
        seed_col.reshape(64, CB),
    )
    sent, flat = call(
        iterate_kernel,
        [((DEPTHS, 24, CB), F32), ((256, CB), F32)],
        8,
        scratch=[
            pltpu.VMEM((96 * ROW, CB), F32),
            pltpu.VMEM((96 * ROW, CB), BF16),
            pltpu.VMEM((64 * ROW, CB), F32),
            pltpu.VMEM((64 * ROW, CB), BF16),
            pltpu.VMEM((96, CB), F32),
            pltpu.VMEM((256, CB), F32),
            pltpu.VMEM((80, CB), F32),
            pltpu.VMEM((4 * DEEP, CB), BF16),
        ],
    )(own, left, right, sensor, ahead, behind, scale, first)
    parts = swap(sent, "depth")

    def share(values, at):
        [values] = call(gather_kernel(at), [((TILES, 8, CB), F32)], 1)(values)
        return swap(values, "tile")

    def look(begin, values, known):
        return call(look_kernel, [((NAMES, CB), F32)], 5, scalars=(0,))(
            begin, values, a_row, a_lane, known
        )[0]

    def another(step, known):
        begin = jnp.reshape(step * CAP, (1,))
        [values] = call(more_kernel, [((DEPTHS, 8, CB), F32)], 4, scalars=(0,))(
            begin, rank, code, flat
        )
        return look(begin, share(swap(values, "depth"), 0), known)

    known = look(jnp.zeros((1,), I32), share(parts, 16), jnp.zeros((NAMES, CB), F32))
    known = lax.fori_loop(1, (most[0, 0] + CAP - 1) // CAP, another, known)
    estimate, proj = call(
        home_kernel,
        [((ROWS, COLS), F32), ((SLOTS, CB), F32)],
        3,
        scratch=[pltpu.VMEM((NCB * ROWS, CB), F32)],
    )(parts, weights, b_col)
    sent, own = call(slots_kernel, [((DEPTHS, 8, CB), F32), ((1, CB), F32)], 5)(
        known, gram, q_row, q_col, proj
    )
    [sent] = call(fold_kernel, [((TILES, 1, CB), F32)], 1)(swap(sent, "depth"))
    [demixed] = call(final_kernel, [((1, CB), F32)], 2)(swap(sent, "tile"), own)
    return estimate[None], demixed[0, :16]


def solution(mesh):
    in_specs = (
        P("depth", "tile", None),
        P("tile", None),
        P("depth", None, None),
        P("tile", "depth"),
        P("tile", "depth"),
        P("tile", "depth", None, None),
        P(),
        P(),
        P(),
        P(),
    )
    out_specs = (P("depth", "tile", None), P(("depth", "tile")))
    return jax.shard_map(body, mesh=mesh, in_specs=in_specs, out_specs=out_specs, check_vma=False)
```

```python
import jax
import jax.numpy as jnp
from jax import lax
from jax.experimental import pallas as pl
from jax.experimental.pallas import tpu as pltpu
from jax.sharding import PartitionSpec as P

F32 = jnp.float32
BF16 = jnp.bfloat16
I32 = jnp.int32
KS = 13
RADIUS = 6
ROWS = 32
COLS = 1024
CB = 128
NCB = COLS // CB
DEPTHS = 16
TILES = 32
SLOTS = 256
NEURONS = 8192
HALO = 24
WIN = 64
LIVE = WIN + 2 * HALO
ROW = DEPTHS
BLOCK = 16
DEEP = 32 * ROW
CAP = 64
NAMES = SLOTS + 16
VMEM = pl.BlockSpec(memory_space=pltpu.VMEM)
SMEM = pl.BlockSpec(memory_space=pltpu.SMEM)


def call(kernel, outs, n_in, scalars=(), scratch=(), mib=24):
    return pl.pallas_call(
        kernel,
        out_shape=[jax.ShapeDtypeStruct(s, t) for s, t in outs],
        in_specs=[SMEM if i in scalars else VMEM for i in range(n_in)],
        out_specs=[VMEM] * len(outs),
        scratch_shapes=list(scratch),
        compiler_params=pltpu.CompilerParams(vmem_limit_bytes=mib * 2**20),
    )


def iota(shape, dim):
    return lax.broadcasted_iota(I32, shape, dim)


def split2(x):
    high = x.astype(BF16)
    return high, (x - high.astype(F32)).astype(BF16)


def split3(x):
    high = x.astype(BF16)
    rest = x - high.astype(F32)
    mid = rest.astype(BF16)
    return high, mid, (rest - mid.astype(F32)).astype(BF16)


def column_of(row):
    n = row.shape[1]
    return jnp.transpose(jnp.broadcast_to(row, (CB, n)))


def lane_sum(x):
    return jnp.sum(x, axis=1, keepdims=True)


def prepare_kernel(
    where, block, neuron, weights, owner, s_plane, s_row, s_col,
    gram, q_row, q_col, b_col, a_row, a_lane, rank, code, first, most,
):
    foot = weights[...]
    product = lax.dot_general(foot, foot, (((1,), (1,)), ((), ())), preferred_element_type=F32)
    blocks = column_of(block[...].astype(F32))
    same = jnp.concatenate([blocks, blocks], axis=1) == block[...].astype(F32)
    gram[...] = jnp.where(same, product, 0.0)
    b_col[...] = blocks.astype(I32)
    table = owner[...]
    number = iota((64, CB), 0) * CB + iota((64, CB), 1)
    own = jnp.zeros((16, CB), F32)
    for i in range(16):
        hit = jnp.sum(jnp.where(table == where[2] + i, number.astype(F32), 0.0), axis=0, keepdims=True)
        own = jnp.where(iota((16, CB), 0) == i, lane_sum(hit), own)
    names = jnp.concatenate([column_of(neuron[...].astype(F32)), own], axis=0).astype(I32)
    row, col = s_row[...], s_col[...]
    tile, window = row >> 5, col >> 6
    tables = [tile, window, table >> 7, table & 127]
    tables = jnp.concatenate([x.astype(F32) for x in tables], axis=1).astype(BF16)
    hot = (iota((NAMES, 64), 1) == (names[:, :64] >> 7)).astype(F32).astype(BF16)
    found = jnp.dot(hot, tables, preferred_element_type=F32)
    lane_hot = iota((NAMES, CB), 1) == (names & 127)
    picked = [lane_sum(jnp.where(lane_hot, found[:, i * CB : (i + 1) * CB], 0.0)) for i in range(4)]
    n_tile, n_window = picked[0].astype(I32), picked[1].astype(I32)
    place = jnp.broadcast_to(picked[2] * 128.0 + picked[3], (NAMES, CB))[:SLOTS]
    place = jnp.where(names[:SLOTS] >= 0, place, -1.0)
    q_col[...] = place.astype(I32)
    q_row[...] = jnp.transpose(place)[0:8, :].astype(I32)
    keys = (tile * DEPTHS + window) * NEURONS + number
    low = jnp.broadcast_to((n_tile * DEPTHS + n_window) * NEURONS, (NAMES, CB))
    high = low + names
    count = jnp.zeros((NAMES, CB), F32)
    for r in range(64):
        key = keys[r : r + 1, :]
        count = count + jnp.where((key >= low) & (key < high), 1.0, 0.0)
    position = jnp.broadcast_to(lane_sum(count), (NAMES, CB)).astype(I32)
    at = (position // CAP) * 256 + n_tile * 8 + (n_window >> 1)
    a_row[...] = jnp.where(names >= 0, at, -1)
    a_lane[...] = (n_window & 1) * CAP + position % CAP
    local = (tile == where[1]) & (window == where[0])
    mask = local.astype(F32)
    before = (iota((CB, CB), 0) < iota((CB, CB), 1)).astype(F32).astype(BF16)
    inside = jnp.dot(mask.astype(BF16), before, preferred_element_type=F32)
    rows = jnp.broadcast_to(lane_sum(mask), (64, CB)).astype(BF16)
    above = (iota((64, 64), 1) < iota((64, 64), 0)).astype(F32).astype(BF16)
    inside = inside + jnp.dot(above, rows, preferred_element_type=F32)
    order = jnp.where(local, inside, -1.0).astype(I32)
    spot = ((row >> 4) & 1) * WIN + (col & (WIN - 1))
    coded = ((row & 15) * ROW + s_plane[...]) * CB + spot + 1
    rank[...] = order
    code[...] = coded
    first[...] = listed(order, coded, 0)
    both = jnp.zeros((TILES, DEPTHS), F32)
    for r in range(0, 64, 8):
        tiles = [iota((TILES, CB), 0) == tile[i : i + 1, :] for i in range(r, r + 8)]
        windows = [iota((DEPTHS, CB), 0) == window[i : i + 1, :] for i in range(r, r + 8)]
        tiles = jnp.concatenate([x.astype(F32) for x in tiles], axis=1).astype(BF16)
        windows = jnp.concatenate([x.astype(F32) for x in windows], axis=1).astype(BF16)
        both = both + lax.dot_general(
            tiles, windows, (((1,), (1,)), ((), ())), preferred_element_type=F32
        )
    top = jnp.max(jnp.max(both, axis=0, keepdims=True), axis=1, keepdims=True)
    most[...] = (jnp.broadcast_to(top, (8, CB)).astype(I32) + (CAP - 1)) >> 6


def listed(order, coded, start):
    result = jnp.zeros((CAP, CB), F32)
    wanted = iota((CAP, CB), 0) + start
    for r in range(64):
        result = result + jnp.where(
            wanted == order[r : r + 1, :], coded[r : r + 1, :].astype(F32), 0.0
        )
    return jnp.broadcast_to(lane_sum(result), (CAP, CB)).astype(I32)


def seed_values(codes, flat):
    index = codes - 1
    key = jnp.concatenate([index, index], axis=1) >> 7
    hot = (iota((CAP, 256), 1) == key).astype(F32).astype(BF16)
    parts = split3(flat)
    found = jnp.dot(hot, parts[0], preferred_element_type=F32)
    found = found + jnp.dot(hot, parts[1], preferred_element_type=F32)
    found = found + jnp.dot(hot, parts[2], preferred_element_type=F32)
    value = lane_sum(jnp.where(iota((CAP, CB), 1) == (index & (CB - 1)), found, 0.0))
    value = jnp.broadcast_to(value, (CAP, CB))
    return jnp.transpose(jnp.concatenate([value, value], axis=0))[0:1, :]


def window_kernel(volume, point_spread, windows, local, spread, arrived):
    small = pltpu.make_async_copy(point_spread, spread, arrived.at[1])
    small.start()
    copy = pltpu.make_async_copy(volume.at[0], local, arrived.at[0])
    copy.start()
    small.wait()
    lane = iota((ROWS, CB), 1)
    taps = jnp.concatenate([spread[0].astype(F32), jnp.zeros((KS, CB - KS), F32)], axis=1)
    taps = jnp.concatenate([pltpu.roll(taps, LIVE, 1), jnp.zeros((ROWS - KS, CB), F32)], axis=0)
    zeros = jnp.zeros((ROWS, CB), F32)
    copy.wait()
    padded = jnp.concatenate([zeros, local[...], zeros], axis=1)
    for j in range(DEPTHS):
        start = CB - HALO + WIN * j
        low = start // CB * CB
        moved = pltpu.roll(padded[:, low : low + 2 * CB], 2 * CB - start % CB, 1)[:, :CB]
        windows[j] = jnp.where(lane < LIVE, moved, taps)


def arrange_kernel(where, parts, measured, own, sensor, down, up, wide):
    lane = iota((ROW, CB), 1)
    for r in range(ROWS):
        line = jnp.where(lane < LIVE, parts[pl.ds(r, ROW, stride=ROWS), :], 0.0)
        own[r * ROW : (r + 1) * ROW, :] = line
        if r < HALO:
            up[r * ROW : (r + 1) * ROW, :] = line.astype(BF16)
        if r >= ROWS - HALO:
            at = (r - ROWS + HALO) * ROW
            down[at : at + ROW, :] = line.astype(BF16)
    zeros = jnp.zeros((ROWS, CB), F32)
    wide[:, :CB] = zeros
    wide[:, CB : CB + COLS] = measured[...]
    wide[:, CB + COLS :] = zeros
    start = CB - HALO + WIN * where[0]
    low = pl.multiple_of((start >> 7) * CB, CB)
    moved = pltpu.roll(wide[:, pl.ds(low, 2 * CB)], 2 * CB - (start & (CB - 1)), 1)[:, :CB]
    view = jnp.where(iota((ROWS, CB), 1) < LIVE, moved, 0.0)
    sensor[...] = view
    for out, part in ((up, view[:HALO]), (down, view[ROWS - HALO :])):
        high = part.astype(BF16).astype(F32)
        out[HALO * ROW :, :] = jnp.concatenate([high, part - high], axis=0).astype(BF16)


def tables_kernel(parts, ahead, behind, scale):
    taps = jnp.concatenate([parts[pl.ds(a, ROW, stride=ROWS), :] for a in range(16)], axis=0)
    taps = jnp.where(iota((256, CB), 1) >= LIVE, taps, 0.0)
    first = jnp.transpose(taps)[LIVE:, :]
    first = jnp.concatenate([first, jnp.zeros((16, 256), F32)], axis=1)
    for i in range(BLOCK):
        moved = pltpu.roll(first, i * ROW, 1) if i else first
        ahead[i * 16 : (i + 1) * 16, :] = moved.astype(BF16)
    lane = iota((CB, DEEP), 1)
    hot = (iota((CB, DEEP), 0) == LIVE + KS - 1 - (lane >> 5)).astype(F32).astype(BF16)
    spread = jnp.dot(taps.astype(BF16), hot, preferred_element_type=F32)
    inside = iota((ROW, DEEP), 1)
    within = jnp.where(inside < KS * 32, inside & 31, 32)
    second = jnp.zeros((ROW, DEEP), F32)
    for a in range(KS):
        second = jnp.where(within == KS - 1 - a, spread[a * ROW : (a + 1) * ROW], second)
    for i in range(BLOCK):
        moved = pltpu.roll(second, i, 1) if i else second
        behind[i * ROW : (i + 1) * ROW, :] = moved.astype(BF16)
    total = taps[:ROW]
    for a in range(1, KS):
        total = total + taps[a * ROW : (a + 1) * ROW]
    norm = jnp.sum(total, axis=1, keepdims=True)
    scale[...] = jnp.broadcast_to(1.0 / norm, (ROW, CB))


def lane_shift(x, b):
    shift = (RADIUS - b) % CB
    return pltpu.roll(x, shift, 1) if shift else x


def iterate_kernel(
    own, left, right, sensor, ahead, behind, scale, codes,
    sent, flat, exact, rounded, first, second, light, sums, ratio, stack,
):
    rows = (HALO * ROW, (HALO + ROWS) * ROW, (2 * HALO + ROWS) * ROW)
    exact[: rows[0], :] = left[: rows[0]].astype(F32)
    exact[rows[0] : rows[1], :] = own[...]
    exact[rows[1] : rows[2], :] = right[: rows[0]].astype(F32)
    exact[rows[2] :, :] = jnp.zeros((16 * ROW, CB), F32)
    rounded[...] = exact[...].astype(BF16)
    before, after = left[rows[0] :].astype(F32), right[rows[0] :].astype(F32)
    light[:HALO, :] = before[:HALO] + before[HALO:]
    light[HALO : HALO + ROWS, :] = sensor[...]
    light[HALO + ROWS : 2 * HALO + ROWS, :] = after[:HALO] + after[HALO:]
    light[2 * HALO + ROWS :, :] = jnp.zeros((16, CB), F32)
    for m in range(4):
        stack[m * DEEP + KS * 32 : (m + 1) * DEEP, :] = jnp.zeros((DEEP - KS * 32, CB), BF16)
    tall = jnp.concatenate([scale[...]] * BLOCK, axis=0)

    def divide(source, blocks, offset, valid):
        for m in range(blocks):
            sums[...] = jnp.dot(
                ahead[...], source[m * 256 : m * 256 + DEEP, :], preferred_element_type=F32
            )
            total = lane_shift(sums[pl.ds(0, BLOCK, stride=16), :], 0)
            for b in range(1, KS):
                total = total + lane_shift(sums[pl.ds(b, BLOCK, stride=16), :], b)
            seen = light[m * BLOCK + offset : (m + 1) * BLOCK + offset, :]
            inside = (iota((BLOCK, CB), 0) < valid - m * BLOCK) & (seen != 0.0) & (total != 0.0)
            value = jnp.where(inside, seen / jnp.where(inside, total, 1.0), 0.0)
            ratio[m * BLOCK : (m + 1) * BLOCK, :] = value

    def spread_back(blocks):
        height = 16 * blocks + 16
        for b in range(KS):
            moved = lane_shift(ratio[:height, :], b).astype(BF16)
            for m in range(blocks):
                stack[m * DEEP + b * 32 : m * DEEP + (b + 1) * 32, :] = moved[m * 16 : m * 16 + 32]

    def back(m):
        value = jnp.dot(behind[...], stack[m * DEEP : (m + 1) * DEEP, :], preferred_element_type=F32)
        return value * tall

    divide(rounded, 5, 6, 68)
    spread_back(4)
    for m in range(4):
        value = exact[(m * 16 + 12) * ROW : (m * 16 + 28) * ROW, :] * back(m)
        first[m * 256 : (m + 1) * 256, :] = value
        second[m * 256 : (m + 1) * 256, :] = value.astype(BF16)
    divide(second, 3, 18, 44)
    spread_back(2)
    done = [first[(m * 16 + 12) * ROW : (m * 16 + 28) * ROW, :] * back(m) for m in range(2)]
    lane = iota((256, CB), 1)
    packed = jnp.where(lane < WIN, pltpu.roll(done[0], CB - HALO, 1), pltpu.roll(done[1], WIN - HALO, 1))
    flat[...] = packed
    values = jnp.broadcast_to(seed_values(codes[...], packed), (8, CB))
    for p in range(DEPTHS):
        sent[p, 0:16, :] = flat[pl.ds(p, 16, stride=ROW), :]
        sent[p, 16:24, :] = values


def more_kernel(start, rank, code, flat, sent):
    codes = listed(rank[...], code[...], start[0])
    values = jnp.broadcast_to(seed_values(codes, flat[...]), (8, CB))
    for p in range(DEPTHS):
        sent[p] = values


def gather_kernel(at):
    def kernel(parts, out):
        lane = iota((1, CB), 1)
        rows = [
            jnp.where(lane < CAP, parts[2 * m, at : at + 1, :], parts[2 * m + 1, at : at + 1, :])
            for m in range(8)
        ]
        total = jnp.concatenate(rows, axis=0)
        for j in range(TILES):
            out[j] = total

    return kernel


def look_kernel(start, parts, a_row, a_lane, known, out):
    table = jnp.concatenate([parts[t] for t in range(TILES)], axis=0)
    row = a_row[...] - start[0] * (256 // CAP)
    hot = (iota((NAMES, 256), 1) == jnp.concatenate([row, row], axis=1)).astype(F32).astype(BF16)
    parts = split3(table)
    found = jnp.dot(hot, parts[0], preferred_element_type=F32)
    found = found + jnp.dot(hot, parts[1], preferred_element_type=F32)
    found = found + jnp.dot(hot, parts[2], preferred_element_type=F32)
    value = lane_sum(jnp.where(iota((NAMES, CB), 1) == a_lane[...], found, 0.0))
    out[...] = known[...] + jnp.broadcast_to(value, (NAMES, CB))


def home_kernel(parts, weights, b_col, estimate, proj, lines):
    lane = iota((16, CB), 1)
    for c in range(NCB):
        a, b = parts[2 * c, :16, :], parts[2 * c + 1, :16, :]
        top = jnp.where(lane < WIN, a, pltpu.roll(b, WIN, 1))
        bottom = jnp.where(lane < WIN, pltpu.roll(a, WIN, 1), b)
        estimate[:16, c * CB : (c + 1) * CB] = top
        estimate[16:, c * CB : (c + 1) * CB] = bottom
        lines[c * ROWS : c * ROWS + 16, :] = top
        lines[c * ROWS + 16 : (c + 1) * ROWS, :] = bottom
    blocks = [lines[pl.ds(br, 64, stride=4), :] for br in range(4)]
    blocked = jnp.concatenate(blocks, axis=1)
    number = b_col[:, :64]
    number = (number & 7) * 8 + (number >> 3)
    hot = (iota((SLOTS, 64), 1) == number).astype(F32).astype(BF16)
    high, low = split2(blocked)
    picked = jnp.dot(hot, high, preferred_element_type=F32) + jnp.dot(hot, low, preferred_element_type=F32)
    product = weights[...].astype(F32) * picked
    total = product[:, :CB]
    for br in range(1, 4):
        total = total + product[:, br * CB : (br + 1) * CB]
    proj[...] = jnp.broadcast_to(jnp.sum(total, axis=1, keepdims=True), (SLOTS, CB))


def slots_kernel(start, gram, q_row, q_col, proj, out, own):
    padded = jnp.concatenate([start[...], jnp.zeros((3 * CB - NAMES, CB), F32)], axis=0)
    row = jnp.transpose(padded)[0:1, :]
    own[...] = row[:, SLOTS:]
    start_row = row[:, :SLOTS]
    terms = gram[...] * start_row
    over = jnp.sum(terms[:, :CB] + terms[:, CB:], axis=1, keepdims=True)
    place = q_col[...]
    lane = iota((SLOTS, CB), 1)
    target = ((place >> 4) & 3) * 32 + (place & 15)
    sent = jnp.where(lane == target, proj[...], 0.0) + jnp.where(lane == target + 16, over, 0.0)
    row_hot = (iota((CB, SLOTS), 0) == (q_row[0:1, :] >> 6)).astype(F32).astype(BF16)
    parts = split3(sent)
    dense = jnp.dot(row_hot, parts[0], preferred_element_type=F32)
    dense = dense + jnp.dot(row_hot, parts[1], preferred_element_type=F32)
    dense = dense + jnp.dot(row_hot, parts[2], preferred_element_type=F32)
    for j in range(DEPTHS):
        out[j] = dense[j * 8 : (j + 1) * 8]


def fold_kernel(parts, out):
    total = parts[0]
    for j in range(1, DEPTHS):
        total = total + parts[j]
    for m in range(4):
        moved = pltpu.roll(total, (CB - 32 * m) % CB, 1) if m else total
        for r in range(8):
            out[4 * r + m] = moved[r : r + 1]


def final_kernel(parts, own, out):
    total = parts[0]
    for j in range(1, TILES):
        total = total + parts[j]
    over = pltpu.roll(total, CB - 16, 1)
    initial = own[...]
    real = iota((1, CB), 1) < 16
    bottom = jnp.where(real, over + 100.0 * initial, 1.0)
    out[...] = (jnp.where(real, initial * total, 0.0) / bottom)[:, :16]


def swap(pieces, axis):
    return lax.all_to_all(pieces, axis, 0, 0)


def body(
    volume,
    measured,
    point_spread,
    entry_block,
    entry_neuron,
    footprints,
    seed_plane,
    seed_row,
    seed_col,
    owner_slot,
):
    d = lax.axis_index("depth")
    t = lax.axis_index("tile")
    where = jnp.stack([d, t, (d * TILES + t) * 16]).astype(I32)
    table = owner_slot.reshape(64, CB)
    [windows] = pl.pallas_call(
        window_kernel,
        out_shape=[jax.ShapeDtypeStruct((DEPTHS, ROWS, CB), F32)],
        in_specs=[pl.BlockSpec(memory_space=pltpu.HBM)] * 2,
        out_specs=[VMEM],
        scratch_shapes=[
            pltpu.VMEM((ROWS, COLS), F32),
            pltpu.VMEM((1, KS, KS), BF16),
            pltpu.SemaphoreType.DMA((2,)),
        ],
        compiler_params=pltpu.CompilerParams(vmem_limit_bytes=24 * 2**20),
    )(volume, point_spread)
    parts = swap(windows, "depth").reshape(DEPTHS * ROWS, CB)
    message = ((HALO * ROW + 2 * HALO, CB), BF16)
    weights = footprints[0].reshape(SLOTS, 512)
    column = ((SLOTS, CB), I32)
    names = ((NAMES, CB), I32)
    square = ((64, CB), I32)
    gram, q_row, q_col, b_col, a_row, a_lane, rank, code, first, most = call(
        prepare_kernel,
        [
            ((SLOTS, SLOTS), F32),
            ((8, SLOTS), I32),
            column,
            column,
            names,
            names,
            square,
            square,
            ((CAP, CB), I32),
            ((8, CB), I32),
        ],
        8,
        scalars=(0,),
    )(
        where,
        entry_block,
        entry_neuron,
        weights,
        table,
        seed_plane.reshape(64, CB),
        seed_row.reshape(64, CB),
        seed_col.reshape(64, CB),
    )
    view, first, rounds = lax.optimization_barrier((measured, first, most[0, 0]))
    own, sensor, down, up = call(
        arrange_kernel,
        [((ROWS * ROW, CB), F32), ((ROWS, CB), F32), message, message],
        3,
        scalars=(0,),
        scratch=[pltpu.VMEM((ROWS, COLS + 2 * CB), F32)],
    )(where, parts, view)
    left = lax.ppermute(down, "tile", [(i, i + 1) for i in range(TILES - 1)])
    right = lax.ppermute(up, "tile", [(i + 1, i) for i in range(TILES - 1)])
    ahead, behind, scale = call(
        tables_kernel, [((256, DEEP), BF16), ((256, DEEP), BF16), ((ROW, CB), F32)], 1
    )(parts)
    sent, flat = call(
        iterate_kernel,
        [((DEPTHS, 24, CB), F32), ((256, CB), F32)],
        8,
        scratch=[
            pltpu.VMEM((96 * ROW, CB), F32),
            pltpu.VMEM((96 * ROW, CB), BF16),
            pltpu.VMEM((64 * ROW, CB), F32),
            pltpu.VMEM((64 * ROW, CB), BF16),
            pltpu.VMEM((96, CB), F32),
            pltpu.VMEM((256, CB), F32),
            pltpu.VMEM((80, CB), F32),
            pltpu.VMEM((4 * DEEP, CB), BF16),
        ],
    )(own, left, right, sensor, ahead, behind, scale, first)
    parts = swap(sent, "depth")

    def share(values, at):
        [values] = call(gather_kernel(at), [((TILES, 8, CB), F32)], 1)(values)
        return swap(values, "tile")

    def look(begin, values, known):
        return call(look_kernel, [((NAMES, CB), F32)], 5, scalars=(0,))(
            begin, values, a_row, a_lane, known
        )[0]

    def another(step, known):
        begin = jnp.reshape(step * CAP, (1,))
        [values] = call(more_kernel, [((DEPTHS, 8, CB), F32)], 4, scalars=(0,))(
            begin, rank, code, flat
        )
        return look(begin, share(swap(values, "depth"), 0), known)

    shared, parts = lax.optimization_barrier((share(parts, 16), parts))
    known = look(jnp.zeros((1,), I32), shared, jnp.zeros((NAMES, CB), F32))
    known = lax.fori_loop(1, rounds, another, known)
    estimate, proj = call(
        home_kernel,
        [((ROWS, COLS), F32), ((SLOTS, CB), F32)],
        3,
        scratch=[pltpu.VMEM((NCB * ROWS, CB), F32)],
    )(parts, weights, b_col)
    sent, own = call(slots_kernel, [((DEPTHS, 8, CB), F32), ((1, CB), F32)], 5)(
        known, gram, q_row, q_col, proj
    )
    [sent] = call(fold_kernel, [((TILES, 1, CB), F32)], 1)(swap(sent, "depth"))
    [demixed] = call(final_kernel, [((1, 16), F32)], 2)(swap(sent, "tile"), own)
    return estimate[None], demixed[0]


def solution(mesh):
    in_specs = (
        P("depth", "tile", None),
        P("tile", None),
        P("depth", None, None),
        P("tile", "depth"),
        P("tile", "depth"),
        P("tile", "depth", None, None),
        P(),
        P(),
        P(),
        P(),
    )
    out_specs = (P("depth", "tile", None), P(("depth", "tile")))
    return jax.shard_map(body, mesh=mesh, in_specs=in_specs, out_specs=out_specs, check_vma=False)
```

```python
import jax
import jax.numpy as jnp
from jax import lax
from jax.experimental import pallas as pl
from jax.experimental.pallas import tpu as pltpu
from jax.sharding import PartitionSpec as P

F32 = jnp.float32
BF16 = jnp.bfloat16
I32 = jnp.int32
KS = 13
RADIUS = 6
ROWS = 32
COLS = 1024
CB = 128
NCB = COLS // CB
DEPTHS = 16
TILES = 32
SLOTS = 256
NEURONS = 8192
HALO = 24
WIN = 64
LIVE = WIN + 2 * HALO
ROW = DEPTHS
BLOCK = 16
DEEP = 32 * ROW
CAP = 384
LANES = CAP // CB
NAMES = SLOTS + 16
VMEM = pl.BlockSpec(memory_space=pltpu.VMEM)
SMEM = pl.BlockSpec(memory_space=pltpu.SMEM)


def call(kernel, outs, n_in, scalars=(), scratch=(), mib=24):
    return pl.pallas_call(
        kernel,
        out_shape=[jax.ShapeDtypeStruct(s, t) for s, t in outs],
        in_specs=[SMEM if i in scalars else VMEM for i in range(n_in)],
        out_specs=[VMEM] * len(outs),
        scratch_shapes=list(scratch),
        compiler_params=pltpu.CompilerParams(vmem_limit_bytes=mib * 2**20),
    )


def iota(shape, dim):
    return lax.broadcasted_iota(I32, shape, dim)


def split2(x):
    high = x.astype(BF16)
    return high, (x - high.astype(F32)).astype(BF16)


def split3(x):
    high = x.astype(BF16)
    rest = x - high.astype(F32)
    mid = rest.astype(BF16)
    return high, mid, (rest - mid.astype(F32)).astype(BF16)


def column_of(row):
    n = row.shape[1]
    return jnp.transpose(jnp.broadcast_to(row, (CB, n)))


def lane_sum(x):
    return jnp.sum(x, axis=1, keepdims=True)


def prepare_kernel(
    where, block, neuron, weights, owner, s_plane, s_row, s_col,
    gram, q_row, q_col, b_col, a_row, a_lane, rank, code, first, most,
):
    foot = weights[...]
    product = lax.dot_general(foot, foot, (((1,), (1,)), ((), ())), preferred_element_type=F32)
    blocks = column_of(block[...].astype(F32))
    same = jnp.concatenate([blocks, blocks], axis=1) == block[...].astype(F32)
    gram[...] = jnp.where(same, product, 0.0)
    b_col[...] = blocks.astype(I32)
    table = owner[...]
    number = iota((64, CB), 0) * CB + iota((64, CB), 1)
    own = jnp.zeros((16, CB), F32)
    for i in range(16):
        hit = jnp.sum(jnp.where(table == where[2] + i, number.astype(F32), 0.0), axis=0, keepdims=True)
        own = jnp.where(iota((16, CB), 0) == i, lane_sum(hit), own)
    names = jnp.concatenate([column_of(neuron[...].astype(F32)), own], axis=0).astype(I32)
    row, col = s_row[...], s_col[...]
    tile, window = row >> 5, col >> 6
    tables = [tile, table >> 7, table & 127]
    tables = jnp.concatenate([x.astype(F32) for x in tables], axis=1).astype(BF16)
    hot = (iota((NAMES, 64), 1) == (names[:, :64] >> 7)).astype(F32).astype(BF16)
    found = jnp.dot(hot, tables, preferred_element_type=F32)
    lane_hot = iota((NAMES, CB), 1) == (names & 127)
    picked = [lane_sum(jnp.where(lane_hot, found[:, i * CB : (i + 1) * CB], 0.0)) for i in range(3)]
    n_tile = picked[0].astype(I32)
    place = jnp.broadcast_to(picked[1] * 128.0 + picked[2], (NAMES, CB))[:SLOTS]
    place = jnp.where(names[:SLOTS] >= 0, place, -1.0)
    q_col[...] = place.astype(I32)
    q_row[...] = jnp.transpose(place)[0:8, :].astype(I32)
    keys = tile * NEURONS + number
    low = jnp.broadcast_to(n_tile * NEURONS, (NAMES, CB))
    high = low + names
    count = jnp.zeros((NAMES, CB), F32)
    for r in range(64):
        key = keys[r : r + 1, :]
        count = count + jnp.where((key >= low) & (key < high), 1.0, 0.0)
    position = jnp.broadcast_to(lane_sum(count), (NAMES, CB)).astype(I32)
    turn = jnp.zeros((NAMES, CB), I32)
    for i in range(1, (NEURONS + CAP - 1) // CAP):
        turn = turn + (position >= i * CAP).astype(I32)
    a_row[...] = jnp.where(names >= 0, turn * TILES + n_tile, -1)
    a_lane[...] = position - turn * CAP
    local = tile == where[1]
    mask = local.astype(F32)
    before = (iota((CB, CB), 0) < iota((CB, CB), 1)).astype(F32).astype(BF16)
    inside = jnp.dot(mask.astype(BF16), before, preferred_element_type=F32)
    rows = jnp.broadcast_to(lane_sum(mask), (64, CB)).astype(BF16)
    above = (iota((64, 64), 1) < iota((64, 64), 0)).astype(F32).astype(BF16)
    inside = inside + jnp.dot(above, rows, preferred_element_type=F32)
    order = jnp.where(local & (window == where[0]), inside, -1.0).astype(I32)
    spot = ((row >> 4) & 1) * WIN + (col & (WIN - 1))
    coded = ((row & 15) * ROW + s_plane[...]) * CB + spot
    rank[...] = order
    code[...] = coded
    first[...] = listed(order, coded, 0)
    both = jnp.zeros((TILES, 1), F32)
    for r in range(0, 64, 8):
        tiles = jnp.zeros((TILES, CB), F32)
        for i in range(r, r + 8):
            tiles = tiles + (iota((TILES, CB), 0) == tile[i : i + 1, :]).astype(F32)
        both = both + lane_sum(tiles)
    top = jnp.max(both, axis=0, keepdims=True)
    most[...] = jnp.broadcast_to(top, (8, CB)).astype(I32)


def listed(order, coded, start):
    place = order - start
    place = jnp.where(place < CAP, place, -1)
    total = jnp.zeros((32, CB), F32)
    for r in range(0, 64, 8):
        lines = [place[i : i + 1, :] for i in range(r, r + 8)]
        codes = [coded[i : i + 1, :] for i in range(r, r + 8)]
        left = []
        for at, code in zip(lines, codes):
            here = iota((8, CB), 0) == (at >> 7)
            left.append(
                jnp.concatenate(
                    [
                        jnp.where(here, (code >> 7).astype(F32), 0.0),
                        jnp.where(here, (code & 127).astype(F32), 0.0),
                        jnp.where(here, 1.0, 0.0),
                        jnp.zeros((8, CB), F32),
                    ],
                    axis=0,
                )
            )
        left = jnp.concatenate(left, axis=1).astype(BF16)
        right = [(iota((CB, CB), 0) == jnp.where(at >= 0, at & 127, -1)).astype(F32) for at in lines]
        right = jnp.concatenate(right, axis=1).astype(BF16)
        total = total + lax.dot_general(
            left, right, (((1,), (1,)), ((), ())), preferred_element_type=F32
        )
    value = total[0:8] * 128.0 + total[8:16]
    return jnp.where(total[16:24] > 0.0, value, -1.0).astype(I32)


def seed_values(codes, flat):
    parts = split3(flat)
    result = []
    for i in range(LANES):
        index = column_of(codes[i : i + 1, :].astype(F32)).astype(I32)
        key = jnp.concatenate([index, index], axis=1) >> 7
        hot = (iota((CB, 256), 1) == key).astype(F32).astype(BF16)
        found = jnp.dot(hot, parts[0], preferred_element_type=F32)
        found = found + jnp.dot(hot, parts[1], preferred_element_type=F32)
        found = found + jnp.dot(hot, parts[2], preferred_element_type=F32)
        picked = jnp.where(iota((CB, CB), 1) == (index & (CB - 1)), found, 0.0)
        result.append(jnp.sum(jnp.transpose(picked), axis=0, keepdims=True))
    result.append(jnp.zeros((8 - LANES, CB), F32))
    return jnp.concatenate(result, axis=0)


def window_kernel(volume, spread, windows):
    lane = iota((ROWS, CB), 1)
    taps = jnp.concatenate([spread[0].astype(F32), jnp.zeros((KS, CB - KS), F32)], axis=1)
    taps = jnp.concatenate([pltpu.roll(taps, LIVE, 1), jnp.zeros((ROWS - KS, CB), F32)], axis=0)
    zeros = jnp.zeros((ROWS, CB), F32)
    padded = jnp.concatenate([zeros, volume[0], zeros], axis=1)
    for j in range(DEPTHS):
        start = CB - HALO + WIN * j
        low = start // CB * CB
        moved = pltpu.roll(padded[:, low : low + 2 * CB], 2 * CB - start % CB, 1)[:, :CB]
        windows[j] = jnp.where(lane < LIVE, moved, taps)


def arrange_kernel(where, parts, measured, own, sensor, down, up, wide):
    lane = iota((ROW, CB), 1)
    for r in range(ROWS):
        line = jnp.where(lane < LIVE, parts[pl.ds(r, ROW, stride=ROWS), :], 0.0)
        own[r * ROW : (r + 1) * ROW, :] = line
        if r < HALO:
            up[r * ROW : (r + 1) * ROW, :] = line.astype(BF16)
        if r >= ROWS - HALO:
            at = (r - ROWS + HALO) * ROW
            down[at : at + ROW, :] = line.astype(BF16)
    zeros = jnp.zeros((ROWS, CB), F32)
    wide[:, :CB] = zeros
    wide[:, CB : CB + COLS] = measured[...]
    wide[:, CB + COLS :] = zeros
    start = CB - HALO + WIN * where[0]
    low = pl.multiple_of((start >> 7) * CB, CB)
    moved = pltpu.roll(wide[:, pl.ds(low, 2 * CB)], 2 * CB - (start & (CB - 1)), 1)[:, :CB]
    view = jnp.where(iota((ROWS, CB), 1) < LIVE, moved, 0.0)
    sensor[...] = view
    for out, part in ((up, view[:HALO]), (down, view[ROWS - HALO :])):
        high = part.astype(BF16).astype(F32)
        out[HALO * ROW :, :] = jnp.concatenate([high, part - high], axis=0).astype(BF16)


def tables_kernel(parts, ahead, behind, scale):
    taps = jnp.concatenate([parts[pl.ds(a, ROW, stride=ROWS), :] for a in range(16)], axis=0)
    taps = jnp.where(iota((256, CB), 1) >= LIVE, taps, 0.0)
    first = jnp.transpose(taps)[LIVE:, :]
    first = jnp.concatenate([first, jnp.zeros((16, 256), F32)], axis=1)
    for i in range(BLOCK):
        moved = pltpu.roll(first, i * ROW, 1) if i else first
        ahead[i * 16 : (i + 1) * 16, :] = moved.astype(BF16)
    lane = iota((CB, DEEP), 1)
    hot = (iota((CB, DEEP), 0) == LIVE + KS - 1 - (lane >> 5)).astype(F32).astype(BF16)
    spread = jnp.dot(taps.astype(BF16), hot, preferred_element_type=F32)
    inside = iota((ROW, DEEP), 1)
    within = jnp.where(inside < KS * 32, inside & 31, 32)
    second = jnp.zeros((ROW, DEEP), F32)
    for a in range(KS):
        second = jnp.where(within == KS - 1 - a, spread[a * ROW : (a + 1) * ROW], second)
    for i in range(BLOCK):
        moved = pltpu.roll(second, i, 1) if i else second
        behind[i * ROW : (i + 1) * ROW, :] = moved.astype(BF16)
    total = taps[:ROW]
    for a in range(1, KS):
        total = total + taps[a * ROW : (a + 1) * ROW]
    norm = jnp.sum(total, axis=1, keepdims=True)
    scale[...] = jnp.broadcast_to(1.0 / norm, (ROW, CB))


def lane_shift(x, b):
    shift = (RADIUS - b) % CB
    return pltpu.roll(x, shift, 1) if shift else x


def iterate_kernel(
    own, left, right, sensor, ahead, behind, scale, codes,
    sent, flat, exact, rounded, first, second, light, sums, ratio, stack,
):
    rows = (HALO * ROW, (HALO + ROWS) * ROW, (2 * HALO + ROWS) * ROW)
    exact[: rows[0], :] = left[: rows[0]].astype(F32)
    exact[rows[0] : rows[1], :] = own[...]
    exact[rows[1] : rows[2], :] = right[: rows[0]].astype(F32)
    exact[rows[2] :, :] = jnp.zeros((16 * ROW, CB), F32)
    rounded[...] = exact[...].astype(BF16)
    before, after = left[rows[0] :].astype(F32), right[rows[0] :].astype(F32)
    light[:HALO, :] = before[:HALO] + before[HALO:]
    light[HALO : HALO + ROWS, :] = sensor[...]
    light[HALO + ROWS : 2 * HALO + ROWS, :] = after[:HALO] + after[HALO:]
    light[2 * HALO + ROWS :, :] = jnp.zeros((16, CB), F32)
    for m in range(4):
        stack[m * DEEP + KS * 32 : (m + 1) * DEEP, :] = jnp.zeros((DEEP - KS * 32, CB), BF16)
    tall = jnp.concatenate([scale[...]] * BLOCK, axis=0)

    def divide(source, blocks, offset, valid):
        for m in range(blocks):
            sums[...] = jnp.dot(
                ahead[...], source[m * 256 : m * 256 + DEEP, :], preferred_element_type=F32
            )
            total = lane_shift(sums[pl.ds(0, BLOCK, stride=16), :], 0)
            for b in range(1, KS):
                total = total + lane_shift(sums[pl.ds(b, BLOCK, stride=16), :], b)
            seen = light[m * BLOCK + offset : (m + 1) * BLOCK + offset, :]
            inside = (iota((BLOCK, CB), 0) < valid - m * BLOCK) & (seen != 0.0) & (total != 0.0)
            value = jnp.where(inside, seen / jnp.where(inside, total, 1.0), 0.0)
            ratio[m * BLOCK : (m + 1) * BLOCK, :] = value

    def spread_back(blocks):
        height = 16 * blocks + 16
        for b in range(KS):
            moved = lane_shift(ratio[:height, :], b).astype(BF16)
            for m in range(blocks):
                stack[m * DEEP + b * 32 : m * DEEP + (b + 1) * 32, :] = moved[m * 16 : m * 16 + 32]

    def back(m):
        value = jnp.dot(behind[...], stack[m * DEEP : (m + 1) * DEEP, :], preferred_element_type=F32)
        return value * tall

    divide(rounded, 5, 6, 68)
    spread_back(4)
    for m in range(4):
        value = exact[(m * 16 + 12) * ROW : (m * 16 + 28) * ROW, :] * back(m)
        first[m * 256 : (m + 1) * 256, :] = value
        second[m * 256 : (m + 1) * 256, :] = value.astype(BF16)
    divide(second, 3, 18, 44)
    spread_back(2)
    done = [first[(m * 16 + 12) * ROW : (m * 16 + 28) * ROW, :] * back(m) for m in range(2)]
    lane = iota((256, CB), 1)
    packed = jnp.where(lane < WIN, pltpu.roll(done[0], CB - HALO, 1), pltpu.roll(done[1], WIN - HALO, 1))
    flat[...] = packed
    values = seed_values(codes[...], packed)
    for p in range(DEPTHS):
        sent[p, 0:16, :] = flat[pl.ds(p, 16, stride=ROW), :]
        sent[p, 16:24, :] = values


def more_kernel(turn, rank, code, flat, sent):
    codes = listed(rank[...], code[...], turn[0] * CAP)
    values = seed_values(codes, flat[...])
    for p in range(DEPTHS):
        sent[p] = values


def gather_kernel(at):
    def kernel(parts, out):
        total = parts[0, at : at + 8, :]
        for j in range(1, DEPTHS):
            total = total + parts[j, at : at + 8, :]
        line = jnp.concatenate([total[i : i + 1, :] for i in range(LANES)], axis=1)
        for j in range(TILES):
            out[j] = line

    return kernel


def look_kernel(turn, parts, a_row, a_lane, known, out):
    table = jnp.concatenate([parts[t] for t in range(TILES)], axis=0)
    row = a_row[...] - turn[0] * TILES
    hot = (iota((NAMES, TILES), 1) == row[:, :TILES]).astype(F32).astype(BF16)
    parts = split3(table)
    found = jnp.dot(hot, parts[0], preferred_element_type=F32)
    found = found + jnp.dot(hot, parts[1], preferred_element_type=F32)
    found = found + jnp.dot(hot, parts[2], preferred_element_type=F32)
    total = jnp.zeros((NAMES, CB), F32)
    for i in range(LANES):
        here = iota((NAMES, CB), 1) + i * CB == a_lane[...]
        total = total + jnp.where(here, found[:, i * CB : (i + 1) * CB], 0.0)
    out[...] = known[...] + jnp.broadcast_to(lane_sum(total), (NAMES, CB))


def home_kernel(parts, weights, b_col, estimate, proj, lines):
    lane = iota((16, CB), 1)
    for c in range(NCB):
        a, b = parts[2 * c, :16, :], parts[2 * c + 1, :16, :]
        top = jnp.where(lane < WIN, a, pltpu.roll(b, WIN, 1))
        bottom = jnp.where(lane < WIN, pltpu.roll(a, WIN, 1), b)
        estimate[:16, c * CB : (c + 1) * CB] = top
        estimate[16:, c * CB : (c + 1) * CB] = bottom
        lines[c * ROWS : c * ROWS + 16, :] = top
        lines[c * ROWS + 16 : (c + 1) * ROWS, :] = bottom
    blocks = [lines[pl.ds(br, 64, stride=4), :] for br in range(4)]
    blocked = jnp.concatenate(blocks, axis=1)
    number = b_col[:, :64]
    number = (number & 7) * 8 + (number >> 3)
    hot = (iota((SLOTS, 64), 1) == number).astype(F32).astype(BF16)
    high, low = split2(blocked)
    picked = jnp.dot(hot, high, preferred_element_type=F32) + jnp.dot(hot, low, preferred_element_type=F32)
    product = weights[...].astype(F32) * picked
    total = product[:, :CB]
    for br in range(1, 4):
        total = total + product[:, br * CB : (br + 1) * CB]
    proj[...] = jnp.broadcast_to(jnp.sum(total, axis=1, keepdims=True), (SLOTS, CB))


def slots_kernel(start, gram, q_row, q_col, proj, out, own):
    padded = jnp.concatenate([start[...], jnp.zeros((3 * CB - NAMES, CB), F32)], axis=0)
    row = jnp.transpose(padded)[0:1, :]
    own[...] = row[:, SLOTS:]
    start_row = row[:, :SLOTS]
    terms = gram[...] * start_row
    over = jnp.sum(terms[:, :CB] + terms[:, CB:], axis=1, keepdims=True)
    place = q_col[...]
    lane = iota((SLOTS, CB), 1)
    target = ((place >> 4) & 3) * 32 + (place & 15)
    sent = jnp.where(lane == target, proj[...], 0.0) + jnp.where(lane == target + 16, over, 0.0)
    row_hot = (iota((CB, SLOTS), 0) == (q_row[0:1, :] >> 6)).astype(F32).astype(BF16)
    parts = split3(sent)
    dense = jnp.dot(row_hot, parts[0], preferred_element_type=F32)
    dense = dense + jnp.dot(row_hot, parts[1], preferred_element_type=F32)
    dense = dense + jnp.dot(row_hot, parts[2], preferred_element_type=F32)
    for j in range(DEPTHS):
        out[j] = dense[j * 8 : (j + 1) * 8]


def fold_kernel(parts, out):
    total = parts[0]
    for j in range(1, DEPTHS):
        total = total + parts[j]
    for m in range(4):
        moved = pltpu.roll(total, (CB - 32 * m) % CB, 1) if m else total
        for r in range(8):
            out[4 * r + m] = moved[r : r + 1]


def final_kernel(parts, own, out):
    total = parts[0]
    for j in range(1, TILES):
        total = total + parts[j]
    over = pltpu.roll(total, CB - 16, 1)
    initial = own[...]
    real = iota((1, CB), 1) < 16
    bottom = jnp.where(real, over + 100.0 * initial, 1.0)
    out[...] = jnp.where(real, initial * total, 0.0) / bottom


def swap(pieces, axis):
    return lax.all_to_all(pieces, axis, 0, 0)


def body(
    volume,
    measured,
    point_spread,
    entry_block,
    entry_neuron,
    footprints,
    seed_plane,
    seed_row,
    seed_col,
    owner_slot,
):
    d = lax.axis_index("depth")
    t = lax.axis_index("tile")
    where = jnp.stack([d, t, (d * TILES + t) * 16]).astype(I32)
    table = owner_slot.reshape(64, CB)
    [windows] = call(window_kernel, [((DEPTHS, ROWS, CB), F32)], 2)(volume, point_spread)
    parts = swap(windows, "depth").reshape(DEPTHS * ROWS, CB)
    message = ((HALO * ROW + 2 * HALO, CB), BF16)
    own, sensor, down, up = call(
        arrange_kernel,
        [((ROWS * ROW, CB), F32), ((ROWS, CB), F32), message, message],
        3,
        scalars=(0,),
        scratch=[pltpu.VMEM((ROWS, COLS + 2 * CB), F32)],
    )(where, parts, measured)
    left = lax.ppermute(down, "tile", [(i, i + 1) for i in range(TILES - 1)])
    right = lax.ppermute(up, "tile", [(i + 1, i) for i in range(TILES - 1)])
    ahead, behind, scale = call(
        tables_kernel, [((256, DEEP), BF16), ((256, DEEP), BF16), ((ROW, CB), F32)], 1
    )(parts)
    weights = footprints[0].reshape(SLOTS, 512)
    column = ((SLOTS, CB), I32)
    names = ((NAMES, CB), I32)
    square = ((64, CB), I32)
    gram, q_row, q_col, b_col, a_row, a_lane, rank, code, first, most = call(
        prepare_kernel,
        [
            ((SLOTS, SLOTS), F32),
            ((8, SLOTS), I32),
            column,
            column,
            names,
            names,
            square,
            square,
            ((8, CB), I32),
            ((8, CB), I32),
        ],
        8,
        scalars=(0,),
    )(
        where,
        entry_block,
        entry_neuron,
        weights,
        table,
        seed_plane.reshape(64, CB),
        seed_row.reshape(64, CB),
        seed_col.reshape(64, CB),
    )
    sent, flat = call(
        iterate_kernel,
        [((DEPTHS, 24, CB), F32), ((256, CB), F32)],
        8,
        scratch=[
            pltpu.VMEM((96 * ROW, CB), F32),
            pltpu.VMEM((96 * ROW, CB), BF16),
            pltpu.VMEM((64 * ROW, CB), F32),
            pltpu.VMEM((64 * ROW, CB), BF16),
            pltpu.VMEM((96, CB), F32),
            pltpu.VMEM((256, CB), F32),
            pltpu.VMEM((80, CB), F32),
            pltpu.VMEM((4 * DEEP, CB), BF16),
        ],
    )(own, left, right, sensor, ahead, behind, scale, first)
    parts = swap(sent, "depth")

    def share(values, at):
        [values] = call(gather_kernel(at), [((TILES, 1, CAP), F32)], 1)(values)
        return swap(values, "tile")

    def look(turn, values, known):
        return call(look_kernel, [((NAMES, CB), F32)], 5, scalars=(0,))(
            turn, values, a_row, a_lane, known
        )[0]

    def another(step, known):
        turn = jnp.reshape(step, (1,))
        [values] = call(more_kernel, [((DEPTHS, 8, CB), F32)], 4, scalars=(0,))(
            turn, rank, code, flat
        )
        return look(turn, share(swap(values, "depth"), 0), known)

    known = look(jnp.zeros((1,), I32), share(parts, 16), jnp.zeros((NAMES, CB), F32))
    known = lax.fori_loop(1, (most[0, 0] + CAP - 1) // CAP, another, known)
    estimate, proj = call(
        home_kernel,
        [((ROWS, COLS), F32), ((SLOTS, CB), F32)],
        3,
        scratch=[pltpu.VMEM((NCB * ROWS, CB), F32)],
    )(parts, weights, b_col)
    sent, own = call(slots_kernel, [((DEPTHS, 8, CB), F32), ((1, CB), F32)], 5)(
        known, gram, q_row, q_col, proj
    )
    [sent] = call(fold_kernel, [((TILES, 1, CB), F32)], 1)(swap(sent, "depth"))
    [demixed] = call(final_kernel, [((1, CB), F32)], 2)(swap(sent, "tile"), own)
    return estimate[None], demixed[0, :16]


def solution(mesh):
    in_specs = (
        P("depth", "tile", None),
        P("tile", None),
        P("depth", None, None),
        P("tile", "depth"),
        P("tile", "depth"),
        P("tile", "depth", None, None),
        P(),
        P(),
        P(),
        P(),
    )
    out_specs = (P("depth", "tile", None), P(("depth", "tile")))
    return jax.shard_map(body, mesh=mesh, in_specs=in_specs, out_specs=out_specs, check_vma=False)
```

```python
import jax
import jax.numpy as jnp
from jax import lax
from jax.experimental import pallas as pl
from jax.experimental.pallas import tpu as pltpu
from jax.sharding import PartitionSpec as P

F32 = jnp.float32
BF16 = jnp.bfloat16
I32 = jnp.int32
KS = 13
RADIUS = 6
ROWS = 32
COLS = 1024
CB = 128
NCB = COLS // CB
DEPTHS = 16
TILES = 32
SLOTS = 256
NEURONS = 8192
HALO = 24
WIN = 64
LIVE = WIN + 2 * HALO
ROW = DEPTHS
BLOCK = 16
DEEP = 32 * ROW
CAP = 384
LANES = CAP // CB
NAMES = SLOTS + 16
VMEM = pl.BlockSpec(memory_space=pltpu.VMEM)
SMEM = pl.BlockSpec(memory_space=pltpu.SMEM)


def call(kernel, outs, n_in, scalars=(), scratch=(), mib=24):
    return pl.pallas_call(
        kernel,
        out_shape=[jax.ShapeDtypeStruct(s, t) for s, t in outs],
        in_specs=[SMEM if i in scalars else VMEM for i in range(n_in)],
        out_specs=[VMEM] * len(outs),
        scratch_shapes=list(scratch),
        compiler_params=pltpu.CompilerParams(vmem_limit_bytes=mib * 2**20),
    )


def iota(shape, dim):
    return lax.broadcasted_iota(I32, shape, dim)


def split2(x):
    high = x.astype(BF16)
    return high, (x - high.astype(F32)).astype(BF16)


def split3(x):
    high = x.astype(BF16)
    rest = x - high.astype(F32)
    mid = rest.astype(BF16)
    return high, mid, (rest - mid.astype(F32)).astype(BF16)


def column_of(row):
    n = row.shape[1]
    return jnp.transpose(jnp.broadcast_to(row, (CB, n)))


def lane_sum(x):
    return jnp.sum(x, axis=1, keepdims=True)


def prepare_kernel(
    where, block, neuron, weights, owner, s_plane, s_row, s_col,
    gram, q_row, q_col, b_col, a_row, a_lane, rank, code, first, most,
):
    foot = weights[...]
    product = lax.dot_general(foot, foot, (((1,), (1,)), ((), ())), preferred_element_type=F32)
    blocks = column_of(block[...].astype(F32))
    same = jnp.concatenate([blocks, blocks], axis=1) == block[...].astype(F32)
    gram[...] = jnp.where(same, product, 0.0)
    b_col[...] = blocks.astype(I32)
    table = owner[...]
    number = iota((64, CB), 0) * CB + iota((64, CB), 1)
    own = jnp.zeros((16, CB), F32)
    for i in range(16):
        hit = jnp.sum(jnp.where(table == where[2] + i, number.astype(F32), 0.0), axis=0, keepdims=True)
        own = jnp.where(iota((16, CB), 0) == i, lane_sum(hit), own)
    names = jnp.concatenate([column_of(neuron[...].astype(F32)), own], axis=0).astype(I32)
    row, col = s_row[...], s_col[...]
    tile, window = row >> 5, col >> 6
    tables = [tile, table >> 7, table & 127]
    tables = jnp.concatenate([x.astype(F32) for x in tables], axis=1).astype(BF16)
    hot = (iota((NAMES, 64), 1) == (names[:, :64] >> 7)).astype(F32).astype(BF16)
    found = jnp.dot(hot, tables, preferred_element_type=F32)
    lane_hot = iota((NAMES, CB), 1) == (names & 127)
    picked = [lane_sum(jnp.where(lane_hot, found[:, i * CB : (i + 1) * CB], 0.0)) for i in range(3)]
    n_tile = picked[0].astype(I32)
    place = jnp.broadcast_to(picked[1] * 128.0 + picked[2], (NAMES, CB))[:SLOTS]
    place = jnp.where(names[:SLOTS] >= 0, place, -1.0)
    q_col[...] = place.astype(I32)
    q_row[...] = jnp.transpose(place)[0:8, :].astype(I32)
    both = jnp.zeros((TILES, 1), F32)
    for r in range(0, 64, 8):
        tiles = jnp.zeros((TILES, CB), F32)
        for i in range(r, r + 8):
            tiles = tiles + (iota((TILES, CB), 0) == tile[i : i + 1, :]).astype(F32)
        both = both + lane_sum(tiles)
    top = jnp.max(both, axis=0, keepdims=True)
    most[...] = jnp.broadcast_to(top, (8, CB)).astype(I32)
    wide = jnp.concatenate([both, jnp.zeros((CB - TILES, 1), F32)], axis=0)
    held = jnp.transpose(jnp.broadcast_to(wide, (CB, CB)))[0:1, :]
    earlier = lane_sum(jnp.where(iota((NAMES, CB), 1) < n_tile, held, 0.0))
    keys = tile * NEURONS + number
    high = jnp.broadcast_to(n_tile * NEURONS, (NAMES, CB)) + names
    count = jnp.zeros((NAMES, CB), F32)
    for r in range(64):
        count = count + jnp.where(keys[r : r + 1, :] < high, 1.0, 0.0)
    position = jnp.broadcast_to(lane_sum(count) - earlier, (NAMES, CB)).astype(I32)
    turn = jnp.zeros((NAMES, CB), I32)
    for i in range(1, (NEURONS + CAP - 1) // CAP):
        turn = turn + (position >= i * CAP).astype(I32)
    a_row[...] = jnp.where(names >= 0, turn * TILES + n_tile, -1)
    a_lane[...] = position - turn * CAP
    local = tile == where[1]
    mask = local.astype(F32)
    before = (iota((CB, CB), 0) < iota((CB, CB), 1)).astype(F32).astype(BF16)
    inside = jnp.dot(mask.astype(BF16), before, preferred_element_type=F32)
    rows = jnp.broadcast_to(lane_sum(mask), (64, CB)).astype(BF16)
    above = (iota((64, 64), 1) < iota((64, 64), 0)).astype(F32).astype(BF16)
    inside = inside + jnp.dot(above, rows, preferred_element_type=F32)
    order = jnp.where(local & (window == where[0]), inside, -1.0).astype(I32)
    spot = ((row >> 4) & 1) * WIN + (col & (WIN - 1))
    coded = ((row & 15) * ROW + s_plane[...]) * CB + spot
    rank[...] = order
    code[...] = coded
    first[...] = listed(order, coded, 0)


def listed(order, coded, start):
    place = order - start
    place = jnp.where(place < CAP, place, -1)
    total = jnp.zeros((32, CB), F32)
    for r in range(0, 64, 8):
        lines = [place[i : i + 1, :] for i in range(r, r + 8)]
        codes = [coded[i : i + 1, :] for i in range(r, r + 8)]
        left = []
        for at, code in zip(lines, codes):
            here = iota((8, CB), 0) == (at >> 7)
            left.append(
                jnp.concatenate(
                    [
                        jnp.where(here, (code >> 7).astype(F32), 0.0),
                        jnp.where(here, (code & 127).astype(F32), 0.0),
                        jnp.where(here, 1.0, 0.0),
                        jnp.zeros((8, CB), F32),
                    ],
                    axis=0,
                )
            )
        left = jnp.concatenate(left, axis=1).astype(BF16)
        right = [(iota((CB, CB), 0) == jnp.where(at >= 0, at & 127, -1)).astype(F32) for at in lines]
        right = jnp.concatenate(right, axis=1).astype(BF16)
        total = total + lax.dot_general(
            left, right, (((1,), (1,)), ((), ())), preferred_element_type=F32
        )
    value = total[0:8] * 128.0 + total[8:16]
    return jnp.where(total[16:24] > 0.0, value, -1.0).astype(I32)


def seed_values(codes, flat):
    parts = split3(flat)
    result = []
    for i in range(LANES):
        index = column_of(codes[i : i + 1, :].astype(F32)).astype(I32)
        key = jnp.concatenate([index, index], axis=1) >> 7
        hot = (iota((CB, 256), 1) == key).astype(F32).astype(BF16)
        found = jnp.dot(hot, parts[0], preferred_element_type=F32)
        found = found + jnp.dot(hot, parts[1], preferred_element_type=F32)
        found = found + jnp.dot(hot, parts[2], preferred_element_type=F32)
        picked = jnp.where(iota((CB, CB), 1) == (index & (CB - 1)), found, 0.0)
        result.append(jnp.sum(jnp.transpose(picked), axis=0, keepdims=True))
    result.append(jnp.zeros((8 - LANES, CB), F32))
    return jnp.concatenate(result, axis=0)


def window_kernel(volume, spread, windows):
    lane = iota((ROWS, CB), 1)
    taps = jnp.concatenate([spread[0].astype(F32), jnp.zeros((KS, CB - KS), F32)], axis=1)
    taps = jnp.concatenate([pltpu.roll(taps, LIVE, 1), jnp.zeros((ROWS - KS, CB), F32)], axis=0)
    zeros = jnp.zeros((ROWS, CB), F32)
    padded = jnp.concatenate([zeros, volume[0], zeros], axis=1)
    for j in range(DEPTHS):
        start = CB - HALO + WIN * j
        low = start // CB * CB
        moved = pltpu.roll(padded[:, low : low + 2 * CB], 2 * CB - start % CB, 1)[:, :CB]
        windows[j] = jnp.where(lane < LIVE, moved, taps)


def arrange_kernel(where, parts, measured, own, sensor, down, up, wide):
    lane = iota((ROW, CB), 1)
    for r in range(ROWS):
        line = jnp.where(lane < LIVE, parts[pl.ds(r, ROW, stride=ROWS), :], 0.0)
        own[r * ROW : (r + 1) * ROW, :] = line
        if r < HALO:
            up[r * ROW : (r + 1) * ROW, :] = line.astype(BF16)
        if r >= ROWS - HALO:
            at = (r - ROWS + HALO) * ROW
            down[at : at + ROW, :] = line.astype(BF16)
    zeros = jnp.zeros((ROWS, CB), F32)
    wide[:, :CB] = zeros
    wide[:, CB : CB + COLS] = measured[...]
    wide[:, CB + COLS :] = zeros
    start = CB - HALO + WIN * where[0]
    low = pl.multiple_of((start >> 7) * CB, CB)
    moved = pltpu.roll(wide[:, pl.ds(low, 2 * CB)], 2 * CB - (start & (CB - 1)), 1)[:, :CB]
    view = jnp.where(iota((ROWS, CB), 1) < LIVE, moved, 0.0)
    sensor[...] = view
    for out, part in ((up, view[:HALO]), (down, view[ROWS - HALO :])):
        high = part.astype(BF16).astype(F32)
        out[HALO * ROW :, :] = jnp.concatenate([high, part - high], axis=0).astype(BF16)


def tables_kernel(parts, ahead, behind, scale):
    taps = jnp.concatenate([parts[pl.ds(a, ROW, stride=ROWS), :] for a in range(16)], axis=0)
    taps = jnp.where(iota((256, CB), 1) >= LIVE, taps, 0.0)
    first = jnp.transpose(taps)[LIVE:, :]
    first = jnp.concatenate([first, jnp.zeros((16, 256), F32)], axis=1)
    for i in range(BLOCK):
        moved = pltpu.roll(first, i * ROW, 1) if i else first
        ahead[i * 16 : (i + 1) * 16, :] = moved.astype(BF16)
    lane = iota((CB, DEEP), 1)
    hot = (iota((CB, DEEP), 0) == LIVE + KS - 1 - (lane >> 5)).astype(F32).astype(BF16)
    spread = jnp.dot(taps.astype(BF16), hot, preferred_element_type=F32)
    inside = iota((ROW, DEEP), 1)
    within = jnp.where(inside < KS * 32, inside & 31, 32)
    second = jnp.zeros((ROW, DEEP), F32)
    for a in range(KS):
        second = jnp.where(within == KS - 1 - a, spread[a * ROW : (a + 1) * ROW], second)
    for i in range(BLOCK):
        moved = pltpu.roll(second, i, 1) if i else second
        behind[i * ROW : (i + 1) * ROW, :] = moved.astype(BF16)
    total = taps[:ROW]
    for a in range(1, KS):
        total = total + taps[a * ROW : (a + 1) * ROW]
    norm = jnp.sum(total, axis=1, keepdims=True)
    scale[...] = jnp.broadcast_to(1.0 / norm, (ROW, CB))


def lane_shift(x, b):
    shift = (RADIUS - b) % CB
    return pltpu.roll(x, shift, 1) if shift else x


def iterate_kernel(
    own, left, right, sensor, ahead, behind, scale, codes,
    sent, flat, exact, rounded, first, second, light, sums, ratio, stack,
):
    rows = (HALO * ROW, (HALO + ROWS) * ROW, (2 * HALO + ROWS) * ROW)
    exact[: rows[0], :] = left[: rows[0]].astype(F32)
    exact[rows[0] : rows[1], :] = own[...]
    exact[rows[1] : rows[2], :] = right[: rows[0]].astype(F32)
    exact[rows[2] :, :] = jnp.zeros((16 * ROW, CB), F32)
    rounded[...] = exact[...].astype(BF16)
    before, after = left[rows[0] :].astype(F32), right[rows[0] :].astype(F32)
    light[:HALO, :] = before[:HALO] + before[HALO:]
    light[HALO : HALO + ROWS, :] = sensor[...]
    light[HALO + ROWS : 2 * HALO + ROWS, :] = after[:HALO] + after[HALO:]
    light[2 * HALO + ROWS :, :] = jnp.zeros((16, CB), F32)
    for m in range(2):
        stack[m * DEEP + KS * 32 : (m + 1) * DEEP, :] = jnp.zeros((DEEP - KS * 32, 2 * CB), BF16)
    tall = jnp.concatenate([scale[...]] * BLOCK, axis=0)

    def divide(source, blocks, offset, valid):
        for m in range(0, blocks, 2):
            pair = range(m, min(m + 2, blocks))
            right = jnp.concatenate([source[i * 256 : i * 256 + DEEP, :] for i in pair], axis=1)
            value = jnp.dot(ahead[...], right, preferred_element_type=F32)
            for i in pair:
                at = (i - m) * CB
                sums[i - m] = value[:, at : at + CB]
            for i in pair:
                total = lane_shift(sums[i - m, pl.ds(0, BLOCK, stride=16), :], 0)
                for b in range(1, KS):
                    total = total + lane_shift(sums[i - m, pl.ds(b, BLOCK, stride=16), :], b)
                seen = light[i * BLOCK + offset : (i + 1) * BLOCK + offset, :]
                inside = (iota((BLOCK, CB), 0) < valid - i * BLOCK) & (seen != 0.0) & (total != 0.0)
                ratio[i * BLOCK : (i + 1) * BLOCK, :] = jnp.where(
                    inside, seen / jnp.where(inside, total, 1.0), 0.0
                )

    def spread_back(blocks):
        height = 16 * blocks + 16
        for b in range(KS):
            moved = lane_shift(ratio[:height, :], b).astype(BF16)
            for m in range(blocks):
                at = (m // 2) * DEEP + b * 32
                stack[at : at + 32, (m % 2) * CB : (m % 2 + 1) * CB] = moved[m * 16 : m * 16 + 32]

    def back(m):
        value = jnp.dot(behind[...], stack[m * DEEP : (m + 1) * DEEP, :], preferred_element_type=F32)
        return value[:, :CB] * tall, value[:, CB:] * tall

    divide(rounded, 5, 6, 68)
    spread_back(4)
    factors = back(0) + back(1)
    for m in range(4):
        value = exact[(m * 16 + 12) * ROW : (m * 16 + 28) * ROW, :] * factors[m]
        first[m * 256 : (m + 1) * 256, :] = value
        second[m * 256 : (m + 1) * 256, :] = value.astype(BF16)
    divide(second, 3, 18, 44)
    spread_back(2)
    factors = back(0)
    done = [first[(m * 16 + 12) * ROW : (m * 16 + 28) * ROW, :] * factors[m] for m in range(2)]
    lane = iota((256, CB), 1)
    packed = jnp.where(lane < WIN, pltpu.roll(done[0], CB - HALO, 1), pltpu.roll(done[1], WIN - HALO, 1))
    flat[...] = packed
    values = seed_values(codes[...], packed)
    for p in range(DEPTHS):
        sent[p, 0:16, :] = flat[pl.ds(p, 16, stride=ROW), :]
        sent[p, 16:24, :] = values


def more_kernel(turn, rank, code, flat, sent):
    codes = listed(rank[...], code[...], turn[0] * CAP)
    values = seed_values(codes, flat[...])
    for p in range(DEPTHS):
        sent[p] = values


def gather_kernel(at):
    def kernel(parts, out):
        total = parts[0, at : at + 8, :]
        for j in range(1, DEPTHS):
            total = total + parts[j, at : at + 8, :]
        line = jnp.concatenate([total[i : i + 1, :] for i in range(LANES)], axis=1)
        for j in range(TILES):
            out[j] = line

    return kernel


def looked(turn, parts, a_row, a_lane):
    table = jnp.concatenate([parts[t] for t in range(TILES)], axis=0)
    row = a_row[...] - turn * TILES
    hot = (iota((NAMES, TILES), 1) == row[:, :TILES]).astype(F32).astype(BF16)
    parts = split3(table)
    found = jnp.dot(hot, parts[0], preferred_element_type=F32)
    found = found + jnp.dot(hot, parts[1], preferred_element_type=F32)
    found = found + jnp.dot(hot, parts[2], preferred_element_type=F32)
    total = jnp.zeros((NAMES, CB), F32)
    for i in range(LANES):
        here = iota((NAMES, CB), 1) + i * CB == a_lane[...]
        total = total + jnp.where(here, found[:, i * CB : (i + 1) * CB], 0.0)
    return jnp.broadcast_to(lane_sum(total), (NAMES, CB))


def look_kernel(turn, parts, a_row, a_lane, known, out):
    out[...] = known[...] + looked(turn[0], parts, a_row, a_lane)


def home_kernel(parts, weights, b_col, estimate, proj, lines):
    lane = iota((16, CB), 1)
    for c in range(NCB):
        a, b = parts[2 * c, :16, :], parts[2 * c + 1, :16, :]
        top = jnp.where(lane < WIN, a, pltpu.roll(b, WIN, 1))
        bottom = jnp.where(lane < WIN, pltpu.roll(a, WIN, 1), b)
        estimate[:16, c * CB : (c + 1) * CB] = top
        estimate[16:, c * CB : (c + 1) * CB] = bottom
        lines[c * ROWS : c * ROWS + 16, :] = top
        lines[c * ROWS + 16 : (c + 1) * ROWS, :] = bottom
    blocks = [lines[pl.ds(br, 64, stride=4), :] for br in range(4)]
    blocked = jnp.concatenate(blocks, axis=1)
    number = b_col[:, :64]
    number = (number & 7) * 8 + (number >> 3)
    hot = (iota((SLOTS, 64), 1) == number).astype(F32).astype(BF16)
    high, low = split2(blocked)
    picked = jnp.dot(hot, high, preferred_element_type=F32) + jnp.dot(hot, low, preferred_element_type=F32)
    product = weights[...].astype(F32) * picked
    total = product[:, :CB]
    for br in range(1, 4):
        total = total + product[:, br * CB : (br + 1) * CB]
    proj[...] = jnp.broadcast_to(jnp.sum(total, axis=1, keepdims=True), (SLOTS, CB))


def slots_kernel(parts, a_row, a_lane, known, gram, q_row, q_col, proj, out, own):
    start = known[...] + looked(0, parts, a_row, a_lane)
    padded = jnp.concatenate([start, jnp.zeros((3 * CB - NAMES, CB), F32)], axis=0)
    row = jnp.transpose(padded)[0:1, :]
    own[...] = row[:, SLOTS:]
    start_row = row[:, :SLOTS]
    terms = gram[...] * start_row
    over = jnp.sum(terms[:, :CB] + terms[:, CB:], axis=1, keepdims=True)
    place = q_col[...]
    lane = iota((SLOTS, CB), 1)
    target = ((place >> 4) & 3) * 32 + (place & 15)
    sent = jnp.where(lane == target, proj[...], 0.0) + jnp.where(lane == target + 16, over, 0.0)
    row_hot = (iota((CB, SLOTS), 0) == (q_row[0:1, :] >> 6)).astype(F32).astype(BF16)
    parts = split3(sent)
    dense = jnp.dot(row_hot, parts[0], preferred_element_type=F32)
    dense = dense + jnp.dot(row_hot, parts[1], preferred_element_type=F32)
    dense = dense + jnp.dot(row_hot, parts[2], preferred_element_type=F32)
    for j in range(DEPTHS):
        out[j] = dense[j * 8 : (j + 1) * 8]


def fold_kernel(parts, out):
    total = parts[0]
    for j in range(1, DEPTHS):
        total = total + parts[j]
    for m in range(4):
        moved = pltpu.roll(total, (CB - 32 * m) % CB, 1) if m else total
        for r in range(8):
            out[4 * r + m] = moved[r : r + 1]


def final_kernel(parts, own, out):
    total = parts[0]
    for j in range(1, TILES):
        total = total + parts[j]
    over = pltpu.roll(total, CB - 16, 1)
    initial = own[...]
    real = iota((1, CB), 1) < 16
    bottom = jnp.where(real, over + 100.0 * initial, 1.0)
    out[...] = jnp.where(real, initial * total, 0.0) / bottom


def swap(pieces, axis):
    return lax.all_to_all(pieces, axis, 0, 0)


def body(
    volume,
    measured,
    point_spread,
    entry_block,
    entry_neuron,
    footprints,
    seed_plane,
    seed_row,
    seed_col,
    owner_slot,
):
    d = lax.axis_index("depth")
    t = lax.axis_index("tile")
    where = jnp.stack([d, t, (d * TILES + t) * 16]).astype(I32)
    [windows] = call(window_kernel, [((DEPTHS, ROWS, CB), F32)], 2)(volume, point_spread)
    windows, where = lax.optimization_barrier((windows, where))
    tied = (swap(windows, "depth"), where, measured, entry_block, entry_neuron, footprints, owner_slot)
    tied = lax.optimization_barrier(tied + (seed_plane, seed_row, seed_col))
    parts, where, measured, entry_block, entry_neuron, footprints, owner_slot = tied[:7]
    seed_plane, seed_row, seed_col = tied[7:]
    parts = parts.reshape(DEPTHS * ROWS, CB)
    table = owner_slot.reshape(64, CB)
    message = ((HALO * ROW + 2 * HALO, CB), BF16)
    own, sensor, down, up = call(
        arrange_kernel,
        [((ROWS * ROW, CB), F32), ((ROWS, CB), F32), message, message],
        3,
        scalars=(0,),
        scratch=[pltpu.VMEM((ROWS, COLS + 2 * CB), F32)],
    )(where, parts, measured)
    left = lax.ppermute(down, "tile", [(i, i + 1) for i in range(TILES - 1)])
    right = lax.ppermute(up, "tile", [(i + 1, i) for i in range(TILES - 1)])
    ahead, behind, scale = call(
        tables_kernel, [((256, DEEP), BF16), ((256, DEEP), BF16), ((ROW, CB), F32)], 1
    )(parts)
    weights = footprints[0].reshape(SLOTS, 512)
    column = ((SLOTS, CB), I32)
    names = ((NAMES, CB), I32)
    square = ((64, CB), I32)
    gram, q_row, q_col, b_col, a_row, a_lane, rank, code, first, most = call(
        prepare_kernel,
        [
            ((SLOTS, SLOTS), F32),
            ((8, SLOTS), I32),
            column,
            column,
            names,
            names,
            square,
            square,
            ((8, CB), I32),
            ((8, CB), I32),
        ],
        8,
        scalars=(0,),
    )(
        where,
        entry_block,
        entry_neuron,
        weights,
        table,
        seed_plane.reshape(64, CB),
        seed_row.reshape(64, CB),
        seed_col.reshape(64, CB),
    )
    sent, flat = call(
        iterate_kernel,
        [((DEPTHS, 24, CB), F32), ((256, CB), F32)],
        8,
        scratch=[
            pltpu.VMEM((96 * ROW, CB), F32),
            pltpu.VMEM((96 * ROW, CB), BF16),
            pltpu.VMEM((64 * ROW, CB), F32),
            pltpu.VMEM((64 * ROW, CB), BF16),
            pltpu.VMEM((96, CB), F32),
            pltpu.VMEM((2, 256, CB), F32),
            pltpu.VMEM((80, CB), F32),
            pltpu.VMEM((2 * DEEP, 2 * CB), BF16),
        ],
    )(own, left, right, sensor, ahead, behind, scale, first)
    parts, most = lax.optimization_barrier((swap(sent, "depth"), most))

    def share(values, at):
        [values] = call(gather_kernel(at), [((TILES, 1, CAP), F32)], 1)(values)
        return swap(values, "tile")

    def look(turn, values, known):
        return call(look_kernel, [((NAMES, CB), F32)], 5, scalars=(0,))(
            turn, values, a_row, a_lane, known
        )[0]

    def another(step, known):
        turn = jnp.reshape(step, (1,))
        [values] = call(more_kernel, [((DEPTHS, 8, CB), F32)], 4, scalars=(0,))(
            turn, rank, code, flat
        )
        return look(turn, share(swap(values, "depth"), 0), known)

    rounds = (most[0, 0] + CAP - 1) // CAP
    shared, none = lax.optimization_barrier((share(parts, 16), jnp.zeros((NAMES, CB), F32)))
    known = lax.fori_loop(1, rounds, another, none)
    estimate, proj = call(
        home_kernel,
        [((ROWS, COLS), F32), ((SLOTS, CB), F32)],
        3,
        scratch=[pltpu.VMEM((NCB * ROWS, CB), F32)],
    )(parts, weights, b_col)
    sent, own = call(slots_kernel, [((DEPTHS, 8, CB), F32), ((1, CB), F32)], 8)(
        shared, a_row, a_lane, known, gram, q_row, q_col, proj
    )
    [sent] = call(fold_kernel, [((TILES, 1, CB), F32)], 1)(swap(sent, "depth"))
    [demixed] = call(final_kernel, [((1, CB), F32)], 2)(swap(sent, "tile"), own)
    return estimate[None], demixed[0, :16]


def solution(mesh):
    in_specs = (
        P("depth", "tile", None),
        P("tile", None),
        P("depth", None, None),
        P("tile", "depth"),
        P("tile", "depth"),
        P("tile", "depth", None, None),
        P(),
        P(),
        P(),
        P(),
    )
    out_specs = (P("depth", "tile", None), P(("depth", "tile")))
    return jax.shard_map(body, mesh=mesh, in_specs=in_specs, out_specs=out_specs, check_vma=False)
```

```python
import jax
import jax.numpy as jnp
from jax import lax
from jax.experimental import pallas as pl
from jax.experimental.pallas import tpu as pltpu
from jax.sharding import PartitionSpec as P

F32 = jnp.float32
BF16 = jnp.bfloat16
I32 = jnp.int32
KS = 13
RADIUS = 6
ROWS = 32
COLS = 1024
CB = 128
NCB = COLS // CB
DEPTHS = 16
TILES = 32
SLOTS = 256
NEURONS = 8192
HALO = 24
WIN = 64
LIVE = WIN + 2 * HALO
ROW = DEPTHS
BLOCK = 16
DEEP = 32 * ROW
CAP = 384
LANES = CAP // CB
NEAR = 12
NAMES = SLOTS + 16
VMEM = pl.BlockSpec(memory_space=pltpu.VMEM)
SMEM = pl.BlockSpec(memory_space=pltpu.SMEM)


def call(kernel, outs, n_in, scalars=(), scratch=(), mib=24):
    return pl.pallas_call(
        kernel,
        out_shape=[jax.ShapeDtypeStruct(s, t) for s, t in outs],
        in_specs=[SMEM if i in scalars else VMEM for i in range(n_in)],
        out_specs=[VMEM] * len(outs),
        scratch_shapes=list(scratch),
        compiler_params=pltpu.CompilerParams(vmem_limit_bytes=mib * 2**20),
    )


def iota(shape, dim):
    return lax.broadcasted_iota(I32, shape, dim)


def split2(x):
    high = x.astype(BF16)
    return high, (x - high.astype(F32)).astype(BF16)


def split3(x):
    high = x.astype(BF16)
    rest = x - high.astype(F32)
    mid = rest.astype(BF16)
    return high, mid, (rest - mid.astype(F32)).astype(BF16)


def column_of(row):
    n = row.shape[1]
    return jnp.transpose(jnp.broadcast_to(row, (CB, n)))


def lane_sum(x):
    return jnp.sum(x, axis=1, keepdims=True)


def prepare_kernel(
    where, block, neuron, weights, owner, s_plane, s_row, s_col,
    gram, q_row, q_col, b_col, a_row, a_lane, rank, code, first, most,
):
    foot = weights[...]
    product = lax.dot_general(foot, foot, (((1,), (1,)), ((), ())), preferred_element_type=F32)
    blocks = column_of(block[...].astype(F32))
    same = jnp.concatenate([blocks, blocks], axis=1) == block[...].astype(F32)
    gram[...] = jnp.where(same, product, 0.0)
    b_col[...] = blocks.astype(I32)
    table = owner[...]
    number = iota((64, CB), 0) * CB + iota((64, CB), 1)
    own = jnp.zeros((16, CB), F32)
    for i in range(16):
        hit = jnp.sum(jnp.where(table == where[2] + i, number.astype(F32), 0.0), axis=0, keepdims=True)
        own = jnp.where(iota((16, CB), 0) == i, lane_sum(hit), own)
    names = jnp.concatenate([column_of(neuron[...].astype(F32)), own], axis=0).astype(I32)
    row, col = s_row[...], s_col[...]
    tile, window = row >> 5, col >> 6
    tables = [tile, table >> 7, table & 127]
    tables = jnp.concatenate([x.astype(F32) for x in tables], axis=1).astype(BF16)
    hot = (iota((NAMES, 64), 1) == (names[:, :64] >> 7)).astype(F32).astype(BF16)
    found = jnp.dot(hot, tables, preferred_element_type=F32)
    lane_hot = iota((NAMES, CB), 1) == (names & 127)
    picked = [lane_sum(jnp.where(lane_hot, found[:, i * CB : (i + 1) * CB], 0.0)) for i in range(3)]
    n_tile = picked[0].astype(I32)
    place = jnp.broadcast_to(picked[1] * 128.0 + picked[2], (NAMES, CB))[:SLOTS]
    place = jnp.where(names[:SLOTS] >= 0, place, -1.0)
    q_col[...] = place.astype(I32)
    q_row[...] = jnp.transpose(place)[0:8, :].astype(I32)
    both = jnp.zeros((TILES, 1), F32)
    for r in range(0, 64, 8):
        tiles = jnp.zeros((TILES, CB), F32)
        for i in range(r, r + 8):
            tiles = tiles + (iota((TILES, CB), 0) == tile[i : i + 1, :]).astype(F32)
        both = both + lane_sum(tiles)
    top = jnp.max(both, axis=0, keepdims=True)
    most[...] = jnp.broadcast_to(top, (8, CB)).astype(I32)
    wide = jnp.concatenate([both, jnp.zeros((CB - TILES, 1), F32)], axis=0)
    held = jnp.transpose(jnp.broadcast_to(wide, (CB, CB)))[0:1, :]
    earlier = lane_sum(jnp.where(iota((NAMES, CB), 1) < n_tile, held, 0.0))
    keys = tile * NEURONS + number
    high = jnp.broadcast_to(n_tile * NEURONS, (NAMES, CB)) + names
    count = jnp.zeros((NAMES, CB), F32)
    for r in range(64):
        count = count + jnp.where(keys[r : r + 1, :] < high, 1.0, 0.0)
    position = jnp.broadcast_to(lane_sum(count) - earlier, (NAMES, CB)).astype(I32)
    turn = jnp.zeros((NAMES, CB), I32)
    for i in range(1, (NEURONS + CAP - 1) // CAP):
        turn = turn + (position >= i * CAP).astype(I32)
    a_row[...] = jnp.where(names >= 0, turn * TILES + n_tile, -1)
    a_lane[...] = position - turn * CAP
    local = tile == where[1]
    mask = local.astype(F32)
    before = (iota((CB, CB), 0) < iota((CB, CB), 1)).astype(F32).astype(BF16)
    inside = jnp.dot(mask.astype(BF16), before, preferred_element_type=F32)
    rows = jnp.broadcast_to(lane_sum(mask), (64, CB)).astype(BF16)
    above = (iota((64, 64), 1) < iota((64, 64), 0)).astype(F32).astype(BF16)
    inside = inside + jnp.dot(above, rows, preferred_element_type=F32)
    order = jnp.where(local & (window == where[0]), inside, -1.0).astype(I32)
    spot = ((row >> 4) & 1) * WIN + (col & (WIN - 1))
    coded = ((row & 15) * ROW + s_plane[...]) * CB + spot
    rank[...] = order
    code[...] = coded
    first[...] = listed(order, coded, 0)


def listed(order, coded, start):
    place = order - start
    place = jnp.where(place < CAP, place, -1)
    total = jnp.zeros((32, CB), F32)
    for r in range(0, 64, 8):
        lines = [place[i : i + 1, :] for i in range(r, r + 8)]
        codes = [coded[i : i + 1, :] for i in range(r, r + 8)]
        left = []
        for at, code in zip(lines, codes):
            here = iota((8, CB), 0) == (at >> 7)
            left.append(
                jnp.concatenate(
                    [
                        jnp.where(here, (code >> 7).astype(F32), 0.0),
                        jnp.where(here, (code & 127).astype(F32), 0.0),
                        jnp.where(here, 1.0, 0.0),
                        jnp.zeros((8, CB), F32),
                    ],
                    axis=0,
                )
            )
        left = jnp.concatenate(left, axis=1).astype(BF16)
        right = [(iota((CB, CB), 0) == jnp.where(at >= 0, at & 127, -1)).astype(F32) for at in lines]
        right = jnp.concatenate(right, axis=1).astype(BF16)
        total = total + lax.dot_general(
            left, right, (((1,), (1,)), ((), ())), preferred_element_type=F32
        )
    value = total[0:8] * 128.0 + total[8:16]
    return jnp.where(total[16:24] > 0.0, value, -1.0).astype(I32)


def seed_values(codes, flat):
    parts = split3(flat)
    result = []
    for i in range(LANES):
        index = column_of(codes[i : i + 1, :].astype(F32)).astype(I32)
        key = jnp.concatenate([index, index], axis=1) >> 7
        hot = (iota((CB, 256), 1) == key).astype(F32).astype(BF16)
        found = jnp.dot(hot, parts[0], preferred_element_type=F32)
        found = found + jnp.dot(hot, parts[1], preferred_element_type=F32)
        found = found + jnp.dot(hot, parts[2], preferred_element_type=F32)
        picked = jnp.where(iota((CB, CB), 1) == (index & (CB - 1)), found, 0.0)
        result.append(jnp.sum(jnp.transpose(picked), axis=0, keepdims=True))
    result.append(jnp.zeros((8 - LANES, CB), F32))
    return jnp.concatenate(result, axis=0)


def window_kernel(volume, spread, windows):
    lane = iota((ROWS, CB), 1)
    taps = jnp.concatenate([spread[0].astype(F32), jnp.zeros((KS, CB - KS), F32)], axis=1)
    taps = jnp.concatenate([pltpu.roll(taps, LIVE, 1), jnp.zeros((ROWS - KS, CB), F32)], axis=0)
    zeros = jnp.zeros((ROWS, CB), F32)
    padded = jnp.concatenate([zeros, volume[0], zeros], axis=1)
    for j in range(DEPTHS):
        start = CB - HALO + WIN * j
        low = start // CB * CB
        moved = pltpu.roll(padded[:, low : low + 2 * CB], 2 * CB - start % CB, 1)[:, :CB]
        windows[j] = jnp.where(lane < LIVE, moved, taps)


def lane_shift(x, b):
    shift = (RADIUS - b) % CB
    return pltpu.roll(x, shift, 1) if shift else x


def forward(ahead, source, sums, blocks):
    result = []
    for m in range(0, blocks, 2):
        pair = range(m, min(m + 2, blocks))
        right = jnp.concatenate([source[i * 256 : i * 256 + DEEP, :] for i in pair], axis=1)
        value = jnp.dot(ahead[...], right, preferred_element_type=F32)
        for i in pair:
            at = (i - m) * CB
            sums[i - m] = value[:, at : at + CB]
        for i in pair:
            total = lane_shift(sums[i - m, pl.ds(0, BLOCK, stride=16), :], 0)
            for b in range(1, KS):
                total = total + lane_shift(sums[i - m, pl.ds(b, BLOCK, stride=16), :], b)
            result.append(total)
    return result


def open_kernel(
    where, parts, measured,
    own, sensor, down, up, ahead, behind, scale, image,
    wide, rounded, sums,
):
    lane = iota((ROW, CB), 1)
    rounded[: NEAR * ROW, :] = jnp.zeros((NEAR * ROW, CB), BF16)
    rounded[(NEAR + ROWS) * ROW :, :] = jnp.zeros(((NEAR + 8) * ROW, CB), BF16)
    for r in range(ROWS):
        line = jnp.where(lane < LIVE, parts[pl.ds(r, ROW, stride=ROWS), :], 0.0)
        own[r * ROW : (r + 1) * ROW, :] = line
        line = line.astype(BF16)
        rounded[(NEAR + r) * ROW : (NEAR + r + 1) * ROW, :] = line
        if r < NEAR:
            up[r * ROW : (r + 1) * ROW, :] = line
        if r >= ROWS - NEAR:
            at = (r - ROWS + NEAR) * ROW
            down[at : at + ROW, :] = line
    zeros = jnp.zeros((ROWS, CB), F32)
    wide[:, :CB] = zeros
    wide[:, CB : CB + COLS] = measured[...]
    wide[:, CB + COLS :] = zeros
    start = CB - HALO + WIN * where[0]
    low = pl.multiple_of((start >> 7) * CB, CB)
    moved = pltpu.roll(wide[:, pl.ds(low, 2 * CB)], 2 * CB - (start & (CB - 1)), 1)[:, :CB]
    view = jnp.where(iota((ROWS, CB), 1) < LIVE, moved, 0.0)
    sensor[...] = view
    taps = jnp.concatenate([parts[pl.ds(a, ROW, stride=ROWS), :] for a in range(16)], axis=0)
    taps = jnp.where(iota((256, CB), 1) >= LIVE, taps, 0.0)
    first = jnp.transpose(taps)[LIVE:, :]
    first = jnp.concatenate([first, jnp.zeros((16, 256), F32)], axis=1)
    for i in range(BLOCK):
        moved = pltpu.roll(first, i * ROW, 1) if i else first
        ahead[i * 16 : (i + 1) * 16, :] = moved.astype(BF16)
    lane = iota((CB, DEEP), 1)
    hot = (iota((CB, DEEP), 0) == LIVE + KS - 1 - (lane >> 5)).astype(F32).astype(BF16)
    spread = jnp.dot(taps.astype(BF16), hot, preferred_element_type=F32)
    inside = iota((ROW, DEEP), 1)
    within = jnp.where(inside < KS * 32, inside & 31, 32)
    second = jnp.zeros((ROW, DEEP), F32)
    for a in range(KS):
        second = jnp.where(within == KS - 1 - a, spread[a * ROW : (a + 1) * ROW], second)
    for i in range(BLOCK):
        moved = pltpu.roll(second, i, 1) if i else second
        behind[i * ROW : (i + 1) * ROW, :] = moved.astype(BF16)
    total = taps[:ROW]
    for a in range(1, KS):
        total = total + taps[a * ROW : (a + 1) * ROW]
    norm = jnp.sum(total, axis=1, keepdims=True)
    scale[...] = jnp.broadcast_to(1.0 / norm, (ROW, CB))
    image[...] = jnp.concatenate(forward(ahead, rounded, sums, 3), axis=0)
    for out, part, lines in (
        (up, view[:HALO], image[:HALO, :]),
        (down, view[ROWS - HALO :], image[20 : 20 + HALO, :]),
    ):
        rows = []
        for x in (part, lines):
            high = x.astype(BF16).astype(F32)
            rows += [high, x - high]
        out[NEAR * ROW :, :] = jnp.concatenate(rows, axis=0).astype(BF16)


def iterate_kernel(
    own, left, right, sensor, image, ahead, behind, scale, codes,
    sent, flat, exact, second, light, whole, sums, ratio, stack,
):
    near = NEAR * ROW
    exact[:near, :] = left[:near].astype(F32)
    exact[near : near + ROWS * ROW, :] = own[...]
    exact[near + ROWS * ROW : 2 * near + ROWS * ROW, :] = right[:near].astype(F32)
    exact[2 * near + ROWS * ROW :, :] = jnp.zeros((8 * ROW, CB), F32)
    before, after = left[near:].astype(F32), right[near:].astype(F32)
    light[:HALO, :] = before[:HALO] + before[HALO : 2 * HALO]
    light[HALO : HALO + ROWS, :] = sensor[...]
    light[HALO + ROWS : 2 * HALO + ROWS, :] = after[:HALO] + after[HALO : 2 * HALO]
    light[2 * HALO + ROWS :, :] = jnp.zeros((16, CB), F32)
    blank = jnp.zeros((20, CB), F32)
    total = jnp.concatenate([blank[:12], image[...], blank], axis=0)
    above = jnp.concatenate([before[2 * HALO : 3 * HALO] + before[3 * HALO :], jnp.zeros((56, CB), F32)], axis=0)
    below = after[2 * HALO : 3 * HALO] + after[3 * HALO :]
    below = jnp.concatenate([jnp.zeros((44, CB), F32), below, blank[:12]], axis=0)
    whole[...] = total + above + below
    for m in range(2):
        stack[m * DEEP + KS * 32 : (m + 1) * DEEP, :] = jnp.zeros((DEEP - KS * 32, 2 * CB), BF16)
    tall = jnp.concatenate([scale[...]] * BLOCK, axis=0)

    def divide(total, offset, valid):
        rows = total.shape[0]
        seen = light[offset : offset + rows, :]
        inside = (iota((rows, CB), 0) < valid) & (seen != 0.0) & (total != 0.0)
        ratio[:rows, :] = jnp.where(inside, seen / jnp.where(inside, total, 1.0), 0.0)

    def spread_back(blocks):
        height = 16 * blocks + 16
        for b in range(KS):
            moved = lane_shift(ratio[:height, :], b).astype(BF16)
            for m in range(blocks):
                at = (m // 2) * DEEP + b * 32
                stack[at : at + 32, (m % 2) * CB : (m % 2 + 1) * CB] = moved[m * 16 : m * 16 + 32]

    def back(m):
        value = jnp.dot(behind[...], stack[m * DEEP : (m + 1) * DEEP, :], preferred_element_type=F32)
        return value[:, :CB] * tall, value[:, CB:] * tall

    divide(whole[...], 6, 68)
    spread_back(4)
    factors = back(0) + back(1)
    for m in range(4):
        value = exact[m * 256 : (m + 1) * 256, :] * factors[m]
        exact[m * 256 : (m + 1) * 256, :] = value
        second[m * 256 : (m + 1) * 256, :] = value.astype(BF16)
    divide(jnp.concatenate(forward(ahead, second, sums, 3), axis=0), 18, 44)
    spread_back(2)
    factors = back(0)
    done = [exact[(m * 16 + 12) * ROW : (m * 16 + 28) * ROW, :] * factors[m] for m in range(2)]
    lane = iota((256, CB), 1)
    packed = jnp.where(lane < WIN, pltpu.roll(done[0], CB - HALO, 1), pltpu.roll(done[1], WIN - HALO, 1))
    flat[...] = packed
    values = seed_values(codes[...], packed)
    for p in range(DEPTHS):
        sent[p, 0:16, :] = flat[pl.ds(p, 16, stride=ROW), :]
        sent[p, 16:24, :] = values


def more_kernel(turn, rank, code, flat, sent):
    codes = listed(rank[...], code[...], turn[0] * CAP)
    values = seed_values(codes, flat[...])
    for p in range(DEPTHS):
        sent[p] = values


def gather_kernel(at):
    def kernel(parts, out):
        total = parts[0, at : at + 8, :]
        for j in range(1, DEPTHS):
            total = total + parts[j, at : at + 8, :]
        line = jnp.concatenate([total[i : i + 1, :] for i in range(LANES)], axis=1)
        for j in range(TILES):
            out[j] = line

    return kernel


def looked(turn, parts, a_row, a_lane):
    table = jnp.concatenate([parts[t] for t in range(TILES)], axis=0)
    row = a_row[...] - turn * TILES
    hot = (iota((NAMES, TILES), 1) == row[:, :TILES]).astype(F32).astype(BF16)
    parts = split3(table)
    found = jnp.dot(hot, parts[0], preferred_element_type=F32)
    found = found + jnp.dot(hot, parts[1], preferred_element_type=F32)
    found = found + jnp.dot(hot, parts[2], preferred_element_type=F32)
    total = jnp.zeros((NAMES, CB), F32)
    for i in range(LANES):
        here = iota((NAMES, CB), 1) + i * CB == a_lane[...]
        total = total + jnp.where(here, found[:, i * CB : (i + 1) * CB], 0.0)
    return jnp.broadcast_to(lane_sum(total), (NAMES, CB))


def look_kernel(turn, parts, a_row, a_lane, known, out):
    out[...] = known[...] + looked(turn[0], parts, a_row, a_lane)


def home_kernel(parts, weights, b_col, estimate, proj, lines):
    lane = iota((16, CB), 1)
    for c in range(NCB):
        a, b = parts[2 * c, :16, :], parts[2 * c + 1, :16, :]
        top = jnp.where(lane < WIN, a, pltpu.roll(b, WIN, 1))
        bottom = jnp.where(lane < WIN, pltpu.roll(a, WIN, 1), b)
        estimate[:16, c * CB : (c + 1) * CB] = top
        estimate[16:, c * CB : (c + 1) * CB] = bottom
        lines[c * ROWS : c * ROWS + 16, :] = top
        lines[c * ROWS + 16 : (c + 1) * ROWS, :] = bottom
    blocks = [lines[pl.ds(br, 64, stride=4), :] for br in range(4)]
    blocked = jnp.concatenate(blocks, axis=1)
    number = b_col[:, :64]
    number = (number & 7) * 8 + (number >> 3)
    hot = (iota((SLOTS, 64), 1) == number).astype(F32).astype(BF16)
    high, low = split2(blocked)
    picked = jnp.dot(hot, high, preferred_element_type=F32) + jnp.dot(hot, low, preferred_element_type=F32)
    product = weights[...].astype(F32) * picked
    total = product[:, :CB]
    for br in range(1, 4):
        total = total + product[:, br * CB : (br + 1) * CB]
    proj[...] = jnp.broadcast_to(jnp.sum(total, axis=1, keepdims=True), (SLOTS, CB))


def slots_kernel(parts, a_row, a_lane, known, gram, q_row, q_col, proj, out, own):
    start = known[...] + looked(0, parts, a_row, a_lane)
    padded = jnp.concatenate([start, jnp.zeros((3 * CB - NAMES, CB), F32)], axis=0)
    row = jnp.transpose(padded)[0:1, :]
    own[...] = row[:, SLOTS:]
    start_row = row[:, :SLOTS]
    terms = gram[...] * start_row
    over = jnp.sum(terms[:, :CB] + terms[:, CB:], axis=1, keepdims=True)
    place = q_col[...]
    lane = iota((SLOTS, CB), 1)
    target = ((place >> 4) & 3) * 32 + (place & 15)
    sent = jnp.where(lane == target, proj[...], 0.0) + jnp.where(lane == target + 16, over, 0.0)
    row_hot = (iota((CB, SLOTS), 0) == (q_row[0:1, :] >> 6)).astype(F32).astype(BF16)
    parts = split3(sent)
    dense = jnp.dot(row_hot, parts[0], preferred_element_type=F32)
    dense = dense + jnp.dot(row_hot, parts[1], preferred_element_type=F32)
    dense = dense + jnp.dot(row_hot, parts[2], preferred_element_type=F32)
    for j in range(DEPTHS):
        out[j] = dense[j * 8 : (j + 1) * 8]


def fold_kernel(parts, out):
    total = parts[0]
    for j in range(1, DEPTHS):
        total = total + parts[j]
    for m in range(4):
        moved = pltpu.roll(total, (CB - 32 * m) % CB, 1) if m else total
        for r in range(8):
            out[4 * r + m] = moved[r : r + 1]


def final_kernel(parts, own, out):
    total = parts[0]
    for j in range(1, TILES):
        total = total + parts[j]
    over = pltpu.roll(total, CB - 16, 1)
    initial = own[...]
    real = iota((1, CB), 1) < 16
    bottom = jnp.where(real, over + 100.0 * initial, 1.0)
    out[...] = jnp.where(real, initial * total, 0.0) / bottom


def swap(pieces, axis):
    return lax.all_to_all(pieces, axis, 0, 0)


def body(
    volume,
    measured,
    point_spread,
    entry_block,
    entry_neuron,
    footprints,
    seed_plane,
    seed_row,
    seed_col,
    owner_slot,
):
    d = lax.axis_index("depth")
    t = lax.axis_index("tile")
    where = jnp.stack([d, t, (d * TILES + t) * 16]).astype(I32)
    [windows] = call(window_kernel, [((DEPTHS, ROWS, CB), F32)], 2)(volume, point_spread)
    windows, where = lax.optimization_barrier((windows, where))
    tied = (swap(windows, "depth"), where, measured, entry_block, entry_neuron, footprints, owner_slot)
    tied = lax.optimization_barrier(tied + (seed_plane, seed_row, seed_col))
    parts, where, measured, entry_block, entry_neuron, footprints, owner_slot = tied[:7]
    seed_plane, seed_row, seed_col = tied[7:]
    parts = parts.reshape(DEPTHS * ROWS, CB)
    table = owner_slot.reshape(64, CB)
    message = ((NEAR * ROW + 4 * HALO, CB), BF16)
    band = ((256, DEEP), BF16)
    own, sensor, down, up, ahead, behind, scale, image = call(
        open_kernel,
        [((ROWS * ROW, CB), F32), ((ROWS, CB), F32), message, message, band, band, ((ROW, CB), F32), ((48, CB), F32)],
        3,
        scalars=(0,),
        scratch=[
            pltpu.VMEM((ROWS, COLS + 2 * CB), F32),
            pltpu.VMEM((64 * ROW, CB), BF16),
            pltpu.VMEM((2, 256, CB), F32),
        ],
    )(where, parts, measured)
    left = lax.ppermute(down, "tile", [(i, i + 1) for i in range(TILES - 1)])
    right = lax.ppermute(up, "tile", [(i + 1, i) for i in range(TILES - 1)])
    weights = footprints[0].reshape(SLOTS, 512)
    column = ((SLOTS, CB), I32)
    names = ((NAMES, CB), I32)
    square = ((64, CB), I32)
    gram, q_row, q_col, b_col, a_row, a_lane, rank, code, first, most = call(
        prepare_kernel,
        [
            ((SLOTS, SLOTS), F32),
            ((8, SLOTS), I32),
            column,
            column,
            names,
            names,
            square,
            square,
            ((8, CB), I32),
            ((8, CB), I32),
        ],
        8,
        scalars=(0,),
    )(
        where,
        entry_block,
        entry_neuron,
        weights,
        table,
        seed_plane.reshape(64, CB),
        seed_row.reshape(64, CB),
        seed_col.reshape(64, CB),
    )
    sent, flat = call(
        iterate_kernel,
        [((DEPTHS, 24, CB), F32), ((256, CB), F32)],
        9,
        scratch=[
            pltpu.VMEM((64 * ROW, CB), F32),
            pltpu.VMEM((64 * ROW, CB), BF16),
            pltpu.VMEM((96, CB), F32),
            pltpu.VMEM((80, CB), F32),
            pltpu.VMEM((2, 256, CB), F32),
            pltpu.VMEM((80, CB), F32),
            pltpu.VMEM((2 * DEEP, 2 * CB), BF16),
        ],
    )(own, left, right, sensor, image, ahead, behind, scale, first)
    parts, most = lax.optimization_barrier((swap(sent, "depth"), most))

    def share(values, at):
        [values] = call(gather_kernel(at), [((TILES, 1, CAP), F32)], 1)(values)
        return swap(values, "tile")

    def look(turn, values, known):
        return call(look_kernel, [((NAMES, CB), F32)], 5, scalars=(0,))(
            turn, values, a_row, a_lane, known
        )[0]

    def another(step, known):
        turn = jnp.reshape(step, (1,))
        [values] = call(more_kernel, [((DEPTHS, 8, CB), F32)], 4, scalars=(0,))(
            turn, rank, code, flat
        )
        return look(turn, share(swap(values, "depth"), 0), known)

    rounds = (most[0, 0] + CAP - 1) // CAP
    shared, none = lax.optimization_barrier((share(parts, 16), jnp.zeros((NAMES, CB), F32)))
    known = lax.fori_loop(1, rounds, another, none)
    estimate, proj = call(
        home_kernel,
        [((ROWS, COLS), F32), ((SLOTS, CB), F32)],
        3,
        scratch=[pltpu.VMEM((NCB * ROWS, CB), F32)],
    )(parts, weights, b_col)
    sent, own = call(slots_kernel, [((DEPTHS, 8, CB), F32), ((1, CB), F32)], 8)(
        shared, a_row, a_lane, known, gram, q_row, q_col, proj
    )
    [sent] = call(fold_kernel, [((TILES, 1, CB), F32)], 1)(swap(sent, "depth"))
    [demixed] = call(final_kernel, [((1, CB), F32)], 2)(swap(sent, "tile"), own)
    return estimate[None], demixed[0, :16]


def solution(mesh):
    in_specs = (
        P("depth", "tile", None),
        P("tile", None),
        P("depth", None, None),
        P("tile", "depth"),
        P("tile", "depth"),
        P("tile", "depth", None, None),
        P(),
        P(),
        P(),
        P(),
    )
    out_specs = (P("depth", "tile", None), P(("depth", "tile")))
    return jax.shard_map(body, mesh=mesh, in_specs=in_specs, out_specs=out_specs, check_vma=False)
```

```python
import jax
import jax.numpy as jnp
from jax import lax
from jax.experimental import pallas as pl
from jax.experimental.pallas import tpu as pltpu
from jax.sharding import PartitionSpec as P

F32 = jnp.float32
BF16 = jnp.bfloat16
I32 = jnp.int32
KS = 13
RADIUS = 6
ROWS = 32
COLS = 1024
CB = 128
NCB = COLS // CB
DEPTHS = 16
TILES = 32
SLOTS = 256
NEURONS = 8192
HALO = 24
WIN = 64
LIVE = WIN + 2 * HALO
ROW = DEPTHS
BLOCK = 16
DEEP = 32 * ROW
CAP = 384
LANES = CAP // CB
NEAR = 12
NAMES = SLOTS + 16
VMEM = pl.BlockSpec(memory_space=pltpu.VMEM)
SMEM = pl.BlockSpec(memory_space=pltpu.SMEM)


def call(kernel, outs, n_in, scalars=(), scratch=(), mib=24):
    return pl.pallas_call(
        kernel,
        out_shape=[jax.ShapeDtypeStruct(s, t) for s, t in outs],
        in_specs=[SMEM if i in scalars else VMEM for i in range(n_in)],
        out_specs=[VMEM] * len(outs),
        scratch_shapes=list(scratch),
        compiler_params=pltpu.CompilerParams(vmem_limit_bytes=mib * 2**20),
    )


def iota(shape, dim):
    return lax.broadcasted_iota(I32, shape, dim)


def split2(x):
    high = x.astype(BF16)
    return high, (x - high.astype(F32)).astype(BF16)


def split3(x):
    high = x.astype(BF16)
    rest = x - high.astype(F32)
    mid = rest.astype(BF16)
    return high, mid, (rest - mid.astype(F32)).astype(BF16)


def column_of(row):
    n = row.shape[1]
    return jnp.transpose(jnp.broadcast_to(row, (CB, n)))


def lane_sum(x):
    return jnp.sum(x, axis=1, keepdims=True)


def prepare_kernel(
    where, block, neuron, weights, owner, s_plane, s_row, s_col,
    gram, q_row, q_col, b_col, a_row, a_lane, rank, code, first, most,
):
    foot = weights[...]
    product = lax.dot_general(foot, foot, (((1,), (1,)), ((), ())), preferred_element_type=F32)
    blocks = column_of(block[...].astype(F32))
    same = jnp.concatenate([blocks, blocks], axis=1) == block[...].astype(F32)
    gram[...] = jnp.where(same, product, 0.0)
    b_col[...] = blocks.astype(I32)
    table = owner[...]
    number = iota((64, CB), 0) * CB + iota((64, CB), 1)
    own = jnp.zeros((16, CB), F32)
    for i in range(16):
        hit = jnp.sum(jnp.where(table == where[2] + i, number.astype(F32), 0.0), axis=0, keepdims=True)
        own = jnp.where(iota((16, CB), 0) == i, lane_sum(hit), own)
    names = jnp.concatenate([column_of(neuron[...].astype(F32)), own], axis=0).astype(I32)
    row, col = s_row[...], s_col[...]
    tile, window = row >> 5, col >> 6
    tables = [tile, table >> 7, table & 127]
    tables = jnp.concatenate([x.astype(F32) for x in tables], axis=1).astype(BF16)
    hot = (iota((NAMES, 64), 1) == (names[:, :64] >> 7)).astype(F32).astype(BF16)
    found = jnp.dot(hot, tables, preferred_element_type=F32)
    lane_hot = iota((NAMES, CB), 1) == (names & 127)
    picked = [lane_sum(jnp.where(lane_hot, found[:, i * CB : (i + 1) * CB], 0.0)) for i in range(3)]
    n_tile = picked[0].astype(I32)
    place = jnp.broadcast_to(picked[1] * 128.0 + picked[2], (NAMES, CB))[:SLOTS]
    place = jnp.where(names[:SLOTS] >= 0, place, -1.0)
    q_col[...] = place.astype(I32)
    q_row[...] = jnp.transpose(place)[0:8, :].astype(I32)
    both = jnp.zeros((TILES, 1), F32)
    for r in range(0, 64, 8):
        tiles = jnp.zeros((TILES, CB), F32)
        for i in range(r, r + 8):
            tiles = tiles + (iota((TILES, CB), 0) == tile[i : i + 1, :]).astype(F32)
        both = both + lane_sum(tiles)
    top = jnp.max(both, axis=0, keepdims=True)
    most[...] = jnp.broadcast_to(top, (8, CB)).astype(I32)
    wide = jnp.concatenate([both, jnp.zeros((CB - TILES, 1), F32)], axis=0)
    held = jnp.transpose(jnp.broadcast_to(wide, (CB, CB)))[0:1, :]
    earlier = lane_sum(jnp.where(iota((NAMES, CB), 1) < n_tile, held, 0.0))
    keys = tile * NEURONS + number
    high = jnp.broadcast_to(n_tile * NEURONS, (NAMES, CB)) + names
    count = jnp.zeros((NAMES, CB), F32)
    for r in range(64):
        count = count + jnp.where(keys[r : r + 1, :] < high, 1.0, 0.0)
    position = jnp.broadcast_to(lane_sum(count) - earlier, (NAMES, CB)).astype(I32)
    turn = jnp.zeros((NAMES, CB), I32)
    for i in range(1, (NEURONS + CAP - 1) // CAP):
        turn = turn + (position >= i * CAP).astype(I32)
    a_row[...] = jnp.where(names >= 0, turn * TILES + n_tile, -1)
    a_lane[...] = position - turn * CAP
    local = tile == where[1]
    mask = local.astype(F32)
    before = (iota((CB, CB), 0) < iota((CB, CB), 1)).astype(F32).astype(BF16)
    inside = jnp.dot(mask.astype(BF16), before, preferred_element_type=F32)
    rows = jnp.broadcast_to(lane_sum(mask), (64, CB)).astype(BF16)
    above = (iota((64, 64), 1) < iota((64, 64), 0)).astype(F32).astype(BF16)
    inside = inside + jnp.dot(above, rows, preferred_element_type=F32)
    order = jnp.where(local & (window == where[0]), inside, -1.0).astype(I32)
    spot = ((row >> 4) & 1) * WIN + (col & (WIN - 1))
    coded = ((row & 15) * ROW + s_plane[...]) * CB + spot
    rank[...] = order
    code[...] = coded
    first[...] = listed(order, coded, 0)


def listed(order, coded, start):
    place = order - start
    place = jnp.where(place < CAP, place, -1)
    total = jnp.zeros((32, CB), F32)
    for r in range(0, 64, 8):
        lines = [place[i : i + 1, :] for i in range(r, r + 8)]
        codes = [coded[i : i + 1, :] for i in range(r, r + 8)]
        left = []
        for at, code in zip(lines, codes):
            here = iota((8, CB), 0) == (at >> 7)
            left.append(
                jnp.concatenate(
                    [
                        jnp.where(here, (code >> 7).astype(F32), 0.0),
                        jnp.where(here, (code & 127).astype(F32), 0.0),
                        jnp.where(here, 1.0, 0.0),
                        jnp.zeros((8, CB), F32),
                    ],
                    axis=0,
                )
            )
        left = jnp.concatenate(left, axis=1).astype(BF16)
        right = [(iota((CB, CB), 0) == jnp.where(at >= 0, at & 127, -1)).astype(F32) for at in lines]
        right = jnp.concatenate(right, axis=1).astype(BF16)
        total = total + lax.dot_general(
            left, right, (((1,), (1,)), ((), ())), preferred_element_type=F32
        )
    value = total[0:8] * 128.0 + total[8:16]
    return jnp.where(total[16:24] > 0.0, value, -1.0).astype(I32)


def seed_values(codes, flat):
    parts = split3(flat)
    result = []
    for i in range(LANES):
        index = column_of(codes[i : i + 1, :].astype(F32)).astype(I32)
        key = jnp.concatenate([index, index], axis=1) >> 7
        hot = (iota((CB, 256), 1) == key).astype(F32).astype(BF16)
        found = jnp.dot(hot, parts[0], preferred_element_type=F32)
        found = found + jnp.dot(hot, parts[1], preferred_element_type=F32)
        found = found + jnp.dot(hot, parts[2], preferred_element_type=F32)
        picked = jnp.where(iota((CB, CB), 1) == (index & (CB - 1)), found, 0.0)
        result.append(jnp.sum(jnp.transpose(picked), axis=0, keepdims=True))
    result.append(jnp.zeros((8 - LANES, CB), F32))
    return jnp.concatenate(result, axis=0)


def window_kernel(volume, spread, windows):
    lane = iota((ROWS, CB), 1)
    taps = jnp.concatenate([spread[0].astype(F32), jnp.zeros((KS, CB - KS), F32)], axis=1)
    taps = jnp.concatenate([pltpu.roll(taps, LIVE, 1), jnp.zeros((ROWS - KS, CB), F32)], axis=0)
    zeros = jnp.zeros((ROWS, CB), F32)
    padded = jnp.concatenate([zeros, volume[0], zeros], axis=1)
    for j in range(DEPTHS):
        start = CB - HALO + WIN * j
        low = start // CB * CB
        moved = pltpu.roll(padded[:, low : low + 2 * CB], 2 * CB - start % CB, 1)[:, :CB]
        windows[j] = jnp.where(lane < LIVE, moved, taps)


def lane_shift(x, b):
    shift = (RADIUS - b) % CB
    return pltpu.roll(x, shift, 1) if shift else x


def forward(ahead, source, sums, blocks):
    result = []
    for m in range(0, blocks, 2):
        pair = range(m, min(m + 2, blocks))
        right = jnp.concatenate([source[i * 256 : i * 256 + DEEP, :] for i in pair], axis=1)
        value = jnp.dot(ahead[...], right, preferred_element_type=F32)
        for i in pair:
            at = (i - m) * CB
            sums[i - m] = value[:, at : at + CB]
        for i in pair:
            total = lane_shift(sums[i - m, pl.ds(0, BLOCK, stride=16), :], 0)
            for b in range(1, KS):
                total = total + lane_shift(sums[i - m, pl.ds(b, BLOCK, stride=16), :], b)
            result.append(total)
    return result


def open_kernel(
    where, parts, measured,
    own, sensor, down, up, ahead, behind, scale, image,
    wide, rounded, sums,
):
    lane = iota((ROW, CB), 1)
    rounded[: NEAR * ROW, :] = jnp.zeros((NEAR * ROW, CB), BF16)
    rounded[(NEAR + ROWS) * ROW :, :] = jnp.zeros(((NEAR + 8) * ROW, CB), BF16)
    for r in range(ROWS):
        line = jnp.where(lane < LIVE, parts[pl.ds(r, ROW, stride=ROWS), :], 0.0)
        own[r * ROW : (r + 1) * ROW, :] = line
        line = line.astype(BF16)
        rounded[(NEAR + r) * ROW : (NEAR + r + 1) * ROW, :] = line
        if r < NEAR:
            up[r * ROW : (r + 1) * ROW, :] = line
        if r >= ROWS - NEAR:
            at = (r - ROWS + NEAR) * ROW
            down[at : at + ROW, :] = line
    zeros = jnp.zeros((ROWS, CB), F32)
    wide[:, :CB] = zeros
    wide[:, CB : CB + COLS] = measured[...]
    wide[:, CB + COLS :] = zeros
    start = CB - HALO + WIN * where[0]
    low = pl.multiple_of((start >> 7) * CB, CB)
    moved = pltpu.roll(wide[:, pl.ds(low, 2 * CB)], 2 * CB - (start & (CB - 1)), 1)[:, :CB]
    view = jnp.where(iota((ROWS, CB), 1) < LIVE, moved, 0.0)
    sensor[...] = view
    taps = jnp.concatenate([parts[pl.ds(a, ROW, stride=ROWS), :] for a in range(16)], axis=0)
    taps = jnp.where(iota((256, CB), 1) >= LIVE, taps, 0.0)
    first = jnp.transpose(taps)[LIVE:, :]
    first = jnp.concatenate([first, jnp.zeros((16, 256), F32)], axis=1)
    for i in range(BLOCK):
        moved = pltpu.roll(first, i * ROW, 1) if i else first
        ahead[i * 16 : (i + 1) * 16, :] = moved.astype(BF16)
    lane = iota((CB, DEEP), 1)
    hot = (iota((CB, DEEP), 0) == LIVE + KS - 1 - (lane >> 5)).astype(F32).astype(BF16)
    spread = jnp.dot(taps.astype(BF16), hot, preferred_element_type=F32)
    inside = iota((ROW, DEEP), 1)
    within = jnp.where(inside < KS * 32, inside & 31, 32)
    second = jnp.zeros((ROW, DEEP), F32)
    for a in range(KS):
        second = jnp.where(within == KS - 1 - a, spread[a * ROW : (a + 1) * ROW], second)
    for i in range(BLOCK):
        moved = pltpu.roll(second, i, 1) if i else second
        behind[i * ROW : (i + 1) * ROW, :] = moved.astype(BF16)
    total = taps[:ROW]
    for a in range(1, KS):
        total = total + taps[a * ROW : (a + 1) * ROW]
    norm = jnp.sum(total, axis=1, keepdims=True)
    scale[...] = jnp.broadcast_to(1.0 / norm, (ROW, CB))
    image[...] = jnp.concatenate(forward(ahead, rounded, sums, 3), axis=0)
    for out, part, lines in (
        (up, view[:HALO], image[:HALO, :]),
        (down, view[ROWS - HALO :], image[20 : 20 + HALO, :]),
    ):
        rows = []
        for x in (part, lines):
            high = x.astype(BF16).astype(F32)
            rows += [high, x - high]
        out[NEAR * ROW :, :] = jnp.concatenate(rows, axis=0).astype(BF16)


def iterate_kernel(
    own, left, right, sensor, image, ahead, behind, scale, codes,
    sent, flat, exact, second, light, whole, sums, ratio, stack,
):
    near = NEAR * ROW
    exact[:near, :] = left[:near].astype(F32)
    exact[near : near + ROWS * ROW, :] = own[...]
    exact[near + ROWS * ROW : 2 * near + ROWS * ROW, :] = right[:near].astype(F32)
    exact[2 * near + ROWS * ROW :, :] = jnp.zeros((8 * ROW, CB), F32)
    before, after = left[near:].astype(F32), right[near:].astype(F32)
    light[:HALO, :] = before[:HALO] + before[HALO : 2 * HALO]
    light[HALO : HALO + ROWS, :] = sensor[...]
    light[HALO + ROWS : 2 * HALO + ROWS, :] = after[:HALO] + after[HALO : 2 * HALO]
    light[2 * HALO + ROWS :, :] = jnp.zeros((16, CB), F32)
    blank = jnp.zeros((20, CB), F32)
    total = jnp.concatenate([blank[:12], image[...], blank], axis=0)
    above = jnp.concatenate([before[2 * HALO : 3 * HALO] + before[3 * HALO :], jnp.zeros((56, CB), F32)], axis=0)
    below = after[2 * HALO : 3 * HALO] + after[3 * HALO :]
    below = jnp.concatenate([jnp.zeros((44, CB), F32), below, blank[:12]], axis=0)
    whole[...] = total + above + below
    for m in range(2):
        stack[m * DEEP + KS * 32 : (m + 1) * DEEP, :] = jnp.zeros((DEEP - KS * 32, 2 * CB), BF16)
    tall = jnp.concatenate([scale[...]] * BLOCK, axis=0)

    def divide(total, offset, valid):
        rows = total.shape[0]
        seen = light[offset : offset + rows, :]
        inside = (iota((rows, CB), 0) < valid) & (seen != 0.0) & (total != 0.0)
        ratio[:rows, :] = jnp.where(inside, seen / jnp.where(inside, total, 1.0), 0.0)

    def spread_back(blocks):
        height = 16 * blocks + 16
        for b in range(KS):
            moved = lane_shift(ratio[:height, :], b).astype(BF16)
            for m in range(blocks):
                at = (m // 2) * DEEP + b * 32
                stack[at : at + 32, (m % 2) * CB : (m % 2 + 1) * CB] = moved[m * 16 : m * 16 + 32]

    def back(m):
        value = jnp.dot(behind[...], stack[m * DEEP : (m + 1) * DEEP, :], preferred_element_type=F32)
        return value[:, :CB] * tall, value[:, CB:] * tall

    divide(whole[...], 6, 68)
    spread_back(4)
    factors = back(0) + back(1)
    for m in range(4):
        value = exact[m * 256 : (m + 1) * 256, :] * factors[m]
        exact[m * 256 : (m + 1) * 256, :] = value
        second[m * 256 : (m + 1) * 256, :] = value.astype(BF16)
    divide(jnp.concatenate(forward(ahead, second, sums, 3), axis=0), 18, 44)
    spread_back(2)
    factors = back(0)
    done = [exact[(m * 16 + 12) * ROW : (m * 16 + 28) * ROW, :] * factors[m] for m in range(2)]
    lane = iota((256, CB), 1)
    packed = jnp.where(lane < WIN, pltpu.roll(done[0], CB - HALO, 1), pltpu.roll(done[1], WIN - HALO, 1))
    flat[...] = packed
    values = seed_values(codes[...], packed)
    for p in range(DEPTHS):
        sent[p, 0:16, :] = flat[pl.ds(p, 16, stride=ROW), :]
        sent[p, 16:24, :] = values


def more_kernel(turn, rank, code, flat, sent):
    codes = listed(rank[...], code[...], turn[0] * CAP)
    values = seed_values(codes, flat[...])
    for p in range(DEPTHS):
        sent[p] = values


def gather_kernel(at):
    def kernel(parts, out):
        total = parts[0, at : at + 8, :]
        for j in range(1, DEPTHS):
            total = total + parts[j, at : at + 8, :]
        line = jnp.concatenate([total[i : i + 1, :] for i in range(LANES)], axis=1)
        for j in range(TILES):
            out[j] = line

    return kernel


def looked(turn, parts, a_row, a_lane):
    table = jnp.concatenate([parts[t] for t in range(TILES)], axis=0)
    row = a_row[...] - turn * TILES
    hot = (iota((NAMES, TILES), 1) == row[:, :TILES]).astype(F32).astype(BF16)
    parts = split3(table)
    found = jnp.dot(hot, parts[0], preferred_element_type=F32)
    found = found + jnp.dot(hot, parts[1], preferred_element_type=F32)
    found = found + jnp.dot(hot, parts[2], preferred_element_type=F32)
    total = jnp.zeros((NAMES, CB), F32)
    for i in range(LANES):
        here = iota((NAMES, CB), 1) + i * CB == a_lane[...]
        total = total + jnp.where(here, found[:, i * CB : (i + 1) * CB], 0.0)
    return jnp.broadcast_to(lane_sum(total), (NAMES, CB))


def look_kernel(turn, parts, a_row, a_lane, known, out):
    out[...] = known[...] + looked(turn[0], parts, a_row, a_lane)


def home_kernel(parts, weights, b_col, estimate, proj, lines):
    lane = iota((16, CB), 1)
    for c in range(NCB):
        a, b = parts[2 * c, :16, :], parts[2 * c + 1, :16, :]
        top = jnp.where(lane < WIN, a, pltpu.roll(b, WIN, 1))
        bottom = jnp.where(lane < WIN, pltpu.roll(a, WIN, 1), b)
        estimate[:16, c * CB : (c + 1) * CB] = top
        estimate[16:, c * CB : (c + 1) * CB] = bottom
        lines[c * ROWS : c * ROWS + 16, :] = top
        lines[c * ROWS + 16 : (c + 1) * ROWS, :] = bottom
    blocks = [lines[pl.ds(br, 64, stride=4), :] for br in range(4)]
    blocked = jnp.concatenate(blocks, axis=1)
    number = b_col[:, :64]
    number = (number & 7) * 8 + (number >> 3)
    hot = (iota((SLOTS, 64), 1) == number).astype(F32).astype(BF16)
    high, low = split2(blocked)
    picked = jnp.dot(hot, high, preferred_element_type=F32) + jnp.dot(hot, low, preferred_element_type=F32)
    product = weights[...].astype(F32) * picked
    total = product[:, :CB]
    for br in range(1, 4):
        total = total + product[:, br * CB : (br + 1) * CB]
    proj[...] = jnp.broadcast_to(jnp.sum(total, axis=1, keepdims=True), (SLOTS, CB))


def slots_kernel(parts, a_row, a_lane, known, gram, q_row, q_col, proj, out, own):
    start = known[...] + looked(0, parts, a_row, a_lane)
    padded = jnp.concatenate([start, jnp.zeros((3 * CB - NAMES, CB), F32)], axis=0)
    row = jnp.transpose(padded)[0:1, :]
    own[...] = row[:, SLOTS:]
    start_row = row[:, :SLOTS]
    terms = gram[...] * start_row
    over = jnp.sum(terms[:, :CB] + terms[:, CB:], axis=1, keepdims=True)
    place = q_col[...]
    lane = iota((SLOTS, CB), 1)
    target = ((place >> 4) & 3) * 32 + (place & 15)
    sent = jnp.where(lane == target, proj[...], 0.0) + jnp.where(lane == target + 16, over, 0.0)
    row_hot = (iota((CB, SLOTS), 0) == (q_row[0:1, :] >> 6)).astype(F32).astype(BF16)
    parts = split3(sent)
    dense = jnp.dot(row_hot, parts[0], preferred_element_type=F32)
    dense = dense + jnp.dot(row_hot, parts[1], preferred_element_type=F32)
    dense = dense + jnp.dot(row_hot, parts[2], preferred_element_type=F32)
    for j in range(DEPTHS):
        out[j] = dense[j * 8 : (j + 1) * 8]


def fold_kernel(parts, out):
    total = parts[0]
    for j in range(1, DEPTHS):
        total = total + parts[j]
    for m in range(4):
        moved = pltpu.roll(total, (CB - 32 * m) % CB, 1) if m else total
        for r in range(8):
            out[4 * r + m] = moved[r : r + 1]


def final_kernel(parts, own, out):
    total = parts[0]
    for j in range(1, TILES):
        total = total + parts[j]
    over = pltpu.roll(total, CB - 16, 1)
    initial = own[...]
    real = iota((1, CB), 1) < 16
    bottom = jnp.where(real, over + 100.0 * initial, 1.0)
    out[...] = jnp.where(real, initial * total, 0.0) / bottom


def swap(pieces, axis):
    return lax.all_to_all(pieces, axis, 0, 0)


def body(
    volume,
    measured,
    point_spread,
    entry_block,
    entry_neuron,
    footprints,
    seed_plane,
    seed_row,
    seed_col,
    owner_slot,
):
    d = lax.axis_index("depth")
    t = lax.axis_index("tile")
    where = jnp.stack([d, t, (d * TILES + t) * 16]).astype(I32)
    table = owner_slot.reshape(64, CB)
    [windows] = call(window_kernel, [((DEPTHS, ROWS, CB), F32)], 2)(volume, point_spread)
    parts = swap(windows, "depth").reshape(DEPTHS * ROWS, CB)
    weights = footprints[0].reshape(SLOTS, 512)
    column = ((SLOTS, CB), I32)
    names = ((NAMES, CB), I32)
    square = ((64, CB), I32)
    gram, q_row, q_col, b_col, a_row, a_lane, rank, code, first, most = call(
        prepare_kernel,
        [
            ((SLOTS, SLOTS), F32),
            ((8, SLOTS), I32),
            column,
            column,
            names,
            names,
            square,
            square,
            ((8, CB), I32),
            ((8, CB), I32),
        ],
        8,
        scalars=(0,),
    )(
        where,
        entry_block,
        entry_neuron,
        weights,
        table,
        seed_plane.reshape(64, CB),
        seed_row.reshape(64, CB),
        seed_col.reshape(64, CB),
    )
    view, first = lax.optimization_barrier((measured, first))
    message = ((NEAR * ROW + 4 * HALO, CB), BF16)
    band = ((256, DEEP), BF16)
    own, sensor, down, up, ahead, behind, scale, image = call(
        open_kernel,
        [((ROWS * ROW, CB), F32), ((ROWS, CB), F32), message, message, band, band, ((ROW, CB), F32), ((48, CB), F32)],
        3,
        scalars=(0,),
        scratch=[
            pltpu.VMEM((ROWS, COLS + 2 * CB), F32),
            pltpu.VMEM((64 * ROW, CB), BF16),
            pltpu.VMEM((2, 256, CB), F32),
        ],
    )(where, parts, view)
    left = lax.ppermute(down, "tile", [(i, i + 1) for i in range(TILES - 1)])
    right = lax.ppermute(up, "tile", [(i + 1, i) for i in range(TILES - 1)])
    sent, flat = call(
        iterate_kernel,
        [((DEPTHS, 24, CB), F32), ((256, CB), F32)],
        9,
        scratch=[
            pltpu.VMEM((64 * ROW, CB), F32),
            pltpu.VMEM((64 * ROW, CB), BF16),
            pltpu.VMEM((96, CB), F32),
            pltpu.VMEM((80, CB), F32),
            pltpu.VMEM((2, 256, CB), F32),
            pltpu.VMEM((80, CB), F32),
            pltpu.VMEM((2 * DEEP, 2 * CB), BF16),
        ],
    )(own, left, right, sensor, image, ahead, behind, scale, first)
    parts, most = lax.optimization_barrier((swap(sent, "depth"), most))

    def share(values, at):
        [values] = call(gather_kernel(at), [((TILES, 1, CAP), F32)], 1)(values)
        return swap(values, "tile")

    def look(turn, values, known):
        return call(look_kernel, [((NAMES, CB), F32)], 5, scalars=(0,))(
            turn, values, a_row, a_lane, known
        )[0]

    def another(step, known):
        turn = jnp.reshape(step, (1,))
        [values] = call(more_kernel, [((DEPTHS, 8, CB), F32)], 4, scalars=(0,))(
            turn, rank, code, flat
        )
        return look(turn, share(swap(values, "depth"), 0), known)

    rounds = (most[0, 0] + CAP - 1) // CAP
    shared, none = lax.optimization_barrier((share(parts, 16), jnp.zeros((NAMES, CB), F32)))
    known = lax.fori_loop(1, rounds, another, none)
    estimate, proj = call(
        home_kernel,
        [((ROWS, COLS), F32), ((SLOTS, CB), F32)],
        3,
        scratch=[pltpu.VMEM((NCB * ROWS, CB), F32)],
    )(parts, weights, b_col)
    sent, own = call(slots_kernel, [((DEPTHS, 8, CB), F32), ((1, CB), F32)], 8)(
        shared, a_row, a_lane, known, gram, q_row, q_col, proj
    )
    [sent] = call(fold_kernel, [((TILES, 1, CB), F32)], 1)(swap(sent, "depth"))
    [demixed] = call(final_kernel, [((1, CB), F32)], 2)(swap(sent, "tile"), own)
    return estimate[None], demixed[0, :16]


def solution(mesh):
    in_specs = (
        P("depth", "tile", None),
        P("tile", None),
        P("depth", None, None),
        P("tile", "depth"),
        P("tile", "depth"),
        P("tile", "depth", None, None),
        P(),
        P(),
        P(),
        P(),
    )
    out_specs = (P("depth", "tile", None), P(("depth", "tile")))
    return jax.shard_map(body, mesh=mesh, in_specs=in_specs, out_specs=out_specs, check_vma=False)
```

```python
import jax
import jax.numpy as jnp
from jax import lax
from jax.experimental import pallas as pl
from jax.experimental.pallas import tpu as pltpu
from jax.sharding import PartitionSpec as P

F32 = jnp.float32
BF16 = jnp.bfloat16
I32 = jnp.int32
KS = 13
RADIUS = 6
ROWS = 32
COLS = 1024
CB = 128
NCB = COLS // CB
DEPTHS = 16
TILES = 32
SLOTS = 256
NEURONS = 8192
HALO = 24
WIN = 64
LIVE = WIN + 2 * HALO
ROW = DEPTHS
BLOCK = 16
DEEP = 32 * ROW
CAP = 384
LANES = CAP // CB
NEAR = 12
NAMES = SLOTS + 16
VMEM = pl.BlockSpec(memory_space=pltpu.VMEM)
SMEM = pl.BlockSpec(memory_space=pltpu.SMEM)


def call(kernel, outs, n_in, scalars=(), scratch=(), mib=24):
    return pl.pallas_call(
        kernel,
        out_shape=[jax.ShapeDtypeStruct(s, t) for s, t in outs],
        in_specs=[SMEM if i in scalars else VMEM for i in range(n_in)],
        out_specs=[VMEM] * len(outs),
        scratch_shapes=list(scratch),
        compiler_params=pltpu.CompilerParams(vmem_limit_bytes=mib * 2**20),
    )


def iota(shape, dim):
    return lax.broadcasted_iota(I32, shape, dim)


def split2(x):
    high = x.astype(BF16)
    return high, (x - high.astype(F32)).astype(BF16)


def split3(x):
    high = x.astype(BF16)
    rest = x - high.astype(F32)
    mid = rest.astype(BF16)
    return high, mid, (rest - mid.astype(F32)).astype(BF16)


def column_of(row):
    n = row.shape[1]
    return jnp.transpose(jnp.broadcast_to(row, (CB, n)))


def lane_sum(x):
    return jnp.sum(x, axis=1, keepdims=True)


def prepare_kernel(
    where, block, neuron, weights, owner, s_plane, s_row, s_col,
    gram, q_row, q_col, b_col, a_row, a_lane, rank, code, first, most,
):
    foot = weights[...]
    product = lax.dot_general(foot, foot, (((1,), (1,)), ((), ())), preferred_element_type=F32)
    blocks = column_of(block[...].astype(F32))
    same = jnp.concatenate([blocks, blocks], axis=1) == block[...].astype(F32)
    gram[...] = jnp.where(same, product, 0.0)
    b_col[...] = blocks.astype(I32)
    table = owner[...]
    number = iota((64, CB), 0) * CB + iota((64, CB), 1)
    own = jnp.zeros((16, CB), F32)
    for i in range(16):
        hit = jnp.sum(jnp.where(table == where[2] + i, number.astype(F32), 0.0), axis=0, keepdims=True)
        own = jnp.where(iota((16, CB), 0) == i, lane_sum(hit), own)
    names = jnp.concatenate([column_of(neuron[...].astype(F32)), own], axis=0).astype(I32)
    row, col = s_row[...], s_col[...]
    tile, window = row >> 5, col >> 6
    tables = [tile, table >> 7, table & 127]
    tables = jnp.concatenate([x.astype(F32) for x in tables], axis=1).astype(BF16)
    hot = (iota((NAMES, 64), 1) == (names[:, :64] >> 7)).astype(F32).astype(BF16)
    found = jnp.dot(hot, tables, preferred_element_type=F32)
    lane_hot = iota((NAMES, CB), 1) == (names & 127)
    picked = [lane_sum(jnp.where(lane_hot, found[:, i * CB : (i + 1) * CB], 0.0)) for i in range(3)]
    n_tile = picked[0].astype(I32)
    place = jnp.broadcast_to(picked[1] * 128.0 + picked[2], (NAMES, CB))[:SLOTS]
    place = jnp.where(names[:SLOTS] >= 0, place, -1.0)
    q_col[...] = place.astype(I32)
    q_row[...] = jnp.transpose(place)[0:8, :].astype(I32)
    both = jnp.zeros((TILES, 1), F32)
    for r in range(0, 64, 8):
        tiles = jnp.zeros((TILES, CB), F32)
        for i in range(r, r + 8):
            tiles = tiles + (iota((TILES, CB), 0) == tile[i : i + 1, :]).astype(F32)
        both = both + lane_sum(tiles)
    top = jnp.max(both, axis=0, keepdims=True)
    most[...] = jnp.broadcast_to(top, (8, CB)).astype(I32)
    wide = jnp.concatenate([both, jnp.zeros((CB - TILES, 1), F32)], axis=0)
    held = jnp.transpose(jnp.broadcast_to(wide, (CB, CB)))[0:1, :]
    earlier = lane_sum(jnp.where(iota((NAMES, CB), 1) < n_tile, held, 0.0))
    keys = tile * NEURONS + number
    high = jnp.broadcast_to(n_tile * NEURONS, (NAMES, CB)) + names
    count = jnp.zeros((NAMES, CB), F32)
    for r in range(64):
        count = count + jnp.where(keys[r : r + 1, :] < high, 1.0, 0.0)
    position = jnp.broadcast_to(lane_sum(count) - earlier, (NAMES, CB)).astype(I32)
    turn = jnp.zeros((NAMES, CB), I32)
    for i in range(1, (NEURONS + CAP - 1) // CAP):
        turn = turn + (position >= i * CAP).astype(I32)
    a_row[...] = jnp.where(names >= 0, turn * TILES + n_tile, -1)
    a_lane[...] = position - turn * CAP
    local = tile == where[1]
    mask = local.astype(F32)
    before = (iota((CB, CB), 0) < iota((CB, CB), 1)).astype(F32).astype(BF16)
    inside = jnp.dot(mask.astype(BF16), before, preferred_element_type=F32)
    rows = jnp.broadcast_to(lane_sum(mask), (64, CB)).astype(BF16)
    above = (iota((64, 64), 1) < iota((64, 64), 0)).astype(F32).astype(BF16)
    inside = inside + jnp.dot(above, rows, preferred_element_type=F32)
    order = jnp.where(local & (window == where[0]), inside, -1.0).astype(I32)
    spot = ((row >> 4) & 1) * WIN + (col & (WIN - 1))
    coded = ((row & 15) * ROW + s_plane[...]) * CB + spot
    rank[...] = order
    code[...] = coded
    first[...] = listed(order, coded, 0)


def listed(order, coded, start):
    place = order - start
    place = jnp.where(place < CAP, place, -1)
    total = jnp.zeros((32, CB), F32)
    for r in range(0, 64, 8):
        lines = [place[i : i + 1, :] for i in range(r, r + 8)]
        codes = [coded[i : i + 1, :] for i in range(r, r + 8)]
        left = []
        for at, code in zip(lines, codes):
            here = iota((8, CB), 0) == (at >> 7)
            left.append(
                jnp.concatenate(
                    [
                        jnp.where(here, (code >> 7).astype(F32), 0.0),
                        jnp.where(here, (code & 127).astype(F32), 0.0),
                        jnp.where(here, 1.0, 0.0),
                        jnp.zeros((8, CB), F32),
                    ],
                    axis=0,
                )
            )
        left = jnp.concatenate(left, axis=1).astype(BF16)
        right = [(iota((CB, CB), 0) == jnp.where(at >= 0, at & 127, -1)).astype(F32) for at in lines]
        right = jnp.concatenate(right, axis=1).astype(BF16)
        total = total + lax.dot_general(
            left, right, (((1,), (1,)), ((), ())), preferred_element_type=F32
        )
    value = total[0:8] * 128.0 + total[8:16]
    return jnp.where(total[16:24] > 0.0, value, -1.0).astype(I32)


def seed_values(codes, flat):
    parts = split3(flat)
    result = []
    for i in range(LANES):
        index = column_of(codes[i : i + 1, :].astype(F32)).astype(I32)
        key = jnp.concatenate([index, index], axis=1) >> 7
        hot = (iota((CB, 256), 1) == key).astype(F32).astype(BF16)
        found = jnp.dot(hot, parts[0], preferred_element_type=F32)
        found = found + jnp.dot(hot, parts[1], preferred_element_type=F32)
        found = found + jnp.dot(hot, parts[2], preferred_element_type=F32)
        picked = jnp.where(iota((CB, CB), 1) == (index & (CB - 1)), found, 0.0)
        result.append(jnp.sum(jnp.transpose(picked), axis=0, keepdims=True))
    result.append(jnp.zeros((8 - LANES, CB), F32))
    return jnp.concatenate(result, axis=0)


def window_kernel(volume, spread, windows):
    lane = iota((ROWS, CB), 1)
    taps = jnp.concatenate([spread[0].astype(F32), jnp.zeros((KS, CB - KS), F32)], axis=1)
    taps = jnp.concatenate([pltpu.roll(taps, LIVE, 1), jnp.zeros((ROWS - KS, CB), F32)], axis=0)
    zeros = jnp.zeros((ROWS, CB), F32)
    padded = jnp.concatenate([zeros, volume[0], zeros], axis=1)
    for j in range(DEPTHS):
        start = CB - HALO + WIN * j
        low = start // CB * CB
        moved = pltpu.roll(padded[:, low : low + 2 * CB], 2 * CB - start % CB, 1)[:, :CB]
        windows[j] = jnp.where(lane < LIVE, moved, taps)


def lane_shift(x, b):
    shift = (RADIUS - b) % CB
    return pltpu.roll(x, shift, 1) if shift else x


def forward(ahead, source, sums, blocks):
    result = []
    for m in range(0, blocks, 2):
        pair = range(m, min(m + 2, blocks))
        right = jnp.concatenate([source[i * 256 : i * 256 + DEEP, :] for i in pair], axis=1)
        value = jnp.dot(ahead[...], right, preferred_element_type=F32)
        for i in pair:
            at = (i - m) * CB
            sums[i - m] = value[:, at : at + CB]
        for i in pair:
            total = lane_shift(sums[i - m, pl.ds(0, BLOCK, stride=16), :], 0)
            for b in range(1, KS):
                total = total + lane_shift(sums[i - m, pl.ds(b, BLOCK, stride=16), :], b)
            result.append(total)
    return result


def open_kernel(
    where, parts, measured,
    own, sensor, down, up, ahead, behind, scale, image,
    wide, rounded, sums,
):
    lane = iota((ROW, CB), 1)
    rounded[: NEAR * ROW, :] = jnp.zeros((NEAR * ROW, CB), BF16)
    rounded[(NEAR + ROWS) * ROW :, :] = jnp.zeros(((NEAR + 8) * ROW, CB), BF16)
    for r in range(ROWS):
        line = jnp.where(lane < LIVE, parts[pl.ds(r, ROW, stride=ROWS), :], 0.0)
        own[r * ROW : (r + 1) * ROW, :] = line
        line = line.astype(BF16)
        rounded[(NEAR + r) * ROW : (NEAR + r + 1) * ROW, :] = line
        if r < NEAR:
            up[r * ROW : (r + 1) * ROW, :] = line
        if r >= ROWS - NEAR:
            at = (r - ROWS + NEAR) * ROW
            down[at : at + ROW, :] = line
    zeros = jnp.zeros((ROWS, CB), F32)
    wide[:, :CB] = zeros
    wide[:, CB : CB + COLS] = measured[...]
    wide[:, CB + COLS :] = zeros
    start = CB - HALO + WIN * where[0]
    low = pl.multiple_of((start >> 7) * CB, CB)
    moved = pltpu.roll(wide[:, pl.ds(low, 2 * CB)], 2 * CB - (start & (CB - 1)), 1)[:, :CB]
    view = jnp.where(iota((ROWS, CB), 1) < LIVE, moved, 0.0)
    sensor[...] = view
    taps = jnp.concatenate([parts[pl.ds(a, ROW, stride=ROWS), :] for a in range(16)], axis=0)
    taps = jnp.where(iota((256, CB), 1) >= LIVE, taps, 0.0)
    first = jnp.transpose(taps)[LIVE:, :]
    first = jnp.concatenate([first, jnp.zeros((16, 256), F32)], axis=1)
    for i in range(BLOCK):
        moved = pltpu.roll(first, i * ROW, 1) if i else first
        ahead[i * 16 : (i + 1) * 16, :] = moved.astype(BF16)
    lane = iota((CB, DEEP), 1)
    hot = (iota((CB, DEEP), 0) == LIVE + KS - 1 - (lane >> 5)).astype(F32).astype(BF16)
    spread = jnp.dot(taps.astype(BF16), hot, preferred_element_type=F32)
    inside = iota((ROW, DEEP), 1)
    within = jnp.where(inside < KS * 32, inside & 31, 32)
    second = jnp.zeros((ROW, DEEP), F32)
    for a in range(KS):
        second = jnp.where(within == KS - 1 - a, spread[a * ROW : (a + 1) * ROW], second)
    for i in range(BLOCK):
        moved = pltpu.roll(second, i, 1) if i else second
        behind[i * ROW : (i + 1) * ROW, :] = moved.astype(BF16)
    total = taps[:ROW]
    for a in range(1, KS):
        total = total + taps[a * ROW : (a + 1) * ROW]
    norm = jnp.sum(total, axis=1, keepdims=True)
    scale[...] = jnp.broadcast_to(1.0 / norm, (ROW, CB))
    image[...] = jnp.concatenate(forward(ahead, rounded, sums, 3), axis=0)
    for out, part, lines in (
        (up, view[:HALO], image[:HALO, :]),
        (down, view[ROWS - HALO :], image[20 : 20 + HALO, :]),
    ):
        rows = []
        for x in (part, lines):
            high = x.astype(BF16).astype(F32)
            rows += [high, x - high]
        out[NEAR * ROW :, :] = jnp.concatenate(rows, axis=0).astype(BF16)


def iterate_kernel(
    own, left, right, sensor, image, ahead, behind, scale, codes,
    sent, flat, exact, second, light, whole, sums, ratio, stack,
):
    near = NEAR * ROW
    exact[:near, :] = left[:near].astype(F32)
    exact[near : near + ROWS * ROW, :] = own[...]
    exact[near + ROWS * ROW : 2 * near + ROWS * ROW, :] = right[:near].astype(F32)
    exact[2 * near + ROWS * ROW :, :] = jnp.zeros((8 * ROW, CB), F32)
    before, after = left[near:].astype(F32), right[near:].astype(F32)
    light[:HALO, :] = before[:HALO] + before[HALO : 2 * HALO]
    light[HALO : HALO + ROWS, :] = sensor[...]
    light[HALO + ROWS : 2 * HALO + ROWS, :] = after[:HALO] + after[HALO : 2 * HALO]
    light[2 * HALO + ROWS :, :] = jnp.zeros((16, CB), F32)
    blank = jnp.zeros((20, CB), F32)
    total = jnp.concatenate([blank[:12], image[...], blank], axis=0)
    above = jnp.concatenate([before[2 * HALO : 3 * HALO] + before[3 * HALO :], jnp.zeros((56, CB), F32)], axis=0)
    below = after[2 * HALO : 3 * HALO] + after[3 * HALO :]
    below = jnp.concatenate([jnp.zeros((44, CB), F32), below, blank[:12]], axis=0)
    whole[...] = total + above + below
    for m in range(2):
        stack[m * DEEP + KS * 32 : (m + 1) * DEEP, :] = jnp.zeros((DEEP - KS * 32, 2 * CB), BF16)
    tall = jnp.concatenate([scale[...]] * BLOCK, axis=0)

    def divide(total, offset, valid):
        rows = total.shape[0]
        seen = light[offset : offset + rows, :]
        inside = (iota((rows, CB), 0) < valid) & (seen != 0.0) & (total != 0.0)
        ratio[:rows, :] = jnp.where(inside, seen / jnp.where(inside, total, 1.0), 0.0)

    def spread_back(blocks):
        height = 16 * blocks + 16
        for b in range(KS):
            moved = lane_shift(ratio[:height, :], b).astype(BF16)
            for m in range(blocks):
                at = (m // 2) * DEEP + b * 32
                stack[at : at + 32, (m % 2) * CB : (m % 2 + 1) * CB] = moved[m * 16 : m * 16 + 32]

    def back(m):
        value = jnp.dot(behind[...], stack[m * DEEP : (m + 1) * DEEP, :], preferred_element_type=F32)
        return value[:, :CB] * tall, value[:, CB:] * tall

    divide(whole[...], 6, 68)
    spread_back(4)
    factors = back(0) + back(1)
    for m in range(4):
        value = exact[m * 256 : (m + 1) * 256, :] * factors[m]
        exact[m * 256 : (m + 1) * 256, :] = value
        second[m * 256 : (m + 1) * 256, :] = value.astype(BF16)
    divide(jnp.concatenate(forward(ahead, second, sums, 3), axis=0), 18, 44)
    spread_back(2)
    factors = back(0)
    done = [exact[(m * 16 + 12) * ROW : (m * 16 + 28) * ROW, :] * factors[m] for m in range(2)]
    lane = iota((256, CB), 1)
    packed = jnp.where(lane < WIN, pltpu.roll(done[0], CB - HALO, 1), pltpu.roll(done[1], WIN - HALO, 1))
    flat[...] = packed
    values = seed_values(codes[...], packed)
    for p in range(DEPTHS):
        sent[p, 0:16, :] = flat[pl.ds(p, 16, stride=ROW), :]
        sent[p, 16:24, :] = values


def more_kernel(turn, rank, code, flat, sent):
    codes = listed(rank[...], code[...], turn[0] * CAP)
    values = seed_values(codes, flat[...])
    for p in range(DEPTHS):
        sent[p] = values


def gather_kernel(at):
    def kernel(parts, out):
        total = parts[0, at : at + 8, :]
        for j in range(1, DEPTHS):
            total = total + parts[j, at : at + 8, :]
        line = jnp.concatenate([total[i : i + 1, :] for i in range(LANES)], axis=1)
        for j in range(TILES):
            out[j] = line

    return kernel


def looked(turn, parts, a_row, a_lane):
    table = jnp.concatenate([parts[t] for t in range(TILES)], axis=0)
    row = a_row[...] - turn * TILES
    hot = (iota((NAMES, TILES), 1) == row[:, :TILES]).astype(F32).astype(BF16)
    parts = split3(table)
    found = jnp.dot(hot, parts[0], preferred_element_type=F32)
    found = found + jnp.dot(hot, parts[1], preferred_element_type=F32)
    found = found + jnp.dot(hot, parts[2], preferred_element_type=F32)
    total = jnp.zeros((NAMES, CB), F32)
    for i in range(LANES):
        here = iota((NAMES, CB), 1) + i * CB == a_lane[...]
        total = total + jnp.where(here, found[:, i * CB : (i + 1) * CB], 0.0)
    return jnp.broadcast_to(lane_sum(total), (NAMES, CB))


def look_kernel(turn, parts, a_row, a_lane, known, out):
    out[...] = known[...] + looked(turn[0], parts, a_row, a_lane)


def home_kernel(parts, weights, b_col, estimate, proj, lines):
    lane = iota((16, CB), 1)
    for c in range(NCB):
        a, b = parts[2 * c, :16, :], parts[2 * c + 1, :16, :]
        top = jnp.where(lane < WIN, a, pltpu.roll(b, WIN, 1))
        bottom = jnp.where(lane < WIN, pltpu.roll(a, WIN, 1), b)
        estimate[:16, c * CB : (c + 1) * CB] = top
        estimate[16:, c * CB : (c + 1) * CB] = bottom
        lines[c * ROWS : c * ROWS + 16, :] = top
        lines[c * ROWS + 16 : (c + 1) * ROWS, :] = bottom
    blocks = [lines[pl.ds(br, 64, stride=4), :] for br in range(4)]
    blocked = jnp.concatenate(blocks, axis=1)
    number = b_col[:, :64]
    number = (number & 7) * 8 + (number >> 3)
    hot = (iota((SLOTS, 64), 1) == number).astype(F32).astype(BF16)
    high, low = split2(blocked)
    picked = jnp.dot(hot, high, preferred_element_type=F32) + jnp.dot(hot, low, preferred_element_type=F32)
    product = weights[...].astype(F32) * picked
    total = product[:, :CB]
    for br in range(1, 4):
        total = total + product[:, br * CB : (br + 1) * CB]
    proj[...] = jnp.broadcast_to(jnp.sum(total, axis=1, keepdims=True), (SLOTS, CB))


def slots_kernel(parts, a_row, a_lane, known, gram, q_row, q_col, proj, out, own):
    start = known[...] + looked(0, parts, a_row, a_lane)
    padded = jnp.concatenate([start, jnp.zeros((3 * CB - NAMES, CB), F32)], axis=0)
    row = jnp.transpose(padded)[0:1, :]
    own[...] = row[:, SLOTS:]
    start_row = row[:, :SLOTS]
    terms = gram[...] * start_row
    over = jnp.sum(terms[:, :CB] + terms[:, CB:], axis=1, keepdims=True)
    place = q_col[...]
    lane = iota((SLOTS, CB), 1)
    target = ((place >> 5) & 3) * 32 + (place & 15)
    sent = jnp.where(lane == target, proj[...], 0.0) + jnp.where(lane == target + 16, over, 0.0)
    spot = q_row[0:1, :]
    line = ((spot >> 9) * 2 + ((spot >> 4) & 1)) * 4 + ((spot >> 7) & 3)
    row_hot = (iota((CB, SLOTS), 0) == jnp.where(spot >= 0, line, -1)).astype(F32).astype(BF16)
    parts = split3(sent)
    dense = jnp.dot(row_hot, parts[0], preferred_element_type=F32)
    dense = dense + jnp.dot(row_hot, parts[1], preferred_element_type=F32)
    dense = dense + jnp.dot(row_hot, parts[2], preferred_element_type=F32)
    for j in range(TILES):
        out[j] = dense[j * 4 : (j + 1) * 4]


def fold_kernel(parts, out):
    total = parts[0]
    for j in range(1, TILES):
        total = total + parts[j]
    total = jnp.concatenate([total, total], axis=0)
    for m in range(4):
        moved = pltpu.roll(total, (CB - 32 * m) % CB, 1) if m else total
        for r in range(4):
            out[4 * r + m] = moved[r : r + 1]


def final_kernel(parts, own, out):
    total = parts[0]
    for j in range(1, TILES // 2):
        total = total + parts[j]
    over = pltpu.roll(total, CB - 16, 1)
    initial = own[...]
    real = iota((1, CB), 1) < 16
    bottom = jnp.where(real, over + 100.0 * initial, 1.0)
    out[...] = jnp.where(real, initial * total, 0.0) / bottom


def swap(pieces, axis, groups=None):
    return lax.all_to_all(pieces, axis, 0, 0, axis_index_groups=groups)


def body(
    volume,
    measured,
    point_spread,
    entry_block,
    entry_neuron,
    footprints,
    seed_plane,
    seed_row,
    seed_col,
    owner_slot,
):
    d = lax.axis_index("depth")
    t = lax.axis_index("tile")
    where = jnp.stack([d, t, (d * TILES + t) * 16]).astype(I32)
    [windows] = call(window_kernel, [((DEPTHS, ROWS, CB), F32)], 2)(volume, point_spread)
    windows, where = lax.optimization_barrier((windows, where))
    tied = (swap(windows, "depth"), where, measured, entry_block, entry_neuron, footprints, owner_slot)
    tied = lax.optimization_barrier(tied + (seed_plane, seed_row, seed_col))
    parts, where, measured, entry_block, entry_neuron, footprints, owner_slot = tied[:7]
    seed_plane, seed_row, seed_col = tied[7:]
    parts = parts.reshape(DEPTHS * ROWS, CB)
    table = owner_slot.reshape(64, CB)
    message = ((NEAR * ROW + 4 * HALO, CB), BF16)
    band = ((256, DEEP), BF16)
    own, sensor, down, up, ahead, behind, scale, image = call(
        open_kernel,
        [((ROWS * ROW, CB), F32), ((ROWS, CB), F32), message, message, band, band, ((ROW, CB), F32), ((48, CB), F32)],
        3,
        scalars=(0,),
        scratch=[
            pltpu.VMEM((ROWS, COLS + 2 * CB), F32),
            pltpu.VMEM((64 * ROW, CB), BF16),
            pltpu.VMEM((2, 256, CB), F32),
        ],
    )(where, parts, measured)
    left = lax.ppermute(down, "tile", [(i, i + 1) for i in range(TILES - 1)])
    right = lax.ppermute(up, "tile", [(i + 1, i) for i in range(TILES - 1)])
    weights = footprints[0].reshape(SLOTS, 512)
    column = ((SLOTS, CB), I32)
    names = ((NAMES, CB), I32)
    square = ((64, CB), I32)
    gram, q_row, q_col, b_col, a_row, a_lane, rank, code, first, most = call(
        prepare_kernel,
        [
            ((SLOTS, SLOTS), F32),
            ((8, SLOTS), I32),
            column,
            column,
            names,
            names,
            square,
            square,
            ((8, CB), I32),
            ((8, CB), I32),
        ],
        8,
        scalars=(0,),
    )(
        where,
        entry_block,
        entry_neuron,
        weights,
        table,
        seed_plane.reshape(64, CB),
        seed_row.reshape(64, CB),
        seed_col.reshape(64, CB),
    )
    sent, flat = call(
        iterate_kernel,
        [((DEPTHS, 24, CB), F32), ((256, CB), F32)],
        9,
        scratch=[
            pltpu.VMEM((64 * ROW, CB), F32),
            pltpu.VMEM((64 * ROW, CB), BF16),
            pltpu.VMEM((96, CB), F32),
            pltpu.VMEM((80, CB), F32),
            pltpu.VMEM((2, 256, CB), F32),
            pltpu.VMEM((80, CB), F32),
            pltpu.VMEM((2 * DEEP, 2 * CB), BF16),
        ],
    )(own, left, right, sensor, image, ahead, behind, scale, first)
    parts, most = lax.optimization_barrier((swap(sent, "depth"), most))

    def share(values, at):
        [values] = call(gather_kernel(at), [((TILES, 1, CAP), F32)], 1)(values)
        return swap(values, "tile")

    def look(turn, values, known):
        return call(look_kernel, [((NAMES, CB), F32)], 5, scalars=(0,))(
            turn, values, a_row, a_lane, known
        )[0]

    def another(step, known):
        turn = jnp.reshape(step, (1,))
        [values] = call(more_kernel, [((DEPTHS, 8, CB), F32)], 4, scalars=(0,))(
            turn, rank, code, flat
        )
        return look(turn, share(swap(values, "depth"), 0), known)

    rounds = (most[0, 0] + CAP - 1) // CAP
    shared, none = lax.optimization_barrier((share(parts, 16), jnp.zeros((NAMES, CB), F32)))
    known = lax.fori_loop(1, rounds, another, none)
    estimate, proj = call(
        home_kernel,
        [((ROWS, COLS), F32), ((SLOTS, CB), F32)],
        3,
        scratch=[pltpu.VMEM((NCB * ROWS, CB), F32)],
    )(parts, weights, b_col)
    sent, own = call(slots_kernel, [((TILES, 4, CB), F32), ((1, CB), F32)], 8)(
        shared, a_row, a_lane, known, gram, q_row, q_col, proj
    )
    pairs = TILES // 2
    near = [[d * TILES + 2 * z + x for d in range(DEPTHS) for x in range(2)] for z in range(pairs)]
    far = [[2 * z + x for z in range(pairs)] for x in range(2)]
    sent = swap(sent, ("depth", "tile"), near)
    [sent] = call(fold_kernel, [((pairs, 1, CB), F32)], 1)(sent)
    [demixed] = call(final_kernel, [((1, CB), F32)], 2)(swap(sent, "tile", far), own)
    return estimate[None], demixed[0, :16]


def solution(mesh):
    in_specs = (
        P("depth", "tile", None),
        P("tile", None),
        P("depth", None, None),
        P("tile", "depth"),
        P("tile", "depth"),
        P("tile", "depth", None, None),
        P(),
        P(),
        P(),
        P(),
    )
    out_specs = (P("depth", "tile", None), P(("depth", "tile")))
    return jax.shard_map(body, mesh=mesh, in_specs=in_specs, out_specs=out_specs, check_vma=False)
```

```python
import jax
import jax.numpy as jnp
from jax import lax
from jax.experimental import pallas as pl
from jax.experimental.pallas import tpu as pltpu
from jax.sharding import PartitionSpec as P

F32 = jnp.float32
BF16 = jnp.bfloat16
I32 = jnp.int32
KS = 13
RADIUS = 6
ROWS = 32
COLS = 1024
CB = 128
NCB = COLS // CB
DEPTHS = 16
TILES = 32
SLOTS = 256
NEURONS = 8192
HALO = 24
WIN = 64
LIVE = WIN + 2 * HALO
ROW = DEPTHS
BLOCK = 16
DEEP = 32 * ROW
CAP = 384
LANES = CAP // CB
NEAR = 12
NAMES = SLOTS + 16
VMEM = pl.BlockSpec(memory_space=pltpu.VMEM)
SMEM = pl.BlockSpec(memory_space=pltpu.SMEM)


def call(kernel, outs, n_in, scalars=(), scratch=(), mib=24):
    return pl.pallas_call(
        kernel,
        out_shape=[jax.ShapeDtypeStruct(s, t) for s, t in outs],
        in_specs=[SMEM if i in scalars else VMEM for i in range(n_in)],
        out_specs=[VMEM] * len(outs),
        scratch_shapes=list(scratch),
        compiler_params=pltpu.CompilerParams(vmem_limit_bytes=mib * 2**20),
    )


def iota(shape, dim):
    return lax.broadcasted_iota(I32, shape, dim)


def split2(x):
    high = x.astype(BF16)
    return high, (x - high.astype(F32)).astype(BF16)


def split3(x):
    high = x.astype(BF16)
    rest = x - high.astype(F32)
    mid = rest.astype(BF16)
    return high, mid, (rest - mid.astype(F32)).astype(BF16)


def column_of(row):
    n = row.shape[1]
    return jnp.transpose(jnp.broadcast_to(row, (CB, n)))


def lane_sum(x):
    return jnp.sum(x, axis=1, keepdims=True)


def prepare_kernel(
    where, block, neuron, weights, owner, s_row,
    gram, q_row, q_col, b_col, a_row, a_lane, most,
):
    foot = weights[...]
    product = lax.dot_general(foot, foot, (((1,), (1,)), ((), ())), preferred_element_type=F32)
    blocks = column_of(block[...].astype(F32))
    same = jnp.concatenate([blocks, blocks], axis=1) == block[...].astype(F32)
    gram[...] = jnp.where(same, product, 0.0)
    b_col[...] = blocks.astype(I32)
    table = owner[...]
    number = iota((64, CB), 0) * CB + iota((64, CB), 1)
    own = jnp.zeros((16, CB), F32)
    for i in range(16):
        hit = jnp.sum(jnp.where(table == where[2] + i, number.astype(F32), 0.0), axis=0, keepdims=True)
        own = jnp.where(iota((16, CB), 0) == i, lane_sum(hit), own)
    names = jnp.concatenate([column_of(neuron[...].astype(F32)), own], axis=0).astype(I32)
    tile = s_row[...] >> 5
    tables = [tile, table >> 7, table & 127]
    tables = jnp.concatenate([x.astype(F32) for x in tables], axis=1).astype(BF16)
    hot = (iota((NAMES, 64), 1) == (names[:, :64] >> 7)).astype(F32).astype(BF16)
    found = jnp.dot(hot, tables, preferred_element_type=F32)
    lane_hot = iota((NAMES, CB), 1) == (names & 127)
    picked = [lane_sum(jnp.where(lane_hot, found[:, i * CB : (i + 1) * CB], 0.0)) for i in range(3)]
    n_tile = picked[0].astype(I32)
    place = jnp.broadcast_to(picked[1] * 128.0 + picked[2], (NAMES, CB))[:SLOTS]
    place = jnp.where(names[:SLOTS] >= 0, place, -1.0)
    q_col[...] = place.astype(I32)
    q_row[...] = jnp.transpose(place)[0:8, :].astype(I32)
    both = jnp.zeros((TILES, 1), F32)
    for r in range(0, 64, 8):
        tiles = jnp.zeros((TILES, CB), F32)
        for i in range(r, r + 8):
            tiles = tiles + (iota((TILES, CB), 0) == tile[i : i + 1, :]).astype(F32)
        both = both + lane_sum(tiles)
    top = jnp.max(both, axis=0, keepdims=True)
    most[...] = jnp.broadcast_to(top, (8, CB)).astype(I32)
    wide = jnp.concatenate([both, jnp.zeros((CB - TILES, 1), F32)], axis=0)
    held = jnp.transpose(jnp.broadcast_to(wide, (CB, CB)))[0:1, :]
    earlier = lane_sum(jnp.where(iota((NAMES, CB), 1) < n_tile, held, 0.0))
    keys = tile * NEURONS + number
    high = jnp.broadcast_to(n_tile * NEURONS, (NAMES, CB)) + names
    count = jnp.zeros((NAMES, CB), F32)
    for r in range(64):
        count = count + jnp.where(keys[r : r + 1, :] < high, 1.0, 0.0)
    position = jnp.broadcast_to(lane_sum(count) - earlier, (NAMES, CB)).astype(I32)
    turn = jnp.zeros((NAMES, CB), I32)
    for i in range(1, (NEURONS + CAP - 1) // CAP):
        turn = turn + (position >= i * CAP).astype(I32)
    a_row[...] = jnp.where(names >= 0, turn * TILES + n_tile, -1)
    a_lane[...] = position - turn * CAP


def lists_kernel(where, s_plane, s_row, s_col, rank, code, first):
    row, col = s_row[...], s_col[...]
    tile, window = row >> 5, col >> 6
    local = tile == where[1]
    mask = local.astype(F32)
    before = (iota((CB, CB), 0) < iota((CB, CB), 1)).astype(F32).astype(BF16)
    inside = jnp.dot(mask.astype(BF16), before, preferred_element_type=F32)
    rows = jnp.broadcast_to(lane_sum(mask), (64, CB)).astype(BF16)
    above = (iota((64, 64), 1) < iota((64, 64), 0)).astype(F32).astype(BF16)
    inside = inside + jnp.dot(above, rows, preferred_element_type=F32)
    order = jnp.where(local & (window == where[0]), inside, -1.0).astype(I32)
    spot = ((row >> 4) & 1) * WIN + (col & (WIN - 1))
    coded = ((row & 15) * ROW + s_plane[...]) * CB + spot
    rank[...] = order
    code[...] = coded
    first[...] = listed(order, coded, 0)


def listed(order, coded, start):
    place = order - start
    place = jnp.where(place < CAP, place, -1)
    total = jnp.zeros((32, CB), F32)
    for r in range(0, 64, 8):
        lines = [place[i : i + 1, :] for i in range(r, r + 8)]
        codes = [coded[i : i + 1, :] for i in range(r, r + 8)]
        left = []
        for at, code in zip(lines, codes):
            here = iota((8, CB), 0) == (at >> 7)
            left.append(
                jnp.concatenate(
                    [
                        jnp.where(here, (code >> 7).astype(F32), 0.0),
                        jnp.where(here, (code & 127).astype(F32), 0.0),
                        jnp.where(here, 1.0, 0.0),
                        jnp.zeros((8, CB), F32),
                    ],
                    axis=0,
                )
            )
        left = jnp.concatenate(left, axis=1).astype(BF16)
        right = [(iota((CB, CB), 0) == jnp.where(at >= 0, at & 127, -1)).astype(F32) for at in lines]
        right = jnp.concatenate(right, axis=1).astype(BF16)
        total = total + lax.dot_general(
            left, right, (((1,), (1,)), ((), ())), preferred_element_type=F32
        )
    value = total[0:8] * 128.0 + total[8:16]
    return jnp.where(total[16:24] > 0.0, value, -1.0).astype(I32)


def seed_values(codes, flat):
    parts = split3(flat)
    result = []
    for i in range(LANES):
        index = column_of(codes[i : i + 1, :].astype(F32)).astype(I32)
        key = jnp.concatenate([index, index], axis=1) >> 7
        hot = (iota((CB, 256), 1) == key).astype(F32).astype(BF16)
        found = jnp.dot(hot, parts[0], preferred_element_type=F32)
        found = found + jnp.dot(hot, parts[1], preferred_element_type=F32)
        found = found + jnp.dot(hot, parts[2], preferred_element_type=F32)
        picked = jnp.where(iota((CB, CB), 1) == (index & (CB - 1)), found, 0.0)
        result.append(jnp.sum(jnp.transpose(picked), axis=0, keepdims=True))
    result.append(jnp.zeros((8 - LANES, CB), F32))
    return jnp.concatenate(result, axis=0)


def window_kernel(volume, spread, windows):
    lane = iota((ROWS, CB), 1)
    taps = jnp.concatenate([spread[0].astype(F32), jnp.zeros((KS, CB - KS), F32)], axis=1)
    taps = jnp.concatenate([pltpu.roll(taps, LIVE, 1), jnp.zeros((ROWS - KS, CB), F32)], axis=0)
    zeros = jnp.zeros((ROWS, CB), F32)
    padded = jnp.concatenate([zeros, volume[0], zeros], axis=1)
    for j in range(DEPTHS):
        start = CB - HALO + WIN * j
        low = start // CB * CB
        moved = pltpu.roll(padded[:, low : low + 2 * CB], 2 * CB - start % CB, 1)[:, :CB]
        windows[j] = jnp.where(lane < LIVE, moved, taps)


def lane_shift(x, b):
    shift = (RADIUS - b) % CB
    return pltpu.roll(x, shift, 1) if shift else x


def forward(ahead, source, sums, blocks):
    result = []
    for m in range(0, blocks, 2):
        pair = range(m, min(m + 2, blocks))
        right = jnp.concatenate([source[i * 256 : i * 256 + DEEP, :] for i in pair], axis=1)
        value = jnp.dot(ahead[...], right, preferred_element_type=F32)
        for i in pair:
            at = (i - m) * CB
            sums[i - m] = value[:, at : at + CB]
        for i in pair:
            total = lane_shift(sums[i - m, pl.ds(0, BLOCK, stride=16), :], 0)
            for b in range(1, KS):
                total = total + lane_shift(sums[i - m, pl.ds(b, BLOCK, stride=16), :], b)
            result.append(total)
    return result


def open_kernel(
    where, parts, measured,
    own, sensor, down, up, ahead, behind, scale, image,
    wide, rounded, sums,
):
    lane = iota((ROW, CB), 1)
    rounded[: NEAR * ROW, :] = jnp.zeros((NEAR * ROW, CB), BF16)
    rounded[(NEAR + ROWS) * ROW :, :] = jnp.zeros(((NEAR + 8) * ROW, CB), BF16)
    for r in range(ROWS):
        line = jnp.where(lane < LIVE, parts[pl.ds(r, ROW, stride=ROWS), :], 0.0)
        own[r * ROW : (r + 1) * ROW, :] = line
        line = line.astype(BF16)
        rounded[(NEAR + r) * ROW : (NEAR + r + 1) * ROW, :] = line
        if r < NEAR:
            up[r * ROW : (r + 1) * ROW, :] = line
        if r >= ROWS - NEAR:
            at = (r - ROWS + NEAR) * ROW
            down[at : at + ROW, :] = line
    zeros = jnp.zeros((ROWS, CB), F32)
    wide[:, :CB] = zeros
    wide[:, CB : CB + COLS] = measured[...]
    wide[:, CB + COLS :] = zeros
    start = CB - HALO + WIN * where[0]
    low = pl.multiple_of((start >> 7) * CB, CB)
    moved = pltpu.roll(wide[:, pl.ds(low, 2 * CB)], 2 * CB - (start & (CB - 1)), 1)[:, :CB]
    view = jnp.where(iota((ROWS, CB), 1) < LIVE, moved, 0.0)
    sensor[...] = view
    taps = jnp.concatenate([parts[pl.ds(a, ROW, stride=ROWS), :] for a in range(16)], axis=0)
    taps = jnp.where(iota((256, CB), 1) >= LIVE, taps, 0.0)
    first = jnp.transpose(taps)[LIVE:, :]
    first = jnp.concatenate([first, jnp.zeros((16, 256), F32)], axis=1)
    for i in range(BLOCK):
        moved = pltpu.roll(first, i * ROW, 1) if i else first
        ahead[i * 16 : (i + 1) * 16, :] = moved.astype(BF16)
    lane = iota((CB, DEEP), 1)
    hot = (iota((CB, DEEP), 0) == LIVE + KS - 1 - (lane >> 5)).astype(F32).astype(BF16)
    spread = jnp.dot(taps.astype(BF16), hot, preferred_element_type=F32)
    inside = iota((ROW, DEEP), 1)
    within = jnp.where(inside < KS * 32, inside & 31, 32)
    second = jnp.zeros((ROW, DEEP), F32)
    for a in range(KS):
        second = jnp.where(within == KS - 1 - a, spread[a * ROW : (a + 1) * ROW], second)
    for i in range(BLOCK):
        moved = pltpu.roll(second, i, 1) if i else second
        behind[i * ROW : (i + 1) * ROW, :] = moved.astype(BF16)
    total = taps[:ROW]
    for a in range(1, KS):
        total = total + taps[a * ROW : (a + 1) * ROW]
    norm = jnp.sum(total, axis=1, keepdims=True)
    scale[...] = jnp.broadcast_to(1.0 / norm, (ROW, CB))
    image[...] = jnp.concatenate(forward(ahead, rounded, sums, 3), axis=0)
    for out, part, lines in (
        (up, view[:HALO], image[:HALO, :]),
        (down, view[ROWS - HALO :], image[20 : 20 + HALO, :]),
    ):
        rows = []
        for x in (part, lines):
            high = x.astype(BF16).astype(F32)
            rows += [high, x - high]
        out[NEAR * ROW :, :] = jnp.concatenate(rows, axis=0).astype(BF16)


def iterate_kernel(
    own, left, right, sensor, image, ahead, behind, scale, codes,
    sent, flat, exact, second, light, whole, sums, ratio, stack,
):
    near = NEAR * ROW
    exact[:near, :] = left[:near].astype(F32)
    exact[near : near + ROWS * ROW, :] = own[...]
    exact[near + ROWS * ROW : 2 * near + ROWS * ROW, :] = right[:near].astype(F32)
    exact[2 * near + ROWS * ROW :, :] = jnp.zeros((8 * ROW, CB), F32)
    before, after = left[near:].astype(F32), right[near:].astype(F32)
    light[:HALO, :] = before[:HALO] + before[HALO : 2 * HALO]
    light[HALO : HALO + ROWS, :] = sensor[...]
    light[HALO + ROWS : 2 * HALO + ROWS, :] = after[:HALO] + after[HALO : 2 * HALO]
    light[2 * HALO + ROWS :, :] = jnp.zeros((16, CB), F32)
    blank = jnp.zeros((20, CB), F32)
    total = jnp.concatenate([blank[:12], image[...], blank], axis=0)
    above = jnp.concatenate([before[2 * HALO : 3 * HALO] + before[3 * HALO :], jnp.zeros((56, CB), F32)], axis=0)
    below = after[2 * HALO : 3 * HALO] + after[3 * HALO :]
    below = jnp.concatenate([jnp.zeros((44, CB), F32), below, blank[:12]], axis=0)
    whole[...] = total + above + below
    for m in range(2):
        stack[m * DEEP + KS * 32 : (m + 1) * DEEP, :] = jnp.zeros((DEEP - KS * 32, 2 * CB), BF16)
    tall = jnp.concatenate([scale[...]] * BLOCK, axis=0)

    def divide(total, offset, valid):
        rows = total.shape[0]
        seen = light[offset : offset + rows, :]
        inside = (iota((rows, CB), 0) < valid) & (seen != 0.0) & (total != 0.0)
        ratio[:rows, :] = jnp.where(inside, seen / jnp.where(inside, total, 1.0), 0.0)

    def spread_back(blocks):
        height = 16 * blocks + 16
        for b in range(KS):
            moved = lane_shift(ratio[:height, :], b).astype(BF16)
            for m in range(blocks):
                at = (m // 2) * DEEP + b * 32
                stack[at : at + 32, (m % 2) * CB : (m % 2 + 1) * CB] = moved[m * 16 : m * 16 + 32]

    def back(m):
        value = jnp.dot(behind[...], stack[m * DEEP : (m + 1) * DEEP, :], preferred_element_type=F32)
        return value[:, :CB] * tall, value[:, CB:] * tall

    divide(whole[...], 6, 68)
    spread_back(4)
    factors = back(0) + back(1)
    for m in range(4):
        value = exact[m * 256 : (m + 1) * 256, :] * factors[m]
        exact[m * 256 : (m + 1) * 256, :] = value
        second[m * 256 : (m + 1) * 256, :] = value.astype(BF16)
    divide(jnp.concatenate(forward(ahead, second, sums, 3), axis=0), 18, 44)
    spread_back(2)
    factors = back(0)
    done = [exact[(m * 16 + 12) * ROW : (m * 16 + 28) * ROW, :] * factors[m] for m in range(2)]
    lane = iota((256, CB), 1)
    packed = jnp.where(lane < WIN, pltpu.roll(done[0], CB - HALO, 1), pltpu.roll(done[1], WIN - HALO, 1))
    flat[...] = packed
    values = seed_values(codes[...], packed)
    for p in range(DEPTHS):
        sent[p, 0:16, :] = flat[pl.ds(p, 16, stride=ROW), :]
        sent[p, 16:24, :] = values


def more_kernel(turn, rank, code, flat, sent):
    codes = listed(rank[...], code[...], turn[0] * CAP)
    values = seed_values(codes, flat[...])
    for p in range(DEPTHS):
        sent[p] = values


def gather_kernel(at):
    def kernel(parts, out):
        total = parts[0, at : at + 8, :]
        for j in range(1, DEPTHS):
            total = total + parts[j, at : at + 8, :]
        line = jnp.concatenate([total[i : i + 1, :] for i in range(LANES)], axis=1)
        for j in range(TILES):
            out[j] = line

    return kernel


def looked(turn, parts, a_row, a_lane):
    table = jnp.concatenate([parts[t] for t in range(TILES)], axis=0)
    row = a_row[...] - turn * TILES
    hot = (iota((NAMES, TILES), 1) == row[:, :TILES]).astype(F32).astype(BF16)
    parts = split3(table)
    found = jnp.dot(hot, parts[0], preferred_element_type=F32)
    found = found + jnp.dot(hot, parts[1], preferred_element_type=F32)
    found = found + jnp.dot(hot, parts[2], preferred_element_type=F32)
    total = jnp.zeros((NAMES, CB), F32)
    for i in range(LANES):
        here = iota((NAMES, CB), 1) + i * CB == a_lane[...]
        total = total + jnp.where(here, found[:, i * CB : (i + 1) * CB], 0.0)
    return jnp.broadcast_to(lane_sum(total), (NAMES, CB))


def look_kernel(turn, parts, a_row, a_lane, known, out):
    out[...] = known[...] + looked(turn[0], parts, a_row, a_lane)


def home_kernel(parts, weights, b_col, estimate, proj, lines):
    lane = iota((16, CB), 1)
    for c in range(NCB):
        a, b = parts[2 * c, :16, :], parts[2 * c + 1, :16, :]
        top = jnp.where(lane < WIN, a, pltpu.roll(b, WIN, 1))
        bottom = jnp.where(lane < WIN, pltpu.roll(a, WIN, 1), b)
        estimate[:16, c * CB : (c + 1) * CB] = top
        estimate[16:, c * CB : (c + 1) * CB] = bottom
        lines[c * ROWS : c * ROWS + 16, :] = top
        lines[c * ROWS + 16 : (c + 1) * ROWS, :] = bottom
    blocks = [lines[pl.ds(br, 64, stride=4), :] for br in range(4)]
    blocked = jnp.concatenate(blocks, axis=1)
    number = b_col[:, :64]
    number = (number & 7) * 8 + (number >> 3)
    hot = (iota((SLOTS, 64), 1) == number).astype(F32).astype(BF16)
    high, low = split2(blocked)
    picked = jnp.dot(hot, high, preferred_element_type=F32) + jnp.dot(hot, low, preferred_element_type=F32)
    product = weights[...].astype(F32) * picked
    total = product[:, :CB]
    for br in range(1, 4):
        total = total + product[:, br * CB : (br + 1) * CB]
    proj[...] = jnp.broadcast_to(jnp.sum(total, axis=1, keepdims=True), (SLOTS, CB))


def slots_kernel(parts, a_row, a_lane, known, gram, q_row, q_col, proj, out, own):
    start = known[...] + looked(0, parts, a_row, a_lane)
    padded = jnp.concatenate([start, jnp.zeros((3 * CB - NAMES, CB), F32)], axis=0)
    row = jnp.transpose(padded)[0:1, :]
    own[...] = row[:, SLOTS:]
    start_row = row[:, :SLOTS]
    terms = gram[...] * start_row
    over = jnp.sum(terms[:, :CB] + terms[:, CB:], axis=1, keepdims=True)
    place = q_col[...]
    lane = iota((SLOTS, CB), 1)
    target = ((place >> 5) & 3) * 32 + (place & 15)
    sent = jnp.where(lane == target, proj[...], 0.0) + jnp.where(lane == target + 16, over, 0.0)
    spot = q_row[0:1, :]
    line = ((spot >> 9) * 2 + ((spot >> 4) & 1)) * 4 + ((spot >> 7) & 3)
    row_hot = (iota((CB, SLOTS), 0) == jnp.where(spot >= 0, line, -1)).astype(F32).astype(BF16)
    parts = split3(sent)
    dense = jnp.dot(row_hot, parts[0], preferred_element_type=F32)
    dense = dense + jnp.dot(row_hot, parts[1], preferred_element_type=F32)
    dense = dense + jnp.dot(row_hot, parts[2], preferred_element_type=F32)
    for j in range(TILES):
        out[j] = dense[j * 4 : (j + 1) * 4]


def fold_kernel(parts, out):
    total = parts[0]
    for j in range(1, TILES):
        total = total + parts[j]
    total = jnp.concatenate([total, total], axis=0)
    for m in range(4):
        moved = pltpu.roll(total, (CB - 32 * m) % CB, 1) if m else total
        for r in range(4):
            out[4 * r + m] = moved[r : r + 1]


def final_kernel(parts, own, out):
    total = parts[0]
    for j in range(1, TILES // 2):
        total = total + parts[j]
    over = pltpu.roll(total, CB - 16, 1)
    initial = own[...]
    real = iota((1, CB), 1) < 16
    bottom = jnp.where(real, over + 100.0 * initial, 1.0)
    out[...] = jnp.where(real, initial * total, 0.0) / bottom


def swap(pieces, axis, groups=None):
    return lax.all_to_all(pieces, axis, 0, 0, axis_index_groups=groups)


def body(
    volume,
    measured,
    point_spread,
    entry_block,
    entry_neuron,
    footprints,
    seed_plane,
    seed_row,
    seed_col,
    owner_slot,
):
    d = lax.axis_index("depth")
    t = lax.axis_index("tile")
    where = jnp.stack([d, t, (d * TILES + t) * 16]).astype(I32)
    [windows] = call(window_kernel, [((DEPTHS, ROWS, CB), F32)], 2)(volume, point_spread)
    windows, where = lax.optimization_barrier((windows, where))
    tied = (swap(windows, "depth"), where, measured, entry_block, entry_neuron, footprints, owner_slot)
    tied = lax.optimization_barrier(tied + (seed_plane, seed_row, seed_col))
    parts, where, measured, entry_block, entry_neuron, footprints, owner_slot = tied[:7]
    seed_plane, seed_row, seed_col = tied[7:]
    parts = parts.reshape(DEPTHS * ROWS, CB)
    table = owner_slot.reshape(64, CB)
    message = ((NEAR * ROW + 4 * HALO, CB), BF16)
    band = ((256, DEEP), BF16)
    own, sensor, down, up, ahead, behind, scale, image = call(
        open_kernel,
        [((ROWS * ROW, CB), F32), ((ROWS, CB), F32), message, message, band, band, ((ROW, CB), F32), ((48, CB), F32)],
        3,
        scalars=(0,),
        scratch=[
            pltpu.VMEM((ROWS, COLS + 2 * CB), F32),
            pltpu.VMEM((64 * ROW, CB), BF16),
            pltpu.VMEM((2, 256, CB), F32),
        ],
    )(where, parts, measured)
    left = lax.ppermute(down, "tile", [(i, i + 1) for i in range(TILES - 1)])
    right = lax.ppermute(up, "tile", [(i + 1, i) for i in range(TILES - 1)])
    lines = [x.reshape(64, CB) for x in (seed_plane, seed_row, seed_col)]
    square = ((64, CB), I32)
    rank, code, first = call(lists_kernel, [square, square, ((8, CB), I32)], 4, scalars=(0,))(where, *lines)
    sent, flat = call(
        iterate_kernel,
        [((DEPTHS, 24, CB), F32), ((256, CB), F32)],
        9,
        scratch=[
            pltpu.VMEM((64 * ROW, CB), F32),
            pltpu.VMEM((64 * ROW, CB), BF16),
            pltpu.VMEM((96, CB), F32),
            pltpu.VMEM((80, CB), F32),
            pltpu.VMEM((2, 256, CB), F32),
            pltpu.VMEM((80, CB), F32),
            pltpu.VMEM((2 * DEEP, 2 * CB), BF16),
        ],
    )(own, left, right, sensor, image, ahead, behind, scale, first)
    later = (swap(sent, "depth"), entry_block, entry_neuron, table, lines[1])
    parts, entry_block, entry_neuron, table, seed_rows = lax.optimization_barrier(later)
    weights = footprints[0].reshape(SLOTS, 512)
    column = ((SLOTS, CB), I32)
    names = ((NAMES, CB), I32)
    gram, q_row, q_col, b_col, a_row, a_lane, most = call(
        prepare_kernel,
        [((SLOTS, SLOTS), F32), ((8, SLOTS), I32), column, column, names, names, ((8, CB), I32)],
        6,
        scalars=(0,),
    )(where, entry_block, entry_neuron, weights, table, seed_rows)

    def share(values, at):
        [values] = call(gather_kernel(at), [((TILES, 1, CAP), F32)], 1)(values)
        return swap(values, "tile")

    def look(turn, values, known):
        return call(look_kernel, [((NAMES, CB), F32)], 5, scalars=(0,))(
            turn, values, a_row, a_lane, known
        )[0]

    def another(step, known):
        turn = jnp.reshape(step, (1,))
        [values] = call(more_kernel, [((DEPTHS, 8, CB), F32)], 4, scalars=(0,))(
            turn, rank, code, flat
        )
        return look(turn, share(swap(values, "depth"), 0), known)

    rounds = (most[0, 0] + CAP - 1) // CAP
    shared, none = lax.optimization_barrier((share(parts, 16), jnp.zeros((NAMES, CB), F32)))
    known = lax.fori_loop(1, rounds, another, none)
    estimate, proj = call(
        home_kernel,
        [((ROWS, COLS), F32), ((SLOTS, CB), F32)],
        3,
        scratch=[pltpu.VMEM((NCB * ROWS, CB), F32)],
    )(parts, weights, b_col)
    sent, own = call(slots_kernel, [((TILES, 4, CB), F32), ((1, CB), F32)], 8)(
        shared, a_row, a_lane, known, gram, q_row, q_col, proj
    )
    pairs = TILES // 2
    near = [[d * TILES + 2 * z + x for d in range(DEPTHS) for x in range(2)] for z in range(pairs)]
    far = [[2 * z + x for z in range(pairs)] for x in range(2)]
    sent = swap(sent, ("depth", "tile"), near)
    [sent] = call(fold_kernel, [((pairs, 1, CB), F32)], 1)(sent)
    [demixed] = call(final_kernel, [((1, CB), F32)], 2)(swap(sent, "tile", far), own)
    return estimate[None], demixed[0, :16]


def solution(mesh):
    in_specs = (
        P("depth", "tile", None),
        P("tile", None),
        P("depth", None, None),
        P("tile", "depth"),
        P("tile", "depth"),
        P("tile", "depth", None, None),
        P(),
        P(),
        P(),
        P(),
    )
    out_specs = (P("depth", "tile", None), P(("depth", "tile")))
    return jax.shard_map(body, mesh=mesh, in_specs=in_specs, out_specs=out_specs, check_vma=False)
```

```python
import jax
import jax.numpy as jnp
from jax import lax
from jax.experimental import pallas as pl
from jax.experimental.pallas import tpu as pltpu
from jax.sharding import PartitionSpec as P

F32 = jnp.float32
BF16 = jnp.bfloat16
I32 = jnp.int32
KS = 13
RADIUS = 6
ROWS = 32
COLS = 1024
CB = 128
NCB = COLS // CB
DEPTHS = 16
TILES = 32
SLOTS = 256
NEURONS = 8192
HALO = 24
WIN = 64
LIVE = WIN + 2 * HALO
ROW = DEPTHS
BLOCK = 16
DEEP = 32 * ROW
CAP = 384
LANES = CAP // CB
NEAR = 12
NAMES = SLOTS + 16
VMEM = pl.BlockSpec(memory_space=pltpu.VMEM)
SMEM = pl.BlockSpec(memory_space=pltpu.SMEM)


def call(kernel, outs, n_in, scalars=(), scratch=(), mib=24):
    return pl.pallas_call(
        kernel,
        out_shape=[jax.ShapeDtypeStruct(s, t) for s, t in outs],
        in_specs=[SMEM if i in scalars else VMEM for i in range(n_in)],
        out_specs=[VMEM] * len(outs),
        scratch_shapes=list(scratch),
        compiler_params=pltpu.CompilerParams(vmem_limit_bytes=mib * 2**20),
    )


def iota(shape, dim):
    return lax.broadcasted_iota(I32, shape, dim)


def split2(x):
    high = x.astype(BF16)
    return high, (x - high.astype(F32)).astype(BF16)


def split3(x):
    high = x.astype(BF16)
    rest = x - high.astype(F32)
    mid = rest.astype(BF16)
    return high, mid, (rest - mid.astype(F32)).astype(BF16)


def column_of(row):
    n = row.shape[1]
    return jnp.transpose(jnp.broadcast_to(row, (CB, n)))


def lane_sum(x):
    return jnp.sum(x, axis=1, keepdims=True)


def prepare_kernel(
    where, block, neuron, weights, owner, s_row,
    gram, q_row, q_col, b_col, a_row, a_lane, most,
):
    foot = weights[...]
    product = lax.dot_general(foot, foot, (((1,), (1,)), ((), ())), preferred_element_type=F32)
    blocks = column_of(block[...].astype(F32))
    same = jnp.concatenate([blocks, blocks], axis=1) == block[...].astype(F32)
    gram[...] = jnp.where(same, product, 0.0)
    b_col[...] = blocks.astype(I32)
    table = owner[...]
    number = iota((64, CB), 0) * CB + iota((64, CB), 1)
    own = jnp.zeros((16, CB), F32)
    for i in range(16):
        hit = jnp.sum(jnp.where(table == where[2] + i, number.astype(F32), 0.0), axis=0, keepdims=True)
        own = jnp.where(iota((16, CB), 0) == i, lane_sum(hit), own)
    names = jnp.concatenate([column_of(neuron[...].astype(F32)), own], axis=0).astype(I32)
    tile = s_row[...] >> 5
    tables = [tile, table >> 7, table & 127]
    tables = jnp.concatenate([x.astype(F32) for x in tables], axis=1).astype(BF16)
    hot = (iota((NAMES, 64), 1) == (names[:, :64] >> 7)).astype(F32).astype(BF16)
    found = jnp.dot(hot, tables, preferred_element_type=F32)
    lane_hot = iota((NAMES, CB), 1) == (names & 127)
    picked = [lane_sum(jnp.where(lane_hot, found[:, i * CB : (i + 1) * CB], 0.0)) for i in range(3)]
    n_tile = picked[0].astype(I32)
    place = jnp.broadcast_to(picked[1] * 128.0 + picked[2], (NAMES, CB))[:SLOTS]
    place = jnp.where(names[:SLOTS] >= 0, place, -1.0)
    q_col[...] = place.astype(I32)
    q_row[...] = jnp.transpose(place)[0:8, :].astype(I32)
    held = jnp.zeros((TILES, CB), F32)
    for r in range(64):
        here = lane_sum((iota((TILES, CB), 0) == tile[r : r + 1, :]).astype(F32))
        held = jnp.where(iota((TILES, CB), 1) == r, here, held)
    top = jnp.max(lane_sum(held), axis=0, keepdims=True)
    most[...] = jnp.broadcast_to(top, (8, CB)).astype(I32)
    before = (iota((CB, CB), 0) < iota((CB, CB), 1)).astype(F32).astype(BF16)
    earlier = jnp.dot(held.astype(BF16), before, preferred_element_type=F32)
    row_hot = (iota((NAMES, CB), 1) == (names >> 7)).astype(F32).astype(BF16)
    counts = jnp.zeros((NAMES, TILES), F32)
    for part in split2(earlier):
        counts = counts + lax.dot_general(
            row_hot, part, (((1,), (1,)), ((), ())), preferred_element_type=F32
        )
    count = lane_sum(jnp.where(iota((NAMES, TILES), 1) == n_tile, counts, 0.0))
    inside = (found[:, :CB] == picked[0]) & (iota((NAMES, CB), 1) < (names & 127))
    count = count + lane_sum(jnp.where(inside, 1.0, 0.0))
    position = jnp.broadcast_to(count, (NAMES, CB)).astype(I32)
    turn = jnp.zeros((NAMES, CB), I32)
    for i in range(1, (NEURONS + CAP - 1) // CAP):
        turn = turn + (position >= i * CAP).astype(I32)
    a_row[...] = jnp.where(names >= 0, turn * TILES + n_tile, -1)
    a_lane[...] = position - turn * CAP


def lists_kernel(where, s_plane, s_row, s_col, rank, code, first):
    row, col = s_row[...], s_col[...]
    tile, window = row >> 5, col >> 6
    local = tile == where[1]
    mask = local.astype(F32)
    before = (iota((CB, CB), 0) < iota((CB, CB), 1)).astype(F32).astype(BF16)
    inside = jnp.dot(mask.astype(BF16), before, preferred_element_type=F32)
    rows = jnp.broadcast_to(lane_sum(mask), (64, CB)).astype(BF16)
    above = (iota((64, 64), 1) < iota((64, 64), 0)).astype(F32).astype(BF16)
    inside = inside + jnp.dot(above, rows, preferred_element_type=F32)
    order = jnp.where(local & (window == where[0]), inside, -1.0).astype(I32)
    spot = ((row >> 4) & 1) * WIN + (col & (WIN - 1))
    coded = ((row & 15) * ROW + s_plane[...]) * CB + spot
    rank[...] = order
    code[...] = coded
    first[...] = listed(order, coded, 0)


def listed(order, coded, start):
    place = order - start
    place = jnp.where(place < CAP, place, -1)
    total = jnp.zeros((32, CB), F32)
    for r in range(0, 64, 8):
        lines = [place[i : i + 1, :] for i in range(r, r + 8)]
        codes = [coded[i : i + 1, :] for i in range(r, r + 8)]
        left = []
        for at, code in zip(lines, codes):
            here = iota((8, CB), 0) == (at >> 7)
            left.append(
                jnp.concatenate(
                    [
                        jnp.where(here, (code >> 7).astype(F32), 0.0),
                        jnp.where(here, (code & 127).astype(F32), 0.0),
                        jnp.where(here, 1.0, 0.0),
                        jnp.zeros((8, CB), F32),
                    ],
                    axis=0,
                )
            )
        left = jnp.concatenate(left, axis=1).astype(BF16)
        right = [(iota((CB, CB), 0) == jnp.where(at >= 0, at & 127, -1)).astype(F32) for at in lines]
        right = jnp.concatenate(right, axis=1).astype(BF16)
        total = total + lax.dot_general(
            left, right, (((1,), (1,)), ((), ())), preferred_element_type=F32
        )
    value = total[0:8] * 128.0 + total[8:16]
    return jnp.where(total[16:24] > 0.0, value, -1.0).astype(I32)


def seed_values(codes, flat):
    parts = split3(flat)
    result = []
    for i in range(LANES):
        index = column_of(codes[i : i + 1, :].astype(F32)).astype(I32)
        key = jnp.concatenate([index, index], axis=1) >> 7
        hot = (iota((CB, 256), 1) == key).astype(F32).astype(BF16)
        found = jnp.dot(hot, parts[0], preferred_element_type=F32)
        found = found + jnp.dot(hot, parts[1], preferred_element_type=F32)
        found = found + jnp.dot(hot, parts[2], preferred_element_type=F32)
        picked = jnp.where(iota((CB, CB), 1) == (index & (CB - 1)), found, 0.0)
        result.append(jnp.sum(jnp.transpose(picked), axis=0, keepdims=True))
    result.append(jnp.zeros((8 - LANES, CB), F32))
    return jnp.concatenate(result, axis=0)


def window_kernel(volume, spread, windows):
    lane = iota((ROWS, CB), 1)
    taps = jnp.concatenate([spread[0].astype(F32), jnp.zeros((KS, CB - KS), F32)], axis=1)
    taps = jnp.concatenate([pltpu.roll(taps, LIVE, 1), jnp.zeros((ROWS - KS, CB), F32)], axis=0)
    zeros = jnp.zeros((ROWS, CB), F32)
    padded = jnp.concatenate([zeros, volume[0], zeros], axis=1)
    for j in range(DEPTHS):
        start = CB - HALO + WIN * j
        low = start // CB * CB
        moved = pltpu.roll(padded[:, low : low + 2 * CB], 2 * CB - start % CB, 1)[:, :CB]
        windows[j] = jnp.where(lane < LIVE, moved, taps)


def lane_shift(x, b):
    shift = (RADIUS - b) % CB
    return pltpu.roll(x, shift, 1) if shift else x


def forward(ahead, source, sums, blocks):
    result = []
    for m in range(0, blocks, 2):
        pair = range(m, min(m + 2, blocks))
        right = jnp.concatenate([source[i * 256 : i * 256 + DEEP, :] for i in pair], axis=1)
        value = jnp.dot(ahead[...], right, preferred_element_type=F32)
        for i in pair:
            at = (i - m) * CB
            sums[i - m] = value[:, at : at + CB]
        for i in pair:
            total = lane_shift(sums[i - m, pl.ds(0, BLOCK, stride=16), :], 0)
            for b in range(1, KS):
                total = total + lane_shift(sums[i - m, pl.ds(b, BLOCK, stride=16), :], b)
            result.append(total)
    return result


def open_kernel(
    where, parts, measured,
    own, sensor, down, up, ahead, behind, scale, image,
    wide, rounded, sums,
):
    lane = iota((ROW, CB), 1)
    rounded[: NEAR * ROW, :] = jnp.zeros((NEAR * ROW, CB), BF16)
    rounded[(NEAR + ROWS) * ROW :, :] = jnp.zeros(((NEAR + 8) * ROW, CB), BF16)
    for r in range(ROWS):
        line = jnp.where(lane < LIVE, parts[pl.ds(r, ROW, stride=ROWS), :], 0.0)
        own[r * ROW : (r + 1) * ROW, :] = line
        line = line.astype(BF16)
        rounded[(NEAR + r) * ROW : (NEAR + r + 1) * ROW, :] = line
        if r < NEAR:
            up[r * ROW : (r + 1) * ROW, :] = line
        if r >= ROWS - NEAR:
            at = (r - ROWS + NEAR) * ROW
            down[at : at + ROW, :] = line
    zeros = jnp.zeros((ROWS, CB), F32)
    wide[:, :CB] = zeros
    wide[:, CB : CB + COLS] = measured[...]
    wide[:, CB + COLS :] = zeros
    start = CB - HALO + WIN * where[0]
    low = pl.multiple_of((start >> 7) * CB, CB)
    moved = pltpu.roll(wide[:, pl.ds(low, 2 * CB)], 2 * CB - (start & (CB - 1)), 1)[:, :CB]
    view = jnp.where(iota((ROWS, CB), 1) < LIVE, moved, 0.0)
    sensor[...] = view
    taps = jnp.concatenate([parts[pl.ds(a, ROW, stride=ROWS), :] for a in range(16)], axis=0)
    taps = jnp.where(iota((256, CB), 1) >= LIVE, taps, 0.0)
    first = jnp.transpose(taps)[LIVE:, :]
    first = jnp.concatenate([first, jnp.zeros((16, 256), F32)], axis=1)
    for i in range(BLOCK):
        moved = pltpu.roll(first, i * ROW, 1) if i else first
        ahead[i * 16 : (i + 1) * 16, :] = moved.astype(BF16)
    lane = iota((CB, DEEP), 1)
    hot = (iota((CB, DEEP), 0) == LIVE + KS - 1 - (lane >> 5)).astype(F32).astype(BF16)
    spread = jnp.dot(taps.astype(BF16), hot, preferred_element_type=F32)
    inside = iota((ROW, DEEP), 1)
    within = jnp.where(inside < KS * 32, inside & 31, 32)
    second = jnp.zeros((ROW, DEEP), F32)
    for a in range(KS):
        second = jnp.where(within == KS - 1 - a, spread[a * ROW : (a + 1) * ROW], second)
    for i in range(BLOCK):
        moved = pltpu.roll(second, i, 1) if i else second
        behind[i * ROW : (i + 1) * ROW, :] = moved.astype(BF16)
    total = taps[:ROW]
    for a in range(1, KS):
        total = total + taps[a * ROW : (a + 1) * ROW]
    norm = jnp.sum(total, axis=1, keepdims=True)
    scale[...] = jnp.broadcast_to(1.0 / norm, (ROW, CB))
    image[...] = jnp.concatenate(forward(ahead, rounded, sums, 3), axis=0)
    for out, part, lines in (
        (up, view[:HALO], image[:HALO, :]),
        (down, view[ROWS - HALO :], image[20 : 20 + HALO, :]),
    ):
        rows = []
        for x in (part, lines):
            high = x.astype(BF16).astype(F32)
            rows += [high, x - high]
        out[NEAR * ROW :, :] = jnp.concatenate(rows, axis=0).astype(BF16)


def iterate_kernel(
    own, left, right, sensor, image, ahead, behind, scale, codes,
    sent, flat, exact, second, light, whole, sums, ratio, stack,
):
    near = NEAR * ROW
    exact[:near, :] = left[:near].astype(F32)
    exact[near : near + ROWS * ROW, :] = own[...]
    exact[near + ROWS * ROW : 2 * near + ROWS * ROW, :] = right[:near].astype(F32)
    exact[2 * near + ROWS * ROW :, :] = jnp.zeros((8 * ROW, CB), F32)
    before, after = left[near:].astype(F32), right[near:].astype(F32)
    light[:HALO, :] = before[:HALO] + before[HALO : 2 * HALO]
    light[HALO : HALO + ROWS, :] = sensor[...]
    light[HALO + ROWS : 2 * HALO + ROWS, :] = after[:HALO] + after[HALO : 2 * HALO]
    light[2 * HALO + ROWS :, :] = jnp.zeros((16, CB), F32)
    blank = jnp.zeros((20, CB), F32)
    total = jnp.concatenate([blank[:12], image[...], blank], axis=0)
    above = jnp.concatenate([before[2 * HALO : 3 * HALO] + before[3 * HALO :], jnp.zeros((56, CB), F32)], axis=0)
    below = after[2 * HALO : 3 * HALO] + after[3 * HALO :]
    below = jnp.concatenate([jnp.zeros((44, CB), F32), below, blank[:12]], axis=0)
    whole[...] = total + above + below
    for m in range(2):
        stack[m * DEEP + KS * 32 : (m + 1) * DEEP, :] = jnp.zeros((DEEP - KS * 32, 2 * CB), BF16)
    tall = jnp.concatenate([scale[...]] * BLOCK, axis=0)

    def divide(total, offset, valid):
        rows = total.shape[0]
        seen = light[offset : offset + rows, :]
        inside = (iota((rows, CB), 0) < valid) & (seen != 0.0) & (total != 0.0)
        ratio[:rows, :] = jnp.where(inside, seen / jnp.where(inside, total, 1.0), 0.0)

    def spread_back(blocks):
        height = 16 * blocks + 16
        for b in range(KS):
            moved = lane_shift(ratio[:height, :], b).astype(BF16)
            for m in range(blocks):
                at = (m // 2) * DEEP + b * 32
                stack[at : at + 32, (m % 2) * CB : (m % 2 + 1) * CB] = moved[m * 16 : m * 16 + 32]

    def back(m):
        value = jnp.dot(behind[...], stack[m * DEEP : (m + 1) * DEEP, :], preferred_element_type=F32)
        return value[:, :CB] * tall, value[:, CB:] * tall

    divide(whole[...], 6, 68)
    spread_back(4)
    factors = back(0) + back(1)
    for m in range(4):
        value = exact[m * 256 : (m + 1) * 256, :] * factors[m]
        exact[m * 256 : (m + 1) * 256, :] = value
        second[m * 256 : (m + 1) * 256, :] = value.astype(BF16)
    divide(jnp.concatenate(forward(ahead, second, sums, 3), axis=0), 18, 44)
    spread_back(2)
    factors = back(0)
    done = [exact[(m * 16 + 12) * ROW : (m * 16 + 28) * ROW, :] * factors[m] for m in range(2)]
    lane = iota((256, CB), 1)
    packed = jnp.where(lane < WIN, pltpu.roll(done[0], CB - HALO, 1), pltpu.roll(done[1], WIN - HALO, 1))
    flat[...] = packed
    values = seed_values(codes[...], packed)
    for p in range(DEPTHS):
        sent[p, 0:16, :] = flat[pl.ds(p, 16, stride=ROW), :]
        sent[p, 16:24, :] = values


def more_kernel(turn, rank, code, flat, sent):
    codes = listed(rank[...], code[...], turn[0] * CAP)
    values = seed_values(codes, flat[...])
    for p in range(DEPTHS):
        sent[p] = values


def gather_kernel(at):
    def kernel(parts, out):
        total = parts[0, at : at + 8, :]
        for j in range(1, DEPTHS):
            total = total + parts[j, at : at + 8, :]
        line = jnp.concatenate([total[i : i + 1, :] for i in range(LANES)], axis=1)
        for j in range(TILES):
            out[j] = line

    return kernel


def looked(turn, parts, a_row, a_lane):
    table = jnp.concatenate([parts[t] for t in range(TILES)], axis=0)
    row = a_row[...] - turn * TILES
    hot = (iota((NAMES, TILES), 1) == row[:, :TILES]).astype(F32).astype(BF16)
    parts = split3(table)
    found = jnp.dot(hot, parts[0], preferred_element_type=F32)
    found = found + jnp.dot(hot, parts[1], preferred_element_type=F32)
    found = found + jnp.dot(hot, parts[2], preferred_element_type=F32)
    total = jnp.zeros((NAMES, CB), F32)
    for i in range(LANES):
        here = iota((NAMES, CB), 1) + i * CB == a_lane[...]
        total = total + jnp.where(here, found[:, i * CB : (i + 1) * CB], 0.0)
    return jnp.broadcast_to(lane_sum(total), (NAMES, CB))


def look_kernel(turn, parts, a_row, a_lane, known, out):
    out[...] = known[...] + looked(turn[0], parts, a_row, a_lane)


def home_kernel(parts, weights, b_col, estimate, proj, lines):
    lane = iota((16, CB), 1)
    for c in range(NCB):
        a, b = parts[2 * c, :16, :], parts[2 * c + 1, :16, :]
        top = jnp.where(lane < WIN, a, pltpu.roll(b, WIN, 1))
        bottom = jnp.where(lane < WIN, pltpu.roll(a, WIN, 1), b)
        estimate[:16, c * CB : (c + 1) * CB] = top
        estimate[16:, c * CB : (c + 1) * CB] = bottom
        lines[c * ROWS : c * ROWS + 16, :] = top
        lines[c * ROWS + 16 : (c + 1) * ROWS, :] = bottom
    blocks = [lines[pl.ds(br, 64, stride=4), :] for br in range(4)]
    blocked = jnp.concatenate(blocks, axis=1)
    number = b_col[:, :64]
    number = (number & 7) * 8 + (number >> 3)
    hot = (iota((SLOTS, 64), 1) == number).astype(F32).astype(BF16)
    high, low = split2(blocked)
    picked = jnp.dot(hot, high, preferred_element_type=F32) + jnp.dot(hot, low, preferred_element_type=F32)
    product = weights[...].astype(F32) * picked
    total = product[:, :CB]
    for br in range(1, 4):
        total = total + product[:, br * CB : (br + 1) * CB]
    proj[...] = jnp.broadcast_to(jnp.sum(total, axis=1, keepdims=True), (SLOTS, CB))


def slots_kernel(parts, a_row, a_lane, known, gram, q_row, q_col, proj, out, own):
    start = known[...] + looked(0, parts, a_row, a_lane)
    padded = jnp.concatenate([start, jnp.zeros((3 * CB - NAMES, CB), F32)], axis=0)
    row = jnp.transpose(padded)[0:1, :]
    own[...] = row[:, SLOTS:]
    start_row = row[:, :SLOTS]
    terms = gram[...] * start_row
    over = jnp.sum(terms[:, :CB] + terms[:, CB:], axis=1, keepdims=True)
    place = q_col[...]
    lane = iota((SLOTS, CB), 1)
    target = ((place >> 5) & 3) * 32 + (place & 15)
    sent = jnp.where(lane == target, proj[...], 0.0) + jnp.where(lane == target + 16, over, 0.0)
    spot = q_row[0:1, :]
    line = ((spot >> 9) * 2 + ((spot >> 4) & 1)) * 4 + ((spot >> 7) & 3)
    row_hot = (iota((CB, SLOTS), 0) == jnp.where(spot >= 0, line, -1)).astype(F32).astype(BF16)
    parts = split3(sent)
    dense = jnp.dot(row_hot, parts[0], preferred_element_type=F32)
    dense = dense + jnp.dot(row_hot, parts[1], preferred_element_type=F32)
    dense = dense + jnp.dot(row_hot, parts[2], preferred_element_type=F32)
    for j in range(TILES):
        out[j] = dense[j * 4 : (j + 1) * 4]


def fold_kernel(parts, out):
    total = parts[0]
    for j in range(1, TILES):
        total = total + parts[j]
    total = jnp.concatenate([total, total], axis=0)
    for m in range(4):
        moved = pltpu.roll(total, (CB - 32 * m) % CB, 1) if m else total
        for r in range(4):
            out[4 * r + m] = moved[r : r + 1]


def final_kernel(parts, own, out):
    total = parts[0]
    for j in range(1, TILES // 2):
        total = total + parts[j]
    over = pltpu.roll(total, CB - 16, 1)
    initial = own[...]
    real = iota((1, CB), 1) < 16
    bottom = jnp.where(real, over + 100.0 * initial, 1.0)
    out[...] = jnp.where(real, initial * total, 0.0) / bottom


def swap(pieces, axis, groups=None):
    return lax.all_to_all(pieces, axis, 0, 0, axis_index_groups=groups)


def body(
    volume,
    measured,
    point_spread,
    entry_block,
    entry_neuron,
    footprints,
    seed_plane,
    seed_row,
    seed_col,
    owner_slot,
):
    d = lax.axis_index("depth")
    t = lax.axis_index("tile")
    where = jnp.stack([d, t, (d * TILES + t) * 16]).astype(I32)
    [windows] = call(window_kernel, [((DEPTHS, ROWS, CB), F32)], 2)(volume, point_spread)
    windows, where = lax.optimization_barrier((windows, where))
    tied = (swap(windows, "depth"), where, measured, entry_block, entry_neuron, footprints, owner_slot)
    tied = lax.optimization_barrier(tied + (seed_plane, seed_row, seed_col))
    parts, where, measured, entry_block, entry_neuron, footprints, owner_slot = tied[:7]
    seed_plane, seed_row, seed_col = tied[7:]
    parts = parts.reshape(DEPTHS * ROWS, CB)
    table = owner_slot.reshape(64, CB)
    message = ((NEAR * ROW + 4 * HALO, CB), BF16)
    band = ((256, DEEP), BF16)
    own, sensor, down, up, ahead, behind, scale, image = call(
        open_kernel,
        [((ROWS * ROW, CB), F32), ((ROWS, CB), F32), message, message, band, band, ((ROW, CB), F32), ((48, CB), F32)],
        3,
        scalars=(0,),
        scratch=[
            pltpu.VMEM((ROWS, COLS + 2 * CB), F32),
            pltpu.VMEM((64 * ROW, CB), BF16),
            pltpu.VMEM((2, 256, CB), F32),
        ],
    )(where, parts, measured)
    left = lax.ppermute(down, "tile", [(i, i + 1) for i in range(TILES - 1)])
    right = lax.ppermute(up, "tile", [(i + 1, i) for i in range(TILES - 1)])
    lines = [x.reshape(64, CB) for x in (seed_plane, seed_row, seed_col)]
    square = ((64, CB), I32)
    rank, code, first = call(lists_kernel, [square, square, ((8, CB), I32)], 4, scalars=(0,))(where, *lines)
    sent, flat = call(
        iterate_kernel,
        [((DEPTHS, 24, CB), F32), ((256, CB), F32)],
        9,
        scratch=[
            pltpu.VMEM((64 * ROW, CB), F32),
            pltpu.VMEM((64 * ROW, CB), BF16),
            pltpu.VMEM((96, CB), F32),
            pltpu.VMEM((80, CB), F32),
            pltpu.VMEM((2, 256, CB), F32),
            pltpu.VMEM((80, CB), F32),
            pltpu.VMEM((2 * DEEP, 2 * CB), BF16),
        ],
    )(own, left, right, sensor, image, ahead, behind, scale, first)
    later = (swap(sent, "depth"), entry_block, entry_neuron, table, lines[1])
    parts, entry_block, entry_neuron, table, seed_rows = lax.optimization_barrier(later)
    weights = footprints[0].reshape(SLOTS, 512)
    column = ((SLOTS, CB), I32)
    names = ((NAMES, CB), I32)
    gram, q_row, q_col, b_col, a_row, a_lane, most = call(
        prepare_kernel,
        [((SLOTS, SLOTS), F32), ((8, SLOTS), I32), column, column, names, names, ((8, CB), I32)],
        6,
        scalars=(0,),
    )(where, entry_block, entry_neuron, weights, table, seed_rows)

    def share(values, at):
        [values] = call(gather_kernel(at), [((TILES, 1, CAP), F32)], 1)(values)
        return swap(values, "tile")

    def look(turn, values, known):
        return call(look_kernel, [((NAMES, CB), F32)], 5, scalars=(0,))(
            turn, values, a_row, a_lane, known
        )[0]

    def another(step, known):
        turn = jnp.reshape(step, (1,))
        [values] = call(more_kernel, [((DEPTHS, 8, CB), F32)], 4, scalars=(0,))(
            turn, rank, code, flat
        )
        return look(turn, share(swap(values, "depth"), 0), known)

    rounds = (most[0, 0] + CAP - 1) // CAP
    shared, none = lax.optimization_barrier((share(parts, 16), jnp.zeros((NAMES, CB), F32)))
    known = lax.fori_loop(1, rounds, another, none)
    estimate, proj = call(
        home_kernel,
        [((ROWS, COLS), F32), ((SLOTS, CB), F32)],
        3,
        scratch=[pltpu.VMEM((NCB * ROWS, CB), F32)],
    )(parts, weights, b_col)
    sent, own = call(slots_kernel, [((TILES, 4, CB), F32), ((1, CB), F32)], 8)(
        shared, a_row, a_lane, known, gram, q_row, q_col, proj
    )
    pairs = TILES // 2
    near = [[d * TILES + 2 * z + x for d in range(DEPTHS) for x in range(2)] for z in range(pairs)]
    far = [[2 * z + x for z in range(pairs)] for x in range(2)]
    sent = swap(sent, ("depth", "tile"), near)
    [sent] = call(fold_kernel, [((pairs, 1, CB), F32)], 1)(sent)
    [demixed] = call(final_kernel, [((1, CB), F32)], 2)(swap(sent, "tile", far), own)
    return estimate[None], demixed[0, :16]


def solution(mesh):
    in_specs = (
        P("depth", "tile", None),
        P("tile", None),
        P("depth", None, None),
        P("tile", "depth"),
        P("tile", "depth"),
        P("tile", "depth", None, None),
        P(),
        P(),
        P(),
        P(),
    )
    out_specs = (P("depth", "tile", None), P(("depth", "tile")))
    return jax.shard_map(body, mesh=mesh, in_specs=in_specs, out_specs=out_specs, check_vma=False)
```

```python
import jax
import jax.numpy as jnp
from jax import lax
from jax.experimental import pallas as pl
from jax.experimental.pallas import tpu as pltpu
from jax.sharding import PartitionSpec as P

F32 = jnp.float32
BF16 = jnp.bfloat16
I32 = jnp.int32
KS = 13
RADIUS = 6
ROWS = 32
COLS = 1024
CB = 128
NCB = COLS // CB
DEPTHS = 16
TILES = 32
SLOTS = 256
NEURONS = 8192
HALO = 24
WIN = 64
LIVE = WIN + 2 * HALO
ROW = DEPTHS
BLOCK = 16
DEEP = 32 * ROW
CAP = 384
LANES = CAP // CB
NEAR = 12
NAMES = SLOTS + 16
VMEM = pl.BlockSpec(memory_space=pltpu.VMEM)
SMEM = pl.BlockSpec(memory_space=pltpu.SMEM)


def call(kernel, outs, n_in, scalars=(), scratch=(), mib=24):
    return pl.pallas_call(
        kernel,
        out_shape=[jax.ShapeDtypeStruct(s, t) for s, t in outs],
        in_specs=[SMEM if i in scalars else VMEM for i in range(n_in)],
        out_specs=[VMEM] * len(outs),
        scratch_shapes=list(scratch),
        compiler_params=pltpu.CompilerParams(vmem_limit_bytes=mib * 2**20),
    )


def iota(shape, dim):
    return lax.broadcasted_iota(I32, shape, dim)


def split2(x):
    high = x.astype(BF16)
    return high, (x - high.astype(F32)).astype(BF16)


def split3(x):
    high = x.astype(BF16)
    rest = x - high.astype(F32)
    mid = rest.astype(BF16)
    return high, mid, (rest - mid.astype(F32)).astype(BF16)


def column_of(row):
    n = row.shape[1]
    return jnp.transpose(jnp.broadcast_to(row, (CB, n)))


def lane_sum(x):
    return jnp.sum(x, axis=1, keepdims=True)


def prepare_kernel(
    where, block, neuron, weights, owner, s_row,
    gram, q_row, q_col, b_col, a_row, a_lane, most,
):
    foot = weights[...]
    product = lax.dot_general(foot, foot, (((1,), (1,)), ((), ())), preferred_element_type=F32)
    blocks = column_of(block[...].astype(F32))
    same = jnp.concatenate([blocks, blocks], axis=1) == block[...].astype(F32)
    gram[...] = jnp.where(same, product, 0.0)
    b_col[...] = blocks.astype(I32)
    table = owner[...]
    number = iota((64, CB), 0) * CB + iota((64, CB), 1)
    own = jnp.zeros((16, CB), F32)
    for i in range(16):
        hit = jnp.sum(jnp.where(table == where[2] + i, number.astype(F32), 0.0), axis=0, keepdims=True)
        own = jnp.where(iota((16, CB), 0) == i, lane_sum(hit), own)
    names = jnp.concatenate([column_of(neuron[...].astype(F32)), own], axis=0).astype(I32)
    tile = s_row[...] >> 5
    tables = [tile, table >> 7, table & 127]
    tables = jnp.concatenate([x.astype(F32) for x in tables], axis=1).astype(BF16)
    hot = (iota((NAMES, 64), 1) == (names[:, :64] >> 7)).astype(F32).astype(BF16)
    found = jnp.dot(hot, tables, preferred_element_type=F32)
    lane_hot = iota((NAMES, CB), 1) == (names & 127)
    picked = [lane_sum(jnp.where(lane_hot, found[:, i * CB : (i + 1) * CB], 0.0)) for i in range(3)]
    n_tile = picked[0].astype(I32)
    place = jnp.broadcast_to(picked[1] * 128.0 + picked[2], (NAMES, CB))[:SLOTS]
    place = jnp.where(names[:SLOTS] >= 0, place, -1.0)
    q_col[...] = place.astype(I32)
    q_row[...] = jnp.transpose(place)[0:8, :].astype(I32)
    held = jnp.zeros((TILES, CB), F32)
    for r in range(64):
        here = lane_sum((iota((TILES, CB), 0) == tile[r : r + 1, :]).astype(F32))
        held = jnp.where(iota((TILES, CB), 1) == r, here, held)
    top = jnp.max(lane_sum(held), axis=0, keepdims=True)
    turns = jnp.zeros((1, 1), I32)
    for i in range((NEURONS + CAP - 1) // CAP):
        turns = turns + (top > i * CAP).astype(I32)
    most[...] = jnp.broadcast_to(turns, (8, CB))
    before = (iota((CB, CB), 0) < iota((CB, CB), 1)).astype(F32).astype(BF16)
    earlier = jnp.dot(held.astype(BF16), before, preferred_element_type=F32)
    row_hot = (iota((NAMES, CB), 1) == (names >> 7)).astype(F32).astype(BF16)
    counts = jnp.zeros((NAMES, TILES), F32)
    for part in split2(earlier):
        counts = counts + lax.dot_general(
            row_hot, part, (((1,), (1,)), ((), ())), preferred_element_type=F32
        )
    count = lane_sum(jnp.where(iota((NAMES, TILES), 1) == n_tile, counts, 0.0))
    inside = (found[:, :CB] == picked[0]) & (iota((NAMES, CB), 1) < (names & 127))
    count = count + lane_sum(jnp.where(inside, 1.0, 0.0))
    position = jnp.broadcast_to(count, (NAMES, CB)).astype(I32)
    turn = jnp.zeros((NAMES, CB), I32)
    for i in range(1, (NEURONS + CAP - 1) // CAP):
        turn = turn + (position >= i * CAP).astype(I32)
    a_row[...] = jnp.where(names >= 0, turn * TILES + n_tile, -1)
    a_lane[...] = position - turn * CAP


def lists_kernel(where, s_plane, s_row, s_col, rank, code, first):
    row, col = s_row[...], s_col[...]
    tile, window = row >> 5, col >> 6
    local = tile == where[1]
    mask = local.astype(F32)
    before = (iota((CB, CB), 0) < iota((CB, CB), 1)).astype(F32).astype(BF16)
    inside = jnp.dot(mask.astype(BF16), before, preferred_element_type=F32)
    rows = jnp.broadcast_to(lane_sum(mask), (64, CB)).astype(BF16)
    above = (iota((64, 64), 1) < iota((64, 64), 0)).astype(F32).astype(BF16)
    inside = inside + jnp.dot(above, rows, preferred_element_type=F32)
    order = jnp.where(local & (window == where[0]), inside, -1.0).astype(I32)
    spot = ((row >> 4) & 1) * WIN + (col & (WIN - 1))
    coded = ((row & 15) * ROW + s_plane[...]) * CB + spot
    rank[...] = order
    code[...] = coded
    first[...] = listed(order, coded, 0)


def listed(order, coded, start):
    place = order - start
    place = jnp.where(place < CAP, place, -1)
    total = jnp.zeros((32, CB), F32)
    for r in range(0, 64, 8):
        lines = [place[i : i + 1, :] for i in range(r, r + 8)]
        codes = [coded[i : i + 1, :] for i in range(r, r + 8)]
        left = []
        for at, code in zip(lines, codes):
            here = iota((8, CB), 0) == (at >> 7)
            left.append(
                jnp.concatenate(
                    [
                        jnp.where(here, (code >> 7).astype(F32), 0.0),
                        jnp.where(here, (code & 127).astype(F32), 0.0),
                        jnp.where(here, 1.0, 0.0),
                        jnp.zeros((8, CB), F32),
                    ],
                    axis=0,
                )
            )
        left = jnp.concatenate(left, axis=1).astype(BF16)
        right = [(iota((CB, CB), 0) == jnp.where(at >= 0, at & 127, -1)).astype(F32) for at in lines]
        right = jnp.concatenate(right, axis=1).astype(BF16)
        total = total + lax.dot_general(
            left, right, (((1,), (1,)), ((), ())), preferred_element_type=F32
        )
    value = total[0:8] * 128.0 + total[8:16]
    return jnp.where(total[16:24] > 0.0, value, -1.0).astype(I32)


def seed_values(codes, flat):
    parts = split3(flat)
    result = []
    for i in range(LANES):
        index = column_of(codes[i : i + 1, :].astype(F32)).astype(I32)
        key = jnp.concatenate([index, index], axis=1) >> 7
        hot = (iota((CB, 256), 1) == key).astype(F32).astype(BF16)
        found = jnp.dot(hot, parts[0], preferred_element_type=F32)
        found = found + jnp.dot(hot, parts[1], preferred_element_type=F32)
        found = found + jnp.dot(hot, parts[2], preferred_element_type=F32)
        picked = jnp.where(iota((CB, CB), 1) == (index & (CB - 1)), found, 0.0)
        result.append(jnp.sum(jnp.transpose(picked), axis=0, keepdims=True))
    result.append(jnp.zeros((8 - LANES, CB), F32))
    return jnp.concatenate(result, axis=0)


def window_kernel(volume, spread, windows):
    lane = iota((ROWS, CB), 1)
    taps = jnp.concatenate([spread[0].astype(F32), jnp.zeros((KS, CB - KS), F32)], axis=1)
    taps = jnp.concatenate([pltpu.roll(taps, LIVE, 1), jnp.zeros((ROWS - KS, CB), F32)], axis=0)
    zeros = jnp.zeros((ROWS, CB), F32)
    padded = jnp.concatenate([zeros, volume[0], zeros], axis=1)
    for j in range(DEPTHS):
        start = CB - HALO + WIN * j
        low = start // CB * CB
        moved = pltpu.roll(padded[:, low : low + 2 * CB], 2 * CB - start % CB, 1)[:, :CB]
        windows[j] = jnp.where(lane < LIVE, moved, taps)


def lane_shift(x, b):
    shift = (RADIUS - b) % CB
    return pltpu.roll(x, shift, 1) if shift else x


def forward(ahead, source, sums, blocks):
    result = []
    for m in range(0, blocks, 2):
        pair = range(m, min(m + 2, blocks))
        right = jnp.concatenate([source[i * 256 : i * 256 + DEEP, :] for i in pair], axis=1)
        value = jnp.dot(ahead[...], right, preferred_element_type=F32)
        for i in pair:
            at = (i - m) * CB
            sums[i - m] = value[:, at : at + CB]
        for i in pair:
            total = lane_shift(sums[i - m, pl.ds(0, BLOCK, stride=16), :], 0)
            for b in range(1, KS):
                total = total + lane_shift(sums[i - m, pl.ds(b, BLOCK, stride=16), :], b)
            result.append(total)
    return result


def open_kernel(
    where, parts, measured,
    own, sensor, down, up, ahead, behind, scale, image,
    wide, rounded, sums,
):
    lane = iota((ROW, CB), 1)
    rounded[: NEAR * ROW, :] = jnp.zeros((NEAR * ROW, CB), BF16)
    rounded[(NEAR + ROWS) * ROW :, :] = jnp.zeros(((NEAR + 8) * ROW, CB), BF16)
    for r in range(ROWS):
        line = jnp.where(lane < LIVE, parts[pl.ds(r, ROW, stride=ROWS), :], 0.0)
        own[r * ROW : (r + 1) * ROW, :] = line
        line = line.astype(BF16)
        rounded[(NEAR + r) * ROW : (NEAR + r + 1) * ROW, :] = line
        if r < NEAR:
            up[r * ROW : (r + 1) * ROW, :] = line
        if r >= ROWS - NEAR:
            at = (r - ROWS + NEAR) * ROW
            down[at : at + ROW, :] = line
    zeros = jnp.zeros((ROWS, CB), F32)
    wide[:, :CB] = zeros
    wide[:, CB : CB + COLS] = measured[...]
    wide[:, CB + COLS :] = zeros
    start = CB - HALO + WIN * where[0]
    low = pl.multiple_of((start >> 7) * CB, CB)
    moved = pltpu.roll(wide[:, pl.ds(low, 2 * CB)], 2 * CB - (start & (CB - 1)), 1)[:, :CB]
    view = jnp.where(iota((ROWS, CB), 1) < LIVE, moved, 0.0)
    sensor[...] = view
    taps = jnp.concatenate([parts[pl.ds(a, ROW, stride=ROWS), :] for a in range(16)], axis=0)
    taps = jnp.where(iota((256, CB), 1) >= LIVE, taps, 0.0)
    first = jnp.transpose(taps)[LIVE:, :]
    first = jnp.concatenate([first, jnp.zeros((16, 256), F32)], axis=1)
    for i in range(BLOCK):
        moved = pltpu.roll(first, i * ROW, 1) if i else first
        ahead[i * 16 : (i + 1) * 16, :] = moved.astype(BF16)
    lane = iota((CB, DEEP), 1)
    hot = (iota((CB, DEEP), 0) == LIVE + KS - 1 - (lane >> 5)).astype(F32).astype(BF16)
    spread = jnp.dot(taps.astype(BF16), hot, preferred_element_type=F32)
    inside = iota((ROW, DEEP), 1)
    within = jnp.where(inside < KS * 32, inside & 31, 32)
    second = jnp.zeros((ROW, DEEP), F32)
    for a in range(KS):
        second = jnp.where(within == KS - 1 - a, spread[a * ROW : (a + 1) * ROW], second)
    for i in range(BLOCK):
        moved = pltpu.roll(second, i, 1) if i else second
        behind[i * ROW : (i + 1) * ROW, :] = moved.astype(BF16)
    total = taps[:ROW]
    for a in range(1, KS):
        total = total + taps[a * ROW : (a + 1) * ROW]
    norm = jnp.sum(total, axis=1, keepdims=True)
    scale[...] = jnp.broadcast_to(1.0 / norm, (ROW, CB))
    image[...] = jnp.concatenate(forward(ahead, rounded, sums, 3), axis=0)
    for out, part, lines in (
        (up, view[:HALO], image[:HALO, :]),
        (down, view[ROWS - HALO :], image[20 : 20 + HALO, :]),
    ):
        rows = []
        for x in (part, lines):
            high = x.astype(BF16).astype(F32)
            rows += [high, x - high]
        out[NEAR * ROW :, :] = jnp.concatenate(rows, axis=0).astype(BF16)


def iterate_kernel(
    own, left, right, sensor, image, ahead, behind, scale, codes,
    sent, flat, exact, second, light, whole, sums, ratio, stack,
):
    near = NEAR * ROW
    exact[:near, :] = left[:near].astype(F32)
    exact[near : near + ROWS * ROW, :] = own[...]
    exact[near + ROWS * ROW : 2 * near + ROWS * ROW, :] = right[:near].astype(F32)
    exact[2 * near + ROWS * ROW :, :] = jnp.zeros((8 * ROW, CB), F32)
    before, after = left[near:].astype(F32), right[near:].astype(F32)
    light[:HALO, :] = before[:HALO] + before[HALO : 2 * HALO]
    light[HALO : HALO + ROWS, :] = sensor[...]
    light[HALO + ROWS : 2 * HALO + ROWS, :] = after[:HALO] + after[HALO : 2 * HALO]
    light[2 * HALO + ROWS :, :] = jnp.zeros((16, CB), F32)
    blank = jnp.zeros((20, CB), F32)
    total = jnp.concatenate([blank[:12], image[...], blank], axis=0)
    above = jnp.concatenate([before[2 * HALO : 3 * HALO] + before[3 * HALO :], jnp.zeros((56, CB), F32)], axis=0)
    below = after[2 * HALO : 3 * HALO] + after[3 * HALO :]
    below = jnp.concatenate([jnp.zeros((44, CB), F32), below, blank[:12]], axis=0)
    whole[...] = total + above + below
    for m in range(2):
        stack[m * DEEP + KS * 32 : (m + 1) * DEEP, :] = jnp.zeros((DEEP - KS * 32, 2 * CB), BF16)
    tall = jnp.concatenate([scale[...]] * BLOCK, axis=0)

    def divide(total, offset, valid):
        rows = total.shape[0]
        seen = light[offset : offset + rows, :]
        inside = (iota((rows, CB), 0) < valid) & (seen != 0.0) & (total != 0.0)
        ratio[:rows, :] = jnp.where(inside, seen / jnp.where(inside, total, 1.0), 0.0)

    def spread_back(blocks):
        height = 16 * blocks + 16
        for b in range(KS):
            moved = lane_shift(ratio[:height, :], b).astype(BF16)
            for m in range(blocks):
                at = (m // 2) * DEEP + b * 32
                stack[at : at + 32, (m % 2) * CB : (m % 2 + 1) * CB] = moved[m * 16 : m * 16 + 32]

    def back(m):
        value = jnp.dot(behind[...], stack[m * DEEP : (m + 1) * DEEP, :], preferred_element_type=F32)
        return value[:, :CB] * tall, value[:, CB:] * tall

    divide(whole[...], 6, 68)
    spread_back(4)
    factors = back(0) + back(1)
    for m in range(4):
        value = exact[m * 256 : (m + 1) * 256, :] * factors[m]
        exact[m * 256 : (m + 1) * 256, :] = value
        second[m * 256 : (m + 1) * 256, :] = value.astype(BF16)
    divide(jnp.concatenate(forward(ahead, second, sums, 3), axis=0), 18, 44)
    spread_back(2)
    factors = back(0)
    done = [exact[(m * 16 + 12) * ROW : (m * 16 + 28) * ROW, :] * factors[m] for m in range(2)]
    lane = iota((256, CB), 1)
    packed = jnp.where(lane < WIN, pltpu.roll(done[0], CB - HALO, 1), pltpu.roll(done[1], WIN - HALO, 1))
    flat[...] = packed
    values = seed_values(codes[...], packed)
    for p in range(DEPTHS):
        sent[p, 0:16, :] = flat[pl.ds(p, 16, stride=ROW), :]
        sent[p, 16:24, :] = values


def more_kernel(turn, rank, code, flat, sent):
    codes = listed(rank[...], code[...], turn[0] * CAP)
    values = seed_values(codes, flat[...])
    for p in range(DEPTHS):
        sent[p] = values


def gather_kernel(at):
    def kernel(parts, out):
        total = parts[0, at : at + 8, :]
        for j in range(1, DEPTHS):
            total = total + parts[j, at : at + 8, :]
        line = jnp.concatenate([total[i : i + 1, :] for i in range(LANES)], axis=1)
        for j in range(TILES):
            out[j] = line

    return kernel


def looked(turn, parts, a_row, a_lane):
    table = jnp.concatenate([parts[t] for t in range(TILES)], axis=0)
    row = a_row[...] - turn * TILES
    hot = (iota((NAMES, TILES), 1) == row[:, :TILES]).astype(F32).astype(BF16)
    parts = split3(table)
    found = jnp.dot(hot, parts[0], preferred_element_type=F32)
    found = found + jnp.dot(hot, parts[1], preferred_element_type=F32)
    found = found + jnp.dot(hot, parts[2], preferred_element_type=F32)
    total = jnp.zeros((NAMES, CB), F32)
    for i in range(LANES):
        here = iota((NAMES, CB), 1) + i * CB == a_lane[...]
        total = total + jnp.where(here, found[:, i * CB : (i + 1) * CB], 0.0)
    return jnp.broadcast_to(lane_sum(total), (NAMES, CB))


def look_kernel(turn, parts, a_row, a_lane, known, out):
    out[...] = known[...] + looked(turn[0], parts, a_row, a_lane)


def home_kernel(parts, weights, b_col, estimate, proj, lines):
    lane = iota((16, CB), 1)
    for c in range(NCB):
        a, b = parts[2 * c, :16, :], parts[2 * c + 1, :16, :]
        top = jnp.where(lane < WIN, a, pltpu.roll(b, WIN, 1))
        bottom = jnp.where(lane < WIN, pltpu.roll(a, WIN, 1), b)
        estimate[:16, c * CB : (c + 1) * CB] = top
        estimate[16:, c * CB : (c + 1) * CB] = bottom
        lines[c * ROWS : c * ROWS + 16, :] = top
        lines[c * ROWS + 16 : (c + 1) * ROWS, :] = bottom
    blocks = [lines[pl.ds(br, 64, stride=4), :] for br in range(4)]
    blocked = jnp.concatenate(blocks, axis=1)
    number = b_col[:, :64]
    number = (number & 7) * 8 + (number >> 3)
    hot = (iota((SLOTS, 64), 1) == number).astype(F32).astype(BF16)
    high, low = split2(blocked)
    picked = jnp.dot(hot, high, preferred_element_type=F32) + jnp.dot(hot, low, preferred_element_type=F32)
    product = weights[...].astype(F32) * picked
    total = product[:, :CB]
    for br in range(1, 4):
        total = total + product[:, br * CB : (br + 1) * CB]
    proj[...] = jnp.broadcast_to(jnp.sum(total, axis=1, keepdims=True), (SLOTS, CB))


def slots_kernel(parts, a_row, a_lane, known, gram, q_row, q_col, proj, out, own):
    start = known[...] + looked(0, parts, a_row, a_lane)
    padded = jnp.concatenate([start, jnp.zeros((3 * CB - NAMES, CB), F32)], axis=0)
    row = jnp.transpose(padded)[0:1, :]
    own[...] = row[:, SLOTS:]
    start_row = row[:, :SLOTS]
    terms = gram[...] * start_row
    over = jnp.sum(terms[:, :CB] + terms[:, CB:], axis=1, keepdims=True)
    place = q_col[...]
    lane = iota((SLOTS, CB), 1)
    target = ((place >> 5) & 3) * 32 + (place & 15)
    sent = jnp.where(lane == target, proj[...], 0.0) + jnp.where(lane == target + 16, over, 0.0)
    spot = q_row[0:1, :]
    line = ((spot >> 9) * 2 + ((spot >> 4) & 1)) * 4 + ((spot >> 7) & 3)
    row_hot = (iota((CB, SLOTS), 0) == jnp.where(spot >= 0, line, -1)).astype(F32).astype(BF16)
    parts = split3(sent)
    dense = jnp.dot(row_hot, parts[0], preferred_element_type=F32)
    dense = dense + jnp.dot(row_hot, parts[1], preferred_element_type=F32)
    dense = dense + jnp.dot(row_hot, parts[2], preferred_element_type=F32)
    for j in range(TILES):
        out[j] = dense[j * 4 : (j + 1) * 4]


def fold_kernel(parts, out):
    total = parts[0]
    for j in range(1, TILES):
        total = total + parts[j]
    total = jnp.concatenate([total, total], axis=0)
    for m in range(4):
        moved = pltpu.roll(total, (CB - 32 * m) % CB, 1) if m else total
        for r in range(4):
            out[4 * r + m] = moved[r : r + 1]


def final_kernel(parts, own, out):
    total = parts[0]
    for j in range(1, TILES // 2):
        total = total + parts[j]
    over = pltpu.roll(total, CB - 16, 1)
    initial = own[...]
    real = iota((1, CB), 1) < 16
    bottom = jnp.where(real, over + 100.0 * initial, 1.0)
    out[...] = jnp.where(real, initial * total, 0.0) / bottom


def swap(pieces, axis, groups=None):
    return lax.all_to_all(pieces, axis, 0, 0, axis_index_groups=groups)


def body(
    volume,
    measured,
    point_spread,
    entry_block,
    entry_neuron,
    footprints,
    seed_plane,
    seed_row,
    seed_col,
    owner_slot,
):
    d = lax.axis_index("depth")
    t = lax.axis_index("tile")
    where = jnp.stack([d, t, (d * TILES + t) * 16]).astype(I32)
    [windows] = call(window_kernel, [((DEPTHS, ROWS, CB), F32)], 2)(volume, point_spread)
    windows, where = lax.optimization_barrier((windows, where))
    tied = (swap(windows, "depth"), where, measured, entry_block, entry_neuron, footprints, owner_slot)
    tied = lax.optimization_barrier(tied + (seed_plane, seed_row, seed_col))
    parts, where, measured, entry_block, entry_neuron, footprints, owner_slot = tied[:7]
    seed_plane, seed_row, seed_col = tied[7:]
    parts = parts.reshape(DEPTHS * ROWS, CB)
    table = owner_slot.reshape(64, CB)
    message = ((NEAR * ROW + 4 * HALO, CB), BF16)
    band = ((256, DEEP), BF16)
    own, sensor, down, up, ahead, behind, scale, image = call(
        open_kernel,
        [((ROWS * ROW, CB), F32), ((ROWS, CB), F32), message, message, band, band, ((ROW, CB), F32), ((48, CB), F32)],
        3,
        scalars=(0,),
        scratch=[
            pltpu.VMEM((ROWS, COLS + 2 * CB), F32),
            pltpu.VMEM((64 * ROW, CB), BF16),
            pltpu.VMEM((2, 256, CB), F32),
        ],
    )(where, parts, measured)
    left = lax.ppermute(down, "tile", [(i, i + 1) for i in range(TILES - 1)])
    right = lax.ppermute(up, "tile", [(i + 1, i) for i in range(TILES - 1)])
    lines = [x.reshape(64, CB) for x in (seed_plane, seed_row, seed_col)]
    square = ((64, CB), I32)
    rank, code, first = call(lists_kernel, [square, square, ((8, CB), I32)], 4, scalars=(0,))(where, *lines)
    sent, flat = call(
        iterate_kernel,
        [((DEPTHS, 24, CB), F32), ((256, CB), F32)],
        9,
        scratch=[
            pltpu.VMEM((64 * ROW, CB), F32),
            pltpu.VMEM((64 * ROW, CB), BF16),
            pltpu.VMEM((96, CB), F32),
            pltpu.VMEM((80, CB), F32),
            pltpu.VMEM((2, 256, CB), F32),
            pltpu.VMEM((80, CB), F32),
            pltpu.VMEM((2 * DEEP, 2 * CB), BF16),
        ],
    )(own, left, right, sensor, image, ahead, behind, scale, first)
    later = (swap(sent, "depth"), entry_block, entry_neuron, table, lines[1])
    parts, entry_block, entry_neuron, table, seed_rows = lax.optimization_barrier(later)
    weights = footprints[0].reshape(SLOTS, 512)
    column = ((SLOTS, CB), I32)
    names = ((NAMES, CB), I32)
    gram, q_row, q_col, b_col, a_row, a_lane, most = call(
        prepare_kernel,
        [((SLOTS, SLOTS), F32), ((8, SLOTS), I32), column, column, names, names, ((8, CB), I32)],
        6,
        scalars=(0,),
    )(where, entry_block, entry_neuron, weights, table, seed_rows)

    def share(values, at):
        [values] = call(gather_kernel(at), [((TILES, 1, CAP), F32)], 1)(values)
        return swap(values, "tile")

    def look(turn, values, known):
        return call(look_kernel, [((NAMES, CB), F32)], 5, scalars=(0,))(
            turn, values, a_row, a_lane, known
        )[0]

    def another(step, known):
        turn = jnp.reshape(step, (1,))
        [values] = call(more_kernel, [((DEPTHS, 8, CB), F32)], 4, scalars=(0,))(
            turn, rank, code, flat
        )
        return look(turn, share(swap(values, "depth"), 0), known)

    shared, none = lax.optimization_barrier((share(parts, 16), jnp.zeros((NAMES, CB), F32)))
    known = lax.fori_loop(1, most[0, 0], another, none)
    estimate, proj = call(
        home_kernel,
        [((ROWS, COLS), F32), ((SLOTS, CB), F32)],
        3,
        scratch=[pltpu.VMEM((NCB * ROWS, CB), F32)],
    )(parts, weights, b_col)
    sent, own = call(slots_kernel, [((TILES, 4, CB), F32), ((1, CB), F32)], 8)(
        shared, a_row, a_lane, known, gram, q_row, q_col, proj
    )
    pairs = TILES // 2
    near = [[d * TILES + 2 * z + x for d in range(DEPTHS) for x in range(2)] for z in range(pairs)]
    far = [[2 * z + x for z in range(pairs)] for x in range(2)]
    sent = swap(sent, ("depth", "tile"), near)
    [sent] = call(fold_kernel, [((pairs, 1, CB), F32)], 1)(sent)
    [demixed] = call(final_kernel, [((1, CB), F32)], 2)(swap(sent, "tile", far), own)
    return estimate[None], demixed[0, :16]


def solution(mesh):
    in_specs = (
        P("depth", "tile", None),
        P("tile", None),
        P("depth", None, None),
        P("tile", "depth"),
        P("tile", "depth"),
        P("tile", "depth", None, None),
        P(),
        P(),
        P(),
        P(),
    )
    out_specs = (P("depth", "tile", None), P(("depth", "tile")))
    return jax.shard_map(body, mesh=mesh, in_specs=in_specs, out_specs=out_specs, check_vma=False)
```

```python
import jax
import jax.numpy as jnp
from jax import lax
from jax.experimental import pallas as pl
from jax.experimental.pallas import tpu as pltpu
from jax.sharding import PartitionSpec as P

F32 = jnp.float32
BF16 = jnp.bfloat16
I32 = jnp.int32
KS = 13
RADIUS = 6
ROWS = 32
COLS = 1024
CB = 128
NCB = COLS // CB
DEPTHS = 16
TILES = 32
SLOTS = 256
NEURONS = 8192
HALO = 24
WIN = 64
LIVE = WIN + 2 * HALO
ROW = DEPTHS
BLOCK = 16
DEEP = 32 * ROW
CAP = 384
LANES = CAP // CB
NEAR = 12
NAMES = SLOTS + 16
VMEM = pl.BlockSpec(memory_space=pltpu.VMEM)
SMEM = pl.BlockSpec(memory_space=pltpu.SMEM)


def call(kernel, outs, n_in, scalars=(), scratch=(), mib=24):
    return pl.pallas_call(
        kernel,
        out_shape=[jax.ShapeDtypeStruct(s, t) for s, t in outs],
        in_specs=[SMEM if i in scalars else VMEM for i in range(n_in)],
        out_specs=[VMEM] * len(outs),
        scratch_shapes=list(scratch),
        compiler_params=pltpu.CompilerParams(vmem_limit_bytes=mib * 2**20),
    )


def iota(shape, dim):
    return lax.broadcasted_iota(I32, shape, dim)


def split2(x):
    high = x.astype(BF16)
    return high, (x - high.astype(F32)).astype(BF16)


def split3(x):
    high = x.astype(BF16)
    rest = x - high.astype(F32)
    mid = rest.astype(BF16)
    return high, mid, (rest - mid.astype(F32)).astype(BF16)


def column_of(row):
    n = row.shape[1]
    return jnp.transpose(jnp.broadcast_to(row, (CB, n)))


def lane_sum(x):
    return jnp.sum(x, axis=1, keepdims=True)


def prepare_kernel(
    where, block, neuron, weights, owner, s_row,
    gram, q_row, q_col, b_col, a_row, a_lane, most,
):
    foot = weights[...]
    product = lax.dot_general(foot, foot, (((1,), (1,)), ((), ())), preferred_element_type=F32)
    blocks = column_of(block[...].astype(F32))
    same = jnp.concatenate([blocks, blocks], axis=1) == block[...].astype(F32)
    gram[...] = jnp.where(same, product, 0.0)
    b_col[...] = blocks.astype(I32)
    table = owner[...]
    number = iota((64, CB), 0) * CB + iota((64, CB), 1)
    own = jnp.zeros((16, CB), F32)
    for i in range(16):
        hit = jnp.sum(jnp.where(table == where[2] + i, number.astype(F32), 0.0), axis=0, keepdims=True)
        own = jnp.where(iota((16, CB), 0) == i, lane_sum(hit), own)
    names = jnp.concatenate([column_of(neuron[...].astype(F32)), own], axis=0).astype(I32)
    tile = s_row[...] >> 5
    tables = [tile, table >> 7, table & 127]
    tables = jnp.concatenate([x.astype(F32) for x in tables], axis=1).astype(BF16)
    hot = (iota((NAMES, 64), 1) == (names[:, :64] >> 7)).astype(F32).astype(BF16)
    found = jnp.dot(hot, tables, preferred_element_type=F32)
    lane_hot = iota((NAMES, CB), 1) == (names & 127)
    picked = [lane_sum(jnp.where(lane_hot, found[:, i * CB : (i + 1) * CB], 0.0)) for i in range(3)]
    n_tile = picked[0].astype(I32)
    place = jnp.broadcast_to(picked[1] * 128.0 + picked[2], (NAMES, CB))[:SLOTS]
    place = jnp.where(names[:SLOTS] >= 0, place, -1.0)
    q_col[...] = place.astype(I32)
    q_row[...] = jnp.transpose(place)[0:8, :].astype(I32)
    held = jnp.zeros((TILES, CB), F32)
    for r in range(64):
        here = lane_sum((iota((TILES, CB), 0) == tile[r : r + 1, :]).astype(F32))
        held = jnp.where(iota((TILES, CB), 1) == r, here, held)
    top = jnp.max(lane_sum(held), axis=0, keepdims=True)
    turns = jnp.zeros((1, 1), I32)
    for i in range((NEURONS + CAP - 1) // CAP):
        turns = turns + (top > i * CAP).astype(I32)
    most[...] = jnp.broadcast_to(turns, (8, CB))
    before = (iota((CB, CB), 0) < iota((CB, CB), 1)).astype(F32).astype(BF16)
    earlier = jnp.dot(held.astype(BF16), before, preferred_element_type=F32)
    row_hot = (iota((NAMES, CB), 1) == (names >> 7)).astype(F32).astype(BF16)
    counts = jnp.zeros((NAMES, TILES), F32)
    for part in split2(earlier):
        counts = counts + lax.dot_general(
            row_hot, part, (((1,), (1,)), ((), ())), preferred_element_type=F32
        )
    count = lane_sum(jnp.where(iota((NAMES, TILES), 1) == n_tile, counts, 0.0))
    inside = (found[:, :CB] == picked[0]) & (iota((NAMES, CB), 1) < (names & 127))
    count = count + lane_sum(jnp.where(inside, 1.0, 0.0))
    position = jnp.broadcast_to(count, (NAMES, CB)).astype(I32)
    turn = jnp.zeros((NAMES, CB), I32)
    for i in range(1, (NEURONS + CAP - 1) // CAP):
        turn = turn + (position >= i * CAP).astype(I32)
    a_row[...] = jnp.where(names >= 0, turn * TILES + n_tile, -1)
    a_lane[...] = position - turn * CAP


def lists_kernel(where, s_plane, s_row, s_col, rank, code, first):
    row, col = s_row[...], s_col[...]
    tile, window = row >> 5, col >> 6
    local = tile == where[1]
    mask = local.astype(F32)
    before = (iota((CB, CB), 0) < iota((CB, CB), 1)).astype(F32).astype(BF16)
    inside = jnp.dot(mask.astype(BF16), before, preferred_element_type=F32)
    rows = jnp.broadcast_to(lane_sum(mask), (64, CB)).astype(BF16)
    above = (iota((64, 64), 1) < iota((64, 64), 0)).astype(F32).astype(BF16)
    inside = inside + jnp.dot(above, rows, preferred_element_type=F32)
    order = jnp.where(local & (window == where[0]), inside, -1.0).astype(I32)
    spot = ((row >> 4) & 1) * WIN + (col & (WIN - 1))
    coded = ((row & 15) * ROW + s_plane[...]) * CB + spot
    rank[...] = order
    code[...] = coded
    first[...] = listed(order, coded, 0)


def listed(order, coded, start):
    place = order - start
    place = jnp.where(place < CAP, place, -1)
    total = jnp.zeros((32, CB), F32)
    for r in range(0, 64, 8):
        lines = [place[i : i + 1, :] for i in range(r, r + 8)]
        codes = [coded[i : i + 1, :] for i in range(r, r + 8)]
        left = []
        for at, code in zip(lines, codes):
            here = iota((8, CB), 0) == (at >> 7)
            left.append(
                jnp.concatenate(
                    [
                        jnp.where(here, (code >> 7).astype(F32), 0.0),
                        jnp.where(here, (code & 127).astype(F32), 0.0),
                        jnp.where(here, 1.0, 0.0),
                        jnp.zeros((8, CB), F32),
                    ],
                    axis=0,
                )
            )
        left = jnp.concatenate(left, axis=1).astype(BF16)
        right = [(iota((CB, CB), 0) == jnp.where(at >= 0, at & 127, -1)).astype(F32) for at in lines]
        right = jnp.concatenate(right, axis=1).astype(BF16)
        total = total + lax.dot_general(
            left, right, (((1,), (1,)), ((), ())), preferred_element_type=F32
        )
    value = total[0:8] * 128.0 + total[8:16]
    return jnp.where(total[16:24] > 0.0, value, -1.0).astype(I32)


def seed_values(codes, flat):
    parts = split3(flat)
    result = []
    for i in range(LANES):
        index = column_of(codes[i : i + 1, :].astype(F32)).astype(I32)
        key = jnp.concatenate([index, index], axis=1) >> 7
        hot = (iota((CB, 256), 1) == key).astype(F32).astype(BF16)
        found = jnp.dot(hot, parts[0], preferred_element_type=F32)
        found = found + jnp.dot(hot, parts[1], preferred_element_type=F32)
        found = found + jnp.dot(hot, parts[2], preferred_element_type=F32)
        picked = jnp.where(iota((CB, CB), 1) == (index & (CB - 1)), found, 0.0)
        result.append(jnp.sum(jnp.transpose(picked), axis=0, keepdims=True))
    result.append(jnp.zeros((8 - LANES, CB), F32))
    return jnp.concatenate(result, axis=0)


def window_kernel(volume, spread, windows):
    lane = iota((ROWS, CB), 1)
    taps = jnp.concatenate([spread[0].astype(F32), jnp.zeros((KS, CB - KS), F32)], axis=1)
    taps = jnp.concatenate([pltpu.roll(taps, LIVE, 1), jnp.zeros((ROWS - KS, CB), F32)], axis=0)
    zeros = jnp.zeros((ROWS, CB), F32)
    padded = jnp.concatenate([zeros, volume[0], zeros], axis=1)
    for j in range(DEPTHS):
        start = CB - HALO + WIN * j
        low = start // CB * CB
        moved = pltpu.roll(padded[:, low : low + 2 * CB], 2 * CB - start % CB, 1)[:, :CB]
        windows[j] = jnp.where(lane < LIVE, moved, taps)


def lane_shift(x, b):
    shift = (RADIUS - b) % CB
    return pltpu.roll(x, shift, 1) if shift else x


def forward(ahead, source, sums, blocks):
    result = []
    for m in range(0, blocks, 2):
        pair = range(m, min(m + 2, blocks))
        right = jnp.concatenate([source[i * 256 : i * 256 + DEEP, :] for i in pair], axis=1)
        value = jnp.dot(ahead[...], right, preferred_element_type=F32)
        for i in pair:
            at = (i - m) * CB
            sums[i - m] = value[:, at : at + CB]
        for i in pair:
            total = lane_shift(sums[i - m, pl.ds(0, BLOCK, stride=16), :], 0)
            for b in range(1, KS):
                total = total + lane_shift(sums[i - m, pl.ds(b, BLOCK, stride=16), :], b)
            result.append(total)
    return result


def open_kernel(
    where, parts, measured,
    own, sensor, down, up, ahead, behind, scale, image,
    wide, rounded, sums,
):
    lane = iota((ROW, CB), 1)
    rounded[: NEAR * ROW, :] = jnp.zeros((NEAR * ROW, CB), BF16)
    rounded[(NEAR + ROWS) * ROW :, :] = jnp.zeros(((NEAR + 8) * ROW, CB), BF16)
    for r in range(ROWS):
        line = jnp.where(lane < LIVE, parts[pl.ds(r, ROW, stride=ROWS), :], 0.0)
        own[r * ROW : (r + 1) * ROW, :] = line
        line = line.astype(BF16)
        rounded[(NEAR + r) * ROW : (NEAR + r + 1) * ROW, :] = line
        if r < NEAR:
            up[r * ROW : (r + 1) * ROW, :] = line
        if r >= ROWS - NEAR:
            at = (r - ROWS + NEAR) * ROW
            down[at : at + ROW, :] = line
    zeros = jnp.zeros((ROWS, CB), F32)
    wide[:, :CB] = zeros
    wide[:, CB : CB + COLS] = measured[...]
    wide[:, CB + COLS :] = zeros
    start = CB - HALO + WIN * where[0]
    low = pl.multiple_of((start >> 7) * CB, CB)
    moved = pltpu.roll(wide[:, pl.ds(low, 2 * CB)], 2 * CB - (start & (CB - 1)), 1)[:, :CB]
    view = jnp.where(iota((ROWS, CB), 1) < LIVE, moved, 0.0)
    sensor[...] = view
    taps = jnp.concatenate([parts[pl.ds(a, ROW, stride=ROWS), :] for a in range(16)], axis=0)
    taps = jnp.where(iota((256, CB), 1) >= LIVE, taps, 0.0)
    first = jnp.transpose(taps)[LIVE:, :]
    first = jnp.concatenate([first, jnp.zeros((16, 256), F32)], axis=1)
    for i in range(BLOCK):
        moved = pltpu.roll(first, i * ROW, 1) if i else first
        ahead[i * 16 : (i + 1) * 16, :] = moved.astype(BF16)
    lane = iota((CB, DEEP), 1)
    hot = (iota((CB, DEEP), 0) == LIVE + KS - 1 - (lane >> 5)).astype(F32).astype(BF16)
    spread = jnp.dot(taps.astype(BF16), hot, preferred_element_type=F32)
    inside = iota((ROW, DEEP), 1)
    within = jnp.where(inside < KS * 32, inside & 31, 32)
    second = jnp.zeros((ROW, DEEP), F32)
    for a in range(KS):
        second = jnp.where(within == KS - 1 - a, spread[a * ROW : (a + 1) * ROW], second)
    for i in range(BLOCK):
        moved = pltpu.roll(second, i, 1) if i else second
        behind[i * ROW : (i + 1) * ROW, :] = moved.astype(BF16)
    total = taps[:ROW]
    for a in range(1, KS):
        total = total + taps[a * ROW : (a + 1) * ROW]
    norm = jnp.sum(total, axis=1, keepdims=True)
    scale[...] = jnp.broadcast_to(1.0 / norm, (ROW, CB))
    image[...] = jnp.concatenate(forward(ahead, rounded, sums, 3), axis=0)
    for out, part, lines in (
        (up, view[:HALO], image[:HALO, :]),
        (down, view[ROWS - HALO :], image[20 : 20 + HALO, :]),
    ):
        rows = []
        for x in (part, lines):
            high = x.astype(BF16).astype(F32)
            rows += [high, x - high]
        out[NEAR * ROW :, :] = jnp.concatenate(rows, axis=0).astype(BF16)


def iterate_kernel(
    own, left, right, sensor, image, ahead, behind, scale, codes,
    sent, flat, exact, second, light, whole, sums, ratio, stack,
):
    near = NEAR * ROW
    exact[:near, :] = left[:near].astype(F32)
    exact[near : near + ROWS * ROW, :] = own[...]
    exact[near + ROWS * ROW : 2 * near + ROWS * ROW, :] = right[:near].astype(F32)
    exact[2 * near + ROWS * ROW :, :] = jnp.zeros((8 * ROW, CB), F32)
    before, after = left[near:].astype(F32), right[near:].astype(F32)
    light[:HALO, :] = before[:HALO] + before[HALO : 2 * HALO]
    light[HALO : HALO + ROWS, :] = sensor[...]
    light[HALO + ROWS : 2 * HALO + ROWS, :] = after[:HALO] + after[HALO : 2 * HALO]
    light[2 * HALO + ROWS :, :] = jnp.zeros((16, CB), F32)
    blank = jnp.zeros((20, CB), F32)
    total = jnp.concatenate([blank[:12], image[...], blank], axis=0)
    above = jnp.concatenate([before[2 * HALO : 3 * HALO] + before[3 * HALO :], jnp.zeros((56, CB), F32)], axis=0)
    below = after[2 * HALO : 3 * HALO] + after[3 * HALO :]
    below = jnp.concatenate([jnp.zeros((44, CB), F32), below, blank[:12]], axis=0)
    whole[...] = total + above + below
    for m in range(2):
        stack[m * DEEP + KS * 32 : (m + 1) * DEEP, :] = jnp.zeros((DEEP - KS * 32, 2 * CB), BF16)
    tall = jnp.concatenate([scale[...]] * BLOCK, axis=0)

    def divide(total, offset, valid):
        rows = total.shape[0]
        seen = light[offset : offset + rows, :]
        inside = (iota((rows, CB), 0) < valid) & (seen != 0.0) & (total != 0.0)
        ratio[:rows, :] = jnp.where(inside, seen / jnp.where(inside, total, 1.0), 0.0)

    def spread_back(blocks):
        height = 16 * blocks + 16
        for b in range(KS):
            moved = lane_shift(ratio[:height, :], b).astype(BF16)
            for m in range(blocks):
                at = (m // 2) * DEEP + b * 32
                stack[at : at + 32, (m % 2) * CB : (m % 2 + 1) * CB] = moved[m * 16 : m * 16 + 32]

    def back(m):
        value = jnp.dot(behind[...], stack[m * DEEP : (m + 1) * DEEP, :], preferred_element_type=F32)
        return value[:, :CB] * tall, value[:, CB:] * tall

    divide(whole[...], 6, 68)
    spread_back(4)
    factors = back(0) + back(1)
    for m in range(4):
        value = exact[m * 256 : (m + 1) * 256, :] * factors[m]
        exact[m * 256 : (m + 1) * 256, :] = value
        second[m * 256 : (m + 1) * 256, :] = value.astype(BF16)
    divide(jnp.concatenate(forward(ahead, second, sums, 3), axis=0), 18, 44)
    spread_back(2)
    factors = back(0)
    done = [exact[(m * 16 + 12) * ROW : (m * 16 + 28) * ROW, :] * factors[m] for m in range(2)]
    lane = iota((256, CB), 1)
    packed = jnp.where(lane < WIN, pltpu.roll(done[0], CB - HALO, 1), pltpu.roll(done[1], WIN - HALO, 1))
    flat[...] = packed
    values = seed_values(codes[...], packed)
    for p in range(DEPTHS):
        sent[p, 0:16, :] = flat[pl.ds(p, 16, stride=ROW), :]
        sent[p, 16:24, :] = values


def more_kernel(turn, rank, code, flat, sent):
    codes = listed(rank[...], code[...], turn[0] * CAP)
    values = seed_values(codes, flat[...])
    for p in range(DEPTHS):
        sent[p] = values


def gather_kernel(at):
    def kernel(parts, out):
        total = parts[0, at : at + 8, :]
        for j in range(1, DEPTHS):
            total = total + parts[j, at : at + 8, :]
        line = jnp.concatenate([total[i : i + 1, :] for i in range(LANES)], axis=1)
        for j in range(TILES):
            out[j] = line

    return kernel


def looked(turn, parts, a_row, a_lane):
    table = jnp.concatenate([parts[t] for t in range(TILES)], axis=0)
    row = a_row[...] - turn * TILES
    hot = (iota((NAMES, TILES), 1) == row[:, :TILES]).astype(F32).astype(BF16)
    parts = split3(table)
    found = jnp.dot(hot, parts[0], preferred_element_type=F32)
    found = found + jnp.dot(hot, parts[1], preferred_element_type=F32)
    found = found + jnp.dot(hot, parts[2], preferred_element_type=F32)
    total = jnp.zeros((NAMES, CB), F32)
    for i in range(LANES):
        here = iota((NAMES, CB), 1) + i * CB == a_lane[...]
        total = total + jnp.where(here, found[:, i * CB : (i + 1) * CB], 0.0)
    return jnp.broadcast_to(lane_sum(total), (NAMES, CB))


def look_kernel(turn, parts, a_row, a_lane, known, out):
    out[...] = known[...] + looked(turn[0], parts, a_row, a_lane)


def home_kernel(parts, weights, b_col, estimate, proj, lines):
    lane = iota((16, CB), 1)
    for c in range(NCB):
        a, b = parts[2 * c, :16, :], parts[2 * c + 1, :16, :]
        top = jnp.where(lane < WIN, a, pltpu.roll(b, WIN, 1))
        bottom = jnp.where(lane < WIN, pltpu.roll(a, WIN, 1), b)
        estimate[:16, c * CB : (c + 1) * CB] = top
        estimate[16:, c * CB : (c + 1) * CB] = bottom
        lines[c * ROWS : c * ROWS + 16, :] = top
        lines[c * ROWS + 16 : (c + 1) * ROWS, :] = bottom
    blocks = [lines[pl.ds(br, 64, stride=4), :] for br in range(4)]
    blocked = jnp.concatenate(blocks, axis=1)
    number = b_col[:, :64]
    number = (number & 7) * 8 + (number >> 3)
    hot = (iota((SLOTS, 64), 1) == number).astype(F32).astype(BF16)
    high, low = split2(blocked)
    picked = jnp.dot(hot, high, preferred_element_type=F32) + jnp.dot(hot, low, preferred_element_type=F32)
    product = weights[...].astype(F32) * picked
    total = product[:, :CB]
    for br in range(1, 4):
        total = total + product[:, br * CB : (br + 1) * CB]
    proj[...] = jnp.broadcast_to(jnp.sum(total, axis=1, keepdims=True), (SLOTS, CB))


def slots_kernel(parts, a_row, a_lane, known, gram, q_row, q_col, proj, out, own):
    start = known[...] + looked(0, parts, a_row, a_lane)
    padded = jnp.concatenate([start, jnp.zeros((3 * CB - NAMES, CB), F32)], axis=0)
    row = jnp.transpose(padded)[0:1, :]
    own[...] = row[:, SLOTS:]
    start_row = row[:, :SLOTS]
    terms = gram[...] * start_row
    over = jnp.sum(terms[:, :CB] + terms[:, CB:], axis=1, keepdims=True)
    place = q_col[...]
    lane = iota((SLOTS, CB), 1)
    target = ((place >> 5) & 3) * 32 + (place & 15)
    sent = jnp.where(lane == target, proj[...], 0.0) + jnp.where(lane == target + 16, over, 0.0)
    spot = q_row[0:1, :]
    line = ((spot >> 9) * 2 + ((spot >> 4) & 1)) * 4 + ((spot >> 7) & 3)
    row_hot = (iota((CB, SLOTS), 0) == jnp.where(spot >= 0, line, -1)).astype(F32).astype(BF16)
    parts = split3(sent)
    dense = jnp.dot(row_hot, parts[0], preferred_element_type=F32)
    dense = dense + jnp.dot(row_hot, parts[1], preferred_element_type=F32)
    dense = dense + jnp.dot(row_hot, parts[2], preferred_element_type=F32)
    for j in range(TILES):
        out[j] = dense[j * 4 : (j + 1) * 4]


def fold_kernel(parts, out):
    total = parts[0]
    for j in range(1, TILES):
        total = total + parts[j]
    total = jnp.concatenate([total, total], axis=0)
    for m in range(4):
        moved = pltpu.roll(total, (CB - 32 * m) % CB, 1) if m else total
        for r in range(4):
            out[4 * r + m] = moved[r : r + 1]


def final_kernel(parts, own, out):
    total = parts[0]
    for j in range(1, TILES // 2):
        total = total + parts[j]
    over = pltpu.roll(total, CB - 16, 1)
    initial = own[...]
    real = iota((1, CB), 1) < 16
    bottom = jnp.where(real, over + 100.0 * initial, 1.0)
    out[...] = jnp.where(real, initial * total, 0.0) / bottom


def swap(pieces, axis, groups=None):
    return lax.all_to_all(pieces, axis, 0, 0, axis_index_groups=groups)


def body(
    volume,
    measured,
    point_spread,
    entry_block,
    entry_neuron,
    footprints,
    seed_plane,
    seed_row,
    seed_col,
    owner_slot,
):
    d = lax.axis_index("depth")
    t = lax.axis_index("tile")
    where = jnp.stack([d, t, (d * TILES + t) * 16]).astype(I32)
    [windows] = call(window_kernel, [((DEPTHS, ROWS, CB), F32)], 2)(volume, point_spread)
    windows, where = lax.optimization_barrier((windows, where))
    tied = (swap(windows, "depth"), where, measured, entry_block, entry_neuron, footprints, owner_slot)
    tied = lax.optimization_barrier(tied + (seed_plane, seed_row, seed_col))
    parts, where, measured, entry_block, entry_neuron, footprints, owner_slot = tied[:7]
    seed_plane, seed_row, seed_col = tied[7:]
    parts = parts.reshape(DEPTHS * ROWS, CB)
    table = owner_slot.reshape(64, CB)
    message = ((NEAR * ROW + 4 * HALO, CB), BF16)
    band = ((256, DEEP), BF16)
    own, sensor, down, up, ahead, behind, scale, image = call(
        open_kernel,
        [((ROWS * ROW, CB), F32), ((ROWS, CB), F32), message, message, band, band, ((ROW, CB), F32), ((48, CB), F32)],
        3,
        scalars=(0,),
        scratch=[
            pltpu.VMEM((ROWS, COLS + 2 * CB), F32),
            pltpu.VMEM((64 * ROW, CB), BF16),
            pltpu.VMEM((2, 256, CB), F32),
        ],
    )(where, parts, measured)
    left = lax.ppermute(down, "tile", [(i, i + 1) for i in range(TILES - 1)])
    right = lax.ppermute(up, "tile", [(i + 1, i) for i in range(TILES - 1)])
    lines = [x.reshape(64, CB) for x in (seed_plane, seed_row, seed_col)]
    square = ((64, CB), I32)
    rank, code, first = call(lists_kernel, [square, square, ((8, CB), I32)], 4, scalars=(0,))(where, *lines)
    sent, flat = call(
        iterate_kernel,
        [((DEPTHS, 24, CB), F32), ((256, CB), F32)],
        9,
        scratch=[
            pltpu.VMEM((64 * ROW, CB), F32),
            pltpu.VMEM((64 * ROW, CB), BF16),
            pltpu.VMEM((96, CB), F32),
            pltpu.VMEM((80, CB), F32),
            pltpu.VMEM((2, 256, CB), F32),
            pltpu.VMEM((80, CB), F32),
            pltpu.VMEM((2 * DEEP, 2 * CB), BF16),
        ],
    )(own, left, right, sensor, image, ahead, behind, scale, first)
    later = (swap(sent, "depth"), entry_block, entry_neuron, table, lines[1])
    parts, entry_block, entry_neuron, table, seed_rows = lax.optimization_barrier(later)
    weights = footprints[0].reshape(SLOTS, 512)
    column = ((SLOTS, CB), I32)
    names = ((NAMES, CB), I32)
    gram, q_row, q_col, b_col, a_row, a_lane, most = call(
        prepare_kernel,
        [((SLOTS, SLOTS), F32), ((8, SLOTS), I32), column, column, names, names, ((8, CB), I32)],
        6,
        scalars=(0,),
    )(where, entry_block, entry_neuron, weights, table, seed_rows)

    def share(values, at):
        [values] = call(gather_kernel(at), [((TILES, 1, CAP), F32)], 1)(values)
        return swap(values, "tile")

    def look(turn, values, known):
        return call(look_kernel, [((NAMES, CB), F32)], 5, scalars=(0,))(
            turn, values, a_row, a_lane, known
        )[0]

    def another(step, known):
        turn = jnp.reshape(step, (1,))
        [values] = call(more_kernel, [((DEPTHS, 8, CB), F32)], 4, scalars=(0,))(
            turn, rank, code, flat
        )
        return look(turn, share(swap(values, "depth"), 0), known)

    rounds = jnp.minimum(most[0, 0], (NEURONS + CAP - 1) // CAP)
    shared, none = lax.optimization_barrier((share(parts, 16), jnp.zeros((NAMES, CB), F32)))
    known = lax.fori_loop(1, rounds, another, none)
    estimate, proj = call(
        home_kernel,
        [((ROWS, COLS), F32), ((SLOTS, CB), F32)],
        3,
        scratch=[pltpu.VMEM((NCB * ROWS, CB), F32)],
    )(parts, weights, b_col)
    sent, own = call(slots_kernel, [((TILES, 4, CB), F32), ((1, CB), F32)], 8)(
        shared, a_row, a_lane, known, gram, q_row, q_col, proj
    )
    pairs = TILES // 2
    near = [[d * TILES + 2 * z + x for d in range(DEPTHS) for x in range(2)] for z in range(pairs)]
    far = [[2 * z + x for z in range(pairs)] for x in range(2)]
    sent = swap(sent, ("depth", "tile"), near)
    [sent] = call(fold_kernel, [((pairs, 1, CB), F32)], 1)(sent)
    [demixed] = call(final_kernel, [((1, CB), F32)], 2)(swap(sent, "tile", far), own)
    return estimate[None], demixed[0, :16]


def solution(mesh):
    in_specs = (
        P("depth", "tile", None),
        P("tile", None),
        P("depth", None, None),
        P("tile", "depth"),
        P("tile", "depth"),
        P("tile", "depth", None, None),
        P(),
        P(),
        P(),
        P(),
    )
    out_specs = (P("depth", "tile", None), P(("depth", "tile")))
    return jax.shard_map(body, mesh=mesh, in_specs=in_specs, out_specs=out_specs, check_vma=False)
```

```python
import jax
import jax.numpy as jnp
from jax import lax
from jax.experimental import pallas as pl
from jax.experimental.pallas import tpu as pltpu
from jax.sharding import PartitionSpec as P

F32 = jnp.float32
BF16 = jnp.bfloat16
I32 = jnp.int32
KS = 13
RADIUS = 6
ROWS = 32
COLS = 1024
CB = 128
NCB = COLS // CB
DEPTHS = 16
TILES = 32
SLOTS = 256
NEURONS = 8192
HALO = 24
WIN = 64
LIVE = WIN + 2 * HALO
ROW = DEPTHS
BLOCK = 16
DEEP = 32 * ROW
CAP = 384
LANES = CAP // CB
NEAR = 12
NAMES = SLOTS + 16
VMEM = pl.BlockSpec(memory_space=pltpu.VMEM)
SMEM = pl.BlockSpec(memory_space=pltpu.SMEM)


def call(kernel, outs, n_in, scalars=(), scratch=(), mib=24):
    return pl.pallas_call(
        kernel,
        out_shape=[jax.ShapeDtypeStruct(s, t) for s, t in outs],
        in_specs=[SMEM if i in scalars else VMEM for i in range(n_in)],
        out_specs=[VMEM] * len(outs),
        scratch_shapes=list(scratch),
        compiler_params=pltpu.CompilerParams(vmem_limit_bytes=mib * 2**20),
    )


def iota(shape, dim):
    return lax.broadcasted_iota(I32, shape, dim)


def split2(x):
    high = x.astype(BF16)
    return high, (x - high.astype(F32)).astype(BF16)


def split3(x):
    high = x.astype(BF16)
    rest = x - high.astype(F32)
    mid = rest.astype(BF16)
    return high, mid, (rest - mid.astype(F32)).astype(BF16)


def column_of(row):
    n = row.shape[1]
    return jnp.transpose(jnp.broadcast_to(row, (CB, n)))


def lane_sum(x):
    return jnp.sum(x, axis=1, keepdims=True)


def prepare_kernel(
    where, block, neuron, weights, owner, s_plane, s_row, s_col,
    gram, q_row, q_col, b_col, a_row, a_lane, rank, code, first, most,
):
    foot = weights[...]
    product = lax.dot_general(foot, foot, (((1,), (1,)), ((), ())), preferred_element_type=F32)
    blocks = column_of(block[...].astype(F32))
    same = jnp.concatenate([blocks, blocks], axis=1) == block[...].astype(F32)
    gram[...] = jnp.where(same, product, 0.0)
    b_col[...] = blocks.astype(I32)
    table = owner[...]
    number = iota((64, CB), 0) * CB + iota((64, CB), 1)
    own = jnp.zeros((16, CB), F32)
    for i in range(16):
        hit = jnp.sum(jnp.where(table == where[2] + i, number.astype(F32), 0.0), axis=0, keepdims=True)
        own = jnp.where(iota((16, CB), 0) == i, lane_sum(hit), own)
    names = jnp.concatenate([column_of(neuron[...].astype(F32)), own], axis=0).astype(I32)
    row, col = s_row[...], s_col[...]
    tile, window = row >> 5, col >> 6
    tables = [tile, table >> 7, table & 127]
    tables = jnp.concatenate([x.astype(F32) for x in tables], axis=1).astype(BF16)
    hot = (iota((NAMES, 64), 1) == (names[:, :64] >> 7)).astype(F32).astype(BF16)
    found = jnp.dot(hot, tables, preferred_element_type=F32)
    lane_hot = iota((NAMES, CB), 1) == (names & 127)
    picked = [lane_sum(jnp.where(lane_hot, found[:, i * CB : (i + 1) * CB], 0.0)) for i in range(3)]
    n_tile = picked[0].astype(I32)
    place = jnp.broadcast_to(picked[1] * 128.0 + picked[2], (NAMES, CB))[:SLOTS]
    place = jnp.where(names[:SLOTS] >= 0, place, -1.0)
    q_col[...] = place.astype(I32)
    q_row[...] = jnp.transpose(place)[0:8, :].astype(I32)
    held = jnp.zeros((TILES, CB), F32)
    for r in range(64):
        here = lane_sum((iota((TILES, CB), 0) == tile[r : r + 1, :]).astype(F32))
        held = jnp.where(iota((TILES, CB), 1) == r, here, held)
    top = jnp.max(lane_sum(held), axis=0, keepdims=True)
    most[...] = jnp.broadcast_to(top, (8, CB)).astype(I32)
    before = (iota((CB, CB), 0) < iota((CB, CB), 1)).astype(F32).astype(BF16)
    earlier = jnp.dot(held.astype(BF16), before, preferred_element_type=F32)
    row_hot = (iota((NAMES, CB), 1) == (names >> 7)).astype(F32).astype(BF16)
    counts = jnp.zeros((NAMES, TILES), F32)
    for part in split2(earlier):
        counts = counts + lax.dot_general(
            row_hot, part, (((1,), (1,)), ((), ())), preferred_element_type=F32
        )
    count = lane_sum(jnp.where(iota((NAMES, TILES), 1) == n_tile, counts, 0.0))
    inside = (found[:, :CB] == picked[0]) & (iota((NAMES, CB), 1) < (names & 127))
    count = count + lane_sum(jnp.where(inside, 1.0, 0.0))
    position = jnp.broadcast_to(count, (NAMES, CB)).astype(I32)
    turn = jnp.zeros((NAMES, CB), I32)
    for i in range(1, (NEURONS + CAP - 1) // CAP):
        turn = turn + (position >= i * CAP).astype(I32)
    a_row[...] = jnp.where(names >= 0, turn * TILES + n_tile, -1)
    a_lane[...] = position - turn * CAP
    local = tile == where[1]
    mask = local.astype(F32)
    before = (iota((CB, CB), 0) < iota((CB, CB), 1)).astype(F32).astype(BF16)
    inside = jnp.dot(mask.astype(BF16), before, preferred_element_type=F32)
    rows = jnp.broadcast_to(lane_sum(mask), (64, CB)).astype(BF16)
    above = (iota((64, 64), 1) < iota((64, 64), 0)).astype(F32).astype(BF16)
    inside = inside + jnp.dot(above, rows, preferred_element_type=F32)
    order = jnp.where(local & (window == where[0]), inside, -1.0).astype(I32)
    spot = ((row >> 4) & 1) * WIN + (col & (WIN - 1))
    coded = ((row & 15) * ROW + s_plane[...]) * CB + spot
    rank[...] = order
    code[...] = coded
    first[...] = listed(order, coded, 0)


def listed(order, coded, start):
    place = order - start
    place = jnp.where(place < CAP, place, -1)
    total = jnp.zeros((32, CB), F32)
    for r in range(0, 64, 8):
        lines = [place[i : i + 1, :] for i in range(r, r + 8)]
        codes = [coded[i : i + 1, :] for i in range(r, r + 8)]
        left = []
        for at, code in zip(lines, codes):
            here = iota((8, CB), 0) == (at >> 7)
            left.append(
                jnp.concatenate(
                    [
                        jnp.where(here, (code >> 7).astype(F32), 0.0),
                        jnp.where(here, (code & 127).astype(F32), 0.0),
                        jnp.where(here, 1.0, 0.0),
                        jnp.zeros((8, CB), F32),
                    ],
                    axis=0,
                )
            )
        left = jnp.concatenate(left, axis=1).astype(BF16)
        right = [(iota((CB, CB), 0) == jnp.where(at >= 0, at & 127, -1)).astype(F32) for at in lines]
        right = jnp.concatenate(right, axis=1).astype(BF16)
        total = total + lax.dot_general(
            left, right, (((1,), (1,)), ((), ())), preferred_element_type=F32
        )
    value = total[0:8] * 128.0 + total[8:16]
    return jnp.where(total[16:24] > 0.0, value, -1.0).astype(I32)


def seed_values(codes, flat):
    parts = split3(flat)
    result = []
    for i in range(LANES):
        index = column_of(codes[i : i + 1, :].astype(F32)).astype(I32)
        key = jnp.concatenate([index, index], axis=1) >> 7
        hot = (iota((CB, 256), 1) == key).astype(F32).astype(BF16)
        found = jnp.dot(hot, parts[0], preferred_element_type=F32)
        found = found + jnp.dot(hot, parts[1], preferred_element_type=F32)
        found = found + jnp.dot(hot, parts[2], preferred_element_type=F32)
        picked = jnp.where(iota((CB, CB), 1) == (index & (CB - 1)), found, 0.0)
        result.append(jnp.sum(jnp.transpose(picked), axis=0, keepdims=True))
    result.append(jnp.zeros((8 - LANES, CB), F32))
    return jnp.concatenate(result, axis=0)


def window_kernel(volume, spread, windows):
    lane = iota((ROWS, CB), 1)
    taps = jnp.concatenate([spread[0].astype(F32), jnp.zeros((KS, CB - KS), F32)], axis=1)
    taps = jnp.concatenate([pltpu.roll(taps, LIVE, 1), jnp.zeros((ROWS - KS, CB), F32)], axis=0)
    zeros = jnp.zeros((ROWS, CB), F32)
    padded = jnp.concatenate([zeros, volume[0], zeros], axis=1)
    for j in range(DEPTHS):
        start = CB - HALO + WIN * j
        low = start // CB * CB
        moved = pltpu.roll(padded[:, low : low + 2 * CB], 2 * CB - start % CB, 1)[:, :CB]
        windows[j] = jnp.where(lane < LIVE, moved, taps)


def lane_shift(x, b):
    shift = (RADIUS - b) % CB
    return pltpu.roll(x, shift, 1) if shift else x


def forward(ahead, source, sums, blocks):
    result = []
    for m in range(0, blocks, 2):
        pair = range(m, min(m + 2, blocks))
        right = jnp.concatenate([source[i * 256 : i * 256 + DEEP, :] for i in pair], axis=1)
        value = jnp.dot(ahead[...], right, preferred_element_type=F32)
        for i in pair:
            at = (i - m) * CB
            sums[i - m] = value[:, at : at + CB]
        for i in pair:
            total = lane_shift(sums[i - m, pl.ds(0, BLOCK, stride=16), :], 0)
            for b in range(1, KS):
                total = total + lane_shift(sums[i - m, pl.ds(b, BLOCK, stride=16), :], b)
            result.append(total)
    return result


def open_kernel(
    where, parts, measured,
    own, sensor, down, up, ahead, behind, scale, image,
    wide, rounded, sums,
):
    lane = iota((ROW, CB), 1)
    rounded[: NEAR * ROW, :] = jnp.zeros((NEAR * ROW, CB), BF16)
    rounded[(NEAR + ROWS) * ROW :, :] = jnp.zeros(((NEAR + 8) * ROW, CB), BF16)
    for r in range(ROWS):
        line = jnp.where(lane < LIVE, parts[pl.ds(r, ROW, stride=ROWS), :], 0.0)
        own[r * ROW : (r + 1) * ROW, :] = line
        line = line.astype(BF16)
        rounded[(NEAR + r) * ROW : (NEAR + r + 1) * ROW, :] = line
        if r < NEAR:
            up[r * ROW : (r + 1) * ROW, :] = line
        if r >= ROWS - NEAR:
            at = (r - ROWS + NEAR) * ROW
            down[at : at + ROW, :] = line
    zeros = jnp.zeros((ROWS, CB), F32)
    wide[:, :CB] = zeros
    wide[:, CB : CB + COLS] = measured[...]
    wide[:, CB + COLS :] = zeros
    start = CB - HALO + WIN * where[0]
    low = pl.multiple_of((start >> 7) * CB, CB)
    moved = pltpu.roll(wide[:, pl.ds(low, 2 * CB)], 2 * CB - (start & (CB - 1)), 1)[:, :CB]
    view = jnp.where(iota((ROWS, CB), 1) < LIVE, moved, 0.0)
    sensor[...] = view
    taps = jnp.concatenate([parts[pl.ds(a, ROW, stride=ROWS), :] for a in range(16)], axis=0)
    taps = jnp.where(iota((256, CB), 1) >= LIVE, taps, 0.0)
    first = jnp.transpose(taps)[LIVE:, :]
    first = jnp.concatenate([first, jnp.zeros((16, 256), F32)], axis=1)
    for i in range(BLOCK):
        moved = pltpu.roll(first, i * ROW, 1) if i else first
        ahead[i * 16 : (i + 1) * 16, :] = moved.astype(BF16)
    lane = iota((CB, DEEP), 1)
    hot = (iota((CB, DEEP), 0) == LIVE + KS - 1 - (lane >> 5)).astype(F32).astype(BF16)
    spread = jnp.dot(taps.astype(BF16), hot, preferred_element_type=F32)
    inside = iota((ROW, DEEP), 1)
    within = jnp.where(inside < KS * 32, inside & 31, 32)
    second = jnp.zeros((ROW, DEEP), F32)
    for a in range(KS):
        second = jnp.where(within == KS - 1 - a, spread[a * ROW : (a + 1) * ROW], second)
    for i in range(BLOCK):
        moved = pltpu.roll(second, i, 1) if i else second
        behind[i * ROW : (i + 1) * ROW, :] = moved.astype(BF16)
    total = taps[:ROW]
    for a in range(1, KS):
        total = total + taps[a * ROW : (a + 1) * ROW]
    norm = jnp.sum(total, axis=1, keepdims=True)
    scale[...] = jnp.broadcast_to(1.0 / norm, (ROW, CB))
    image[...] = jnp.concatenate(forward(ahead, rounded, sums, 3), axis=0)
    for out, part, lines in (
        (up, view[:HALO], image[:HALO, :]),
        (down, view[ROWS - HALO :], image[20 : 20 + HALO, :]),
    ):
        rows = []
        for x in (part, lines):
            high = x.astype(BF16).astype(F32)
            rows += [high, x - high]
        out[NEAR * ROW :, :] = jnp.concatenate(rows, axis=0).astype(BF16)


def iterate_kernel(
    own, left, right, sensor, image, ahead, behind, scale, codes,
    sent, flat, exact, second, light, whole, sums, ratio, stack,
):
    near = NEAR * ROW
    exact[:near, :] = left[:near].astype(F32)
    exact[near : near + ROWS * ROW, :] = own[...]
    exact[near + ROWS * ROW : 2 * near + ROWS * ROW, :] = right[:near].astype(F32)
    exact[2 * near + ROWS * ROW :, :] = jnp.zeros((8 * ROW, CB), F32)
    before, after = left[near:].astype(F32), right[near:].astype(F32)
    light[:HALO, :] = before[:HALO] + before[HALO : 2 * HALO]
    light[HALO : HALO + ROWS, :] = sensor[...]
    light[HALO + ROWS : 2 * HALO + ROWS, :] = after[:HALO] + after[HALO : 2 * HALO]
    light[2 * HALO + ROWS :, :] = jnp.zeros((16, CB), F32)
    blank = jnp.zeros((20, CB), F32)
    total = jnp.concatenate([blank[:12], image[...], blank], axis=0)
    above = jnp.concatenate([before[2 * HALO : 3 * HALO] + before[3 * HALO :], jnp.zeros((56, CB), F32)], axis=0)
    below = after[2 * HALO : 3 * HALO] + after[3 * HALO :]
    below = jnp.concatenate([jnp.zeros((44, CB), F32), below, blank[:12]], axis=0)
    whole[...] = total + above + below
    for m in range(2):
        stack[m * DEEP + KS * 32 : (m + 1) * DEEP, :] = jnp.zeros((DEEP - KS * 32, 2 * CB), BF16)
    tall = jnp.concatenate([scale[...]] * BLOCK, axis=0)

    def divide(total, offset, valid):
        rows = total.shape[0]
        seen = light[offset : offset + rows, :]
        inside = (iota((rows, CB), 0) < valid) & (seen != 0.0) & (total != 0.0)
        ratio[:rows, :] = jnp.where(inside, seen / jnp.where(inside, total, 1.0), 0.0)

    def spread_back(blocks):
        height = 16 * blocks + 16
        for b in range(KS):
            moved = lane_shift(ratio[:height, :], b).astype(BF16)
            for m in range(blocks):
                at = (m // 2) * DEEP + b * 32
                stack[at : at + 32, (m % 2) * CB : (m % 2 + 1) * CB] = moved[m * 16 : m * 16 + 32]

    def back(m):
        value = jnp.dot(behind[...], stack[m * DEEP : (m + 1) * DEEP, :], preferred_element_type=F32)
        return value[:, :CB] * tall, value[:, CB:] * tall

    divide(whole[...], 6, 68)
    spread_back(4)
    factors = back(0) + back(1)
    for m in range(4):
        value = exact[m * 256 : (m + 1) * 256, :] * factors[m]
        exact[m * 256 : (m + 1) * 256, :] = value
        second[m * 256 : (m + 1) * 256, :] = value.astype(BF16)
    divide(jnp.concatenate(forward(ahead, second, sums, 3), axis=0), 18, 44)
    spread_back(2)
    factors = back(0)
    done = [exact[(m * 16 + 12) * ROW : (m * 16 + 28) * ROW, :] * factors[m] for m in range(2)]
    lane = iota((256, CB), 1)
    packed = jnp.where(lane < WIN, pltpu.roll(done[0], CB - HALO, 1), pltpu.roll(done[1], WIN - HALO, 1))
    flat[...] = packed
    values = seed_values(codes[...], packed)
    for p in range(DEPTHS):
        sent[p, 0:16, :] = flat[pl.ds(p, 16, stride=ROW), :]
        sent[p, 16:24, :] = values


def more_kernel(turn, rank, code, flat, sent):
    codes = listed(rank[...], code[...], turn[0] * CAP)
    values = seed_values(codes, flat[...])
    for p in range(DEPTHS):
        sent[p] = values


def gather_kernel(at):
    def kernel(parts, out):
        total = parts[0, at : at + 8, :]
        for j in range(1, DEPTHS):
            total = total + parts[j, at : at + 8, :]
        line = jnp.concatenate([total[i : i + 1, :] for i in range(LANES)], axis=1)
        for j in range(TILES):
            out[j] = line

    return kernel


def looked(turn, parts, a_row, a_lane):
    table = jnp.concatenate([parts[t] for t in range(TILES)], axis=0)
    row = a_row[...] - turn * TILES
    hot = (iota((NAMES, TILES), 1) == row[:, :TILES]).astype(F32).astype(BF16)
    parts = split3(table)
    found = jnp.dot(hot, parts[0], preferred_element_type=F32)
    found = found + jnp.dot(hot, parts[1], preferred_element_type=F32)
    found = found + jnp.dot(hot, parts[2], preferred_element_type=F32)
    total = jnp.zeros((NAMES, CB), F32)
    for i in range(LANES):
        here = iota((NAMES, CB), 1) + i * CB == a_lane[...]
        total = total + jnp.where(here, found[:, i * CB : (i + 1) * CB], 0.0)
    return jnp.broadcast_to(lane_sum(total), (NAMES, CB))


def look_kernel(turn, parts, a_row, a_lane, known, out):
    out[...] = known[...] + looked(turn[0], parts, a_row, a_lane)


def home_kernel(parts, weights, b_col, estimate, proj, lines):
    lane = iota((16, CB), 1)
    for c in range(NCB):
        a, b = parts[2 * c, :16, :], parts[2 * c + 1, :16, :]
        top = jnp.where(lane < WIN, a, pltpu.roll(b, WIN, 1))
        bottom = jnp.where(lane < WIN, pltpu.roll(a, WIN, 1), b)
        estimate[:16, c * CB : (c + 1) * CB] = top
        estimate[16:, c * CB : (c + 1) * CB] = bottom
        lines[c * ROWS : c * ROWS + 16, :] = top
        lines[c * ROWS + 16 : (c + 1) * ROWS, :] = bottom
    blocks = [lines[pl.ds(br, 64, stride=4), :] for br in range(4)]
    blocked = jnp.concatenate(blocks, axis=1)
    number = b_col[:, :64]
    number = (number & 7) * 8 + (number >> 3)
    hot = (iota((SLOTS, 64), 1) == number).astype(F32).astype(BF16)
    high, low = split2(blocked)
    picked = jnp.dot(hot, high, preferred_element_type=F32) + jnp.dot(hot, low, preferred_element_type=F32)
    product = weights[...].astype(F32) * picked
    total = product[:, :CB]
    for br in range(1, 4):
        total = total + product[:, br * CB : (br + 1) * CB]
    proj[...] = jnp.broadcast_to(jnp.sum(total, axis=1, keepdims=True), (SLOTS, CB))


def slots_kernel(parts, a_row, a_lane, known, gram, q_row, q_col, proj, out, own):
    start = known[...] + looked(0, parts, a_row, a_lane)
    padded = jnp.concatenate([start, jnp.zeros((3 * CB - NAMES, CB), F32)], axis=0)
    row = jnp.transpose(padded)[0:1, :]
    own[...] = row[:, SLOTS:]
    start_row = row[:, :SLOTS]
    terms = gram[...] * start_row
    over = jnp.sum(terms[:, :CB] + terms[:, CB:], axis=1, keepdims=True)
    place = q_col[...]
    lane = iota((SLOTS, CB), 1)
    target = ((place >> 5) & 3) * 32 + (place & 15)
    sent = jnp.where(lane == target, proj[...], 0.0) + jnp.where(lane == target + 16, over, 0.0)
    spot = q_row[0:1, :]
    line = ((spot >> 9) * 2 + ((spot >> 4) & 1)) * 4 + ((spot >> 7) & 3)
    row_hot = (iota((CB, SLOTS), 0) == jnp.where(spot >= 0, line, -1)).astype(F32).astype(BF16)
    parts = split3(sent)
    dense = jnp.dot(row_hot, parts[0], preferred_element_type=F32)
    dense = dense + jnp.dot(row_hot, parts[1], preferred_element_type=F32)
    dense = dense + jnp.dot(row_hot, parts[2], preferred_element_type=F32)
    for j in range(TILES):
        out[j] = dense[j * 4 : (j + 1) * 4]


def fold_kernel(parts, out):
    total = parts[0]
    for j in range(1, TILES):
        total = total + parts[j]
    total = jnp.concatenate([total, total], axis=0)
    for m in range(4):
        moved = pltpu.roll(total, (CB - 32 * m) % CB, 1) if m else total
        for r in range(4):
            out[4 * r + m] = moved[r : r + 1]


def final_kernel(parts, own, out):
    total = parts[0]
    for j in range(1, TILES // 2):
        total = total + parts[j]
    over = pltpu.roll(total, CB - 16, 1)
    initial = own[...]
    real = iota((1, CB), 1) < 16
    bottom = jnp.where(real, over + 100.0 * initial, 1.0)
    out[...] = jnp.where(real, initial * total, 0.0) / bottom


def swap(pieces, axis, groups=None):
    return lax.all_to_all(pieces, axis, 0, 0, axis_index_groups=groups)


def body(
    volume,
    measured,
    point_spread,
    entry_block,
    entry_neuron,
    footprints,
    seed_plane,
    seed_row,
    seed_col,
    owner_slot,
):
    d = lax.axis_index("depth")
    t = lax.axis_index("tile")
    where = jnp.stack([d, t, (d * TILES + t) * 16]).astype(I32)
    [windows] = call(window_kernel, [((DEPTHS, ROWS, CB), F32)], 2)(volume, point_spread)
    windows, where = lax.optimization_barrier((windows, where))
    tied = (swap(windows, "depth"), where, measured, entry_block, entry_neuron, footprints, owner_slot)
    tied = lax.optimization_barrier(tied + (seed_plane, seed_row, seed_col))
    parts, where, measured, entry_block, entry_neuron, footprints, owner_slot = tied[:7]
    seed_plane, seed_row, seed_col = tied[7:]
    parts = parts.reshape(DEPTHS * ROWS, CB)
    table = owner_slot.reshape(64, CB)
    message = ((NEAR * ROW + 4 * HALO, CB), BF16)
    band = ((256, DEEP), BF16)
    own, sensor, down, up, ahead, behind, scale, image = call(
        open_kernel,
        [((ROWS * ROW, CB), F32), ((ROWS, CB), F32), message, message, band, band, ((ROW, CB), F32), ((48, CB), F32)],
        3,
        scalars=(0,),
        scratch=[
            pltpu.VMEM((ROWS, COLS + 2 * CB), F32),
            pltpu.VMEM((64 * ROW, CB), BF16),
            pltpu.VMEM((2, 256, CB), F32),
        ],
    )(where, parts, measured)
    left = lax.ppermute(down, "tile", [(i, i + 1) for i in range(TILES - 1)])
    right = lax.ppermute(up, "tile", [(i + 1, i) for i in range(TILES - 1)])
    weights = footprints[0].reshape(SLOTS, 512)
    column = ((SLOTS, CB), I32)
    names = ((NAMES, CB), I32)
    square = ((64, CB), I32)
    gram, q_row, q_col, b_col, a_row, a_lane, rank, code, first, most = call(
        prepare_kernel,
        [
            ((SLOTS, SLOTS), F32),
            ((8, SLOTS), I32),
            column,
            column,
            names,
            names,
            square,
            square,
            ((8, CB), I32),
            ((8, CB), I32),
        ],
        8,
        scalars=(0,),
    )(
        where,
        entry_block,
        entry_neuron,
        weights,
        table,
        seed_plane.reshape(64, CB),
        seed_row.reshape(64, CB),
        seed_col.reshape(64, CB),
    )
    sent, flat = call(
        iterate_kernel,
        [((DEPTHS, 24, CB), F32), ((256, CB), F32)],
        9,
        scratch=[
            pltpu.VMEM((64 * ROW, CB), F32),
            pltpu.VMEM((64 * ROW, CB), BF16),
            pltpu.VMEM((96, CB), F32),
            pltpu.VMEM((80, CB), F32),
            pltpu.VMEM((2, 256, CB), F32),
            pltpu.VMEM((80, CB), F32),
            pltpu.VMEM((2 * DEEP, 2 * CB), BF16),
        ],
    )(own, left, right, sensor, image, ahead, behind, scale, first)
    parts, most = lax.optimization_barrier((swap(sent, "depth"), most))

    def share(values, at):
        [values] = call(gather_kernel(at), [((TILES, 1, CAP), F32)], 1)(values)
        return swap(values, "tile")

    def look(turn, values, known):
        return call(look_kernel, [((NAMES, CB), F32)], 5, scalars=(0,))(
            turn, values, a_row, a_lane, known
        )[0]

    def another(step, known):
        turn = jnp.reshape(step, (1,))
        [values] = call(more_kernel, [((DEPTHS, 8, CB), F32)], 4, scalars=(0,))(
            turn, rank, code, flat
        )
        return look(turn, share(swap(values, "depth"), 0), known)

    rounds = (most[0, 0] + CAP - 1) // CAP
    shared, none = lax.optimization_barrier((share(parts, 16), jnp.zeros((NAMES, CB), F32)))
    known = lax.fori_loop(1, rounds, another, none)
    estimate, proj = call(
        home_kernel,
        [((ROWS, COLS), F32), ((SLOTS, CB), F32)],
        3,
        scratch=[pltpu.VMEM((NCB * ROWS, CB), F32)],
    )(parts, weights, b_col)
    sent, own = call(slots_kernel, [((TILES, 4, CB), F32), ((1, CB), F32)], 8)(
        shared, a_row, a_lane, known, gram, q_row, q_col, proj
    )
    pairs = TILES // 2
    near = [[d * TILES + 2 * z + x for d in range(DEPTHS) for x in range(2)] for z in range(pairs)]
    far = [[2 * z + x for z in range(pairs)] for x in range(2)]
    sent = swap(sent, ("depth", "tile"), near)
    [sent] = call(fold_kernel, [((pairs, 1, CB), F32)], 1)(sent)
    [demixed] = call(final_kernel, [((1, CB), F32)], 2)(swap(sent, "tile", far), own)
    return estimate[None], demixed[0, :16]


def solution(mesh):
    in_specs = (
        P("depth", "tile", None),
        P("tile", None),
        P("depth", None, None),
        P("tile", "depth"),
        P("tile", "depth"),
        P("tile", "depth", None, None),
        P(),
        P(),
        P(),
        P(),
    )
    out_specs = (P("depth", "tile", None), P(("depth", "tile")))
    return jax.shard_map(body, mesh=mesh, in_specs=in_specs, out_specs=out_specs, check_vma=False)
```
